128 devices in a mesh: gx: 32 (over x, y_hi, z), gy: 4 (over y_lo, core).
Axes of the slice: x: 4, y: 4 (y_hi: 2, y_lo: 2; y = y_hi * 2 + y_lo), z: 4, core: 2. Of those that a mesh axis runs over, the one named last changes fastest.
Arguments:
- misfit: float32 [2, 16, 1024, 1024], P(None, None, 'gx', 'gy'), may hold values from -6 to 6
- viscosity: float32 [16, 1024, 1024], P(None, 'gx', 'gy'), may hold values from 0.1 to 10
- friction: float32 [1024, 1024], P('gx', 'gy'), may hold values from 0.5 to 50
- ice_mask: int32 [1024, 1024], P('gx', 'gy'), may hold values 0 or 1
- grounded: int32 [1024, 1024], P('gx', 'gy'), may hold values 0 or 1
Outputs:
- adjoint_velocity: float32 [2, 16, 1024, 1024], P(None, None, 'gx', 'gy')
The draws below stay inside these ranges and needn't reach their ends.
All inputs are finite; a program needn't handle non-finite values. No bound on the sum of `ice_mask` or of `grounded` on one device may be relied on, other than what follows from the above.
Results may differ from the reference program's by a relative error of at most 0.00002.
Values sent between devices are 32-bit elements; how exact they have to be, the bound alone decides.
A program may use at most 128 MiB of HBM per device.

```python
import math
import jax
import jax.numpy as jnp
from jax import lax

NZ = 16
LEVELS = 4
SWEEPS = 2
COARSE_ITERS = 20
NX = 1024
NY = 1024


def touch_ends(values, key, smallest, high):
    spot = [jax.random.randint(jax.random.fold_in(key, axis), (), 0, length) for axis, length in enumerate(values.shape)]
    widest = values.shape.index(max(values.shape))
    neighbour = spot[:widest] + [(spot[widest] + 1) % values.shape[widest]] + spot[widest + 1:]
    return values.at[tuple(spot)].set(smallest).at[tuple(neighbour)].set(high)


def shard_levels(key, shape, shards, smallest, top_value):
    def one(position, parts):
        steps = jax.random.uniform(jax.random.fold_in(jax.random.fold_in(key, 6), position), (parts,), jnp.float32, smallest / len(shards), top_value / len(shards))
        return jnp.repeat(jnp.exp(steps), shape[position] // parts).reshape((-1,) + (1,) * (len(shape) - position - 1))

    gain = one(*shards[0])
    for cut in shards[1:]:
        gain = gain * one(*cut)
    return gain


def bell_draw(key, shape, spread, most, cuts=(), dtype=jnp.bfloat16):
    entries = jax.random.normal(key, shape, jnp.float32) * spread
    if len(cuts) > 0:
        entries = shard_levels(key, shape, cuts, -0.22, 0.18) * entries
    return jnp.clip(entries, min=-most, max=most).astype(dtype)


def setup_inputs(seed: int = 0) -> dict:
    key_of = jax.random.split(jax.random.key(seed), 6)
    return {
        "misfit": bell_draw(key_of[0], (2, NZ, NX, NY), 1.0, 6.0, ((2, 32), (3, 4)), jnp.float32),
        "viscosity": jnp.clip(jnp.exp(math.log(10.0) - 4.6051702 * jax.random.uniform(key_of[1], (NZ, NX, NY), jnp.float32) ** shard_levels(key_of[1], (NZ, NX, NY), ((1, 32), (2, 4)), -0.2, 0.2)), 0.1, 10.0),
        "friction": jnp.clip(jnp.exp(math.log(50.0) - 4.6051702 * jax.random.uniform(key_of[2], (NX, NY), jnp.float32) ** shard_levels(key_of[2], (NX, NY), ((0, 32), (1, 4)), -0.2, 0.2)), 0.5, 50.0),
        "ice_mask": touch_ends((jax.random.randint(key_of[3], (NX, NY), 0, 10) < 9).astype(jnp.int32), jax.random.fold_in(key_of[3], 1), 0, 1),
        "grounded": touch_ends((jax.random.randint(key_of[4], (NX, NY), 0, 4) < 3).astype(jnp.int32), jax.random.fold_in(key_of[4], 1), 0, 1),
    }


OMEGA = 0.6
ZWEIGHT = 4.0
CROSS = 0.75


def apply_operator(padded, coef_pad, horizontal):
    layers = padded.shape[1]
    viscous = coef_pad[:layers]
    ice_share = coef_pad[layers, 1:-1, 1:-1]
    drag_term = coef_pad[layers + 1, 1:-1, 1:-1]
    centre = viscous[:, 1:-1, 1:-1]
    east_face = 0.5 * (centre + viscous[:, 2:, 1:-1])
    west_face = 0.5 * (centre + viscous[:, :-2, 1:-1])
    north_face = 0.5 * (centre + viscous[:, 1:-1, 2:])
    south_face = 0.5 * (centre + viscous[:, 1:-1, :-2])
    vertical = ZWEIGHT * 0.5 * (centre[1:] + centre[:-1])
    layer_index = lax.broadcasted_iota(jnp.int32, centre.shape, 0)
    bottom = jnp.where(layer_index == 0, drag_term, jnp.zeros_like(centre))
    vert_diag = jnp.pad(vertical, ((1, 0), (0, 0), (0, 0))) + jnp.pad(vertical, ((0, 1), (0, 0), (0, 0)))
    images = []
    diagonals = []
    for component, (x_weight, y_weight) in enumerate(((4.0, 1.0), (1.0, 4.0))):
        field = padded[component]
        middle = field[:, 1:-1, 1:-1]
        lateral = x_weight * (east_face * (middle - field[:, 2:, 1:-1]) + west_face * (middle - field[:, :-2, 1:-1]))
        lateral = lateral + y_weight * (north_face * (middle - field[:, 1:-1, 2:]) + south_face * (middle - field[:, 1:-1, :-2]))
        fluxes = vertical * (middle[1:] - middle[:-1])
        column = jnp.pad(fluxes, ((1, 0), (0, 0), (0, 0))) - jnp.pad(fluxes, ((0, 1), (0, 0), (0, 0)))
        other = padded[1 - component]
        mixed = other[:, 2:, 2:] - other[:, 2:, :-2] - other[:, :-2, 2:] + other[:, :-2, :-2]
        flow = horizontal * (lateral - CROSS * centre * mixed) + column + bottom * middle
        images.append(ice_share * flow + (1.0 - ice_share) * middle)
        lateral_diag = x_weight * (east_face + west_face) + y_weight * (north_face + south_face)
        diagonals.append(ice_share * (horizontal * lateral_diag + vert_diag + bottom) + (1.0 - ice_share))
    return jnp.stack(images), jnp.stack(diagonals)


def jacobi_update(inside, target, padded, coef_pad, horizontal):
    image, diagonal = apply_operator(padded, coef_pad, horizontal)
    return inside + OMEGA * (target - image) / diagonal


def pad_rim(array, width):
    widths = ((0, 0),) * (array.ndim - 2) + ((width, width), (width, width))
    return jnp.pad(array, widths)


def restrict(array):
    shape = array.shape
    blocks = array.reshape(shape[:-2] + (shape[-2] // 2, 2, shape[-1] // 2, 2))
    return jnp.mean(blocks, axis=(-3, -1))


def prolong(array):
    return jnp.repeat(jnp.repeat(array, 2, axis=-2), 2, axis=-1)


def cycle(level, target, coefs):
    horizontal = 0.25 ** level
    coef_pad = pad_rim(coefs, 1)
    solution = jnp.zeros_like(target)
    if level == LEVELS - 1:
        def coarse_step(iteration, current):
            return jacobi_update(current, target, pad_rim(current, 1), coef_pad, horizontal)
        return lax.fori_loop(0, COARSE_ITERS, coarse_step, solution)
    for sweep in range(SWEEPS):
        solution = jacobi_update(solution, target, pad_rim(solution, 1), coef_pad, horizontal)
    image, diagonal = apply_operator(pad_rim(solution, 1), coef_pad, horizontal)
    remainder = target - image
    correction = cycle(level + 1, restrict(remainder), restrict(coefs))
    solution = solution + prolong(correction)
    for sweep in range(SWEEPS):
        solution = jacobi_update(solution, target, pad_rim(solution, 1), coef_pad, horizontal)
    return solution


def reference(misfit, viscosity, friction, ice_mask, grounded):
    ice_share = ice_mask.astype(jnp.float32)
    drag_term = friction * grounded.astype(jnp.float32)
    coefs = jnp.concatenate([viscosity, ice_share[None], drag_term[None]], 0)
    return cycle(0, misfit * ice_share, coefs)
```

```python
import functools

import jax
import jax.numpy as jnp
from jax import lax
from jax.experimental import pallas as pl
from jax.experimental.pallas import tpu as pltpu
from jax.sharding import PartitionSpec as P

MESH = pl.DeviceIdType.MESH
HBM = pltpu.MemorySpace.HBM
OMEGA = 0.6
CROSS = 0.75
ITERS = 20

OX = (32, 16, 8, 4)
OY = (256, 128, 64, 32)
LN = (384, 256, 128, 128)
RIM = (4, 5, 6, 24)
PW = (4, 8, 16, 32)
TX = tuple(o + 2 * h for o, h in zip(OX, RIM))
REACH = 6
FAR = 2 * REACH + 1
SIDES = ((0, -1), (0, 1), (-1, -1), (-1, 1), (1, -1), (1, 1))


def lane_iota(rows):
    return lax.broadcasted_iota(jnp.int32, (rows, 128), 1)


def roll(x, shift, axis):
    return pltpu.roll(x, shift % x.shape[axis], axis)


def exact_dot(x, sel):
    hi = x.astype(jnp.bfloat16)
    rest = x - hi.astype(jnp.float32)
    mid = rest.astype(jnp.bfloat16)
    low = (rest - mid.astype(jnp.float32)).astype(jnp.bfloat16)
    rows = x.shape[0]
    out = jnp.dot(
        jnp.concatenate([hi, mid, low], 0), sel, preferred_element_type=jnp.float32
    )
    return (out[:rows] + out[rows : 2 * rows]) + out[2 * rows :]


def restrict_matrix(level):
    width = min(LN[level], OY[level]) if OY[level] >= 128 else 128
    fine = lax.broadcasted_iota(jnp.int32, (width, 128), 0)
    coarse = lax.broadcasted_iota(jnp.int32, (width, 128), 1)
    hit = (fine // 2 == coarse) & (fine < OY[level])
    return jnp.where(hit, 0.25, 0.0).astype(jnp.bfloat16)


def prolong_matrix(level):
    lc, lf = LN[level + 1], LN[level]
    coarse = lax.broadcasted_iota(jnp.int32, (lc, lf), 0)
    fine = lax.broadcasted_iota(jnp.int32, (lc, lf), 1)
    middle = (OY[level] + lf) // 2
    source = jnp.where(fine < middle, fine // 2, lc - (lf - fine + 1) // 2)
    return jnp.where(source == coarse, 1.0, 0.0).astype(jnp.bfloat16)


class Message:
    def __init__(self, place, sems, index, src, dst, dx, dy):
        gx, gy, nx, ny = place
        self.to_there = (gx + dx >= 0) & (gx + dx < nx) & (gy + dy >= 0) & (gy + dy < ny)
        self.from_there = (gx - dx >= 0) & (gx - dx < nx) & (gy - dy >= 0) & (gy - dy < ny)
        target = (jnp.clip(gx + dx, 0, nx - 1), jnp.clip(gy + dy, 0, ny - 1))
        self.dst = dst
        self.copy = pltpu.make_async_remote_copy(
            src_ref=src,
            dst_ref=dst,
            send_sem=sems[0].at[index],
            recv_sem=sems[1].at[index],
            device_id=target,
            device_id_type=MESH,
        )

    def clear(self):
        @pl.when(jnp.logical_not(self.from_there))
        def _():
            self.dst[...] = jnp.zeros(self.dst.shape, self.dst.dtype)

    def start(self):
        @pl.when(self.to_there)
        def _():
            self.copy.start()

    def arrived(self):
        @pl.when(self.from_there)
        def _():
            self.copy.wait_recv()

    def sent(self):
        @pl.when(self.to_there)
        def _():
            self.copy.wait_send()


def pack_columns(level, source, dest, planes):
    w, rim = PW[level], RIM[level]
    lane = lane_iota(planes)
    tile = (OY[level] - 1) // 128
    edge = (OY[level] - w) % 128

    def body(i, acc):
        left, right = acc
        here = (lane >= w * i) & (lane < w * i + w)
        a = source[rim + i, :, 0:128]
        b = source[rim + i, :, tile * 128 : tile * 128 + 128]
        left = jnp.where(here, pltpu.roll(a, w * i, 1), left)
        right = jnp.where(here, pltpu.roll(b, lax.rem(w * i + 128 - edge, 128), 1), right)
        return left, right

    zero = jnp.zeros((planes, 128), jnp.float32)
    left, right = lax.fori_loop(0, OX[level], body, (zero, zero), unroll=4)
    dest[0] = left
    dest[1] = right


def unpack_columns(level, dest, packs, planes, reach):
    w, rim, own = PW[level], RIM[level], OX[level]
    lane = lane_iota(planes)
    last = LN[level] - 128
    start = OY[level] % 128
    for row0, count, shift, pl_left, pl_right in (
        (-reach, reach, own - reach, 2, 3),
        (0, own, 0, 0, 1),
        (own, reach, 0, 4, 5),
    ):

        def body(i, _, row0=row0, shift=shift, pl_left=pl_left, pl_right=pl_right):
            at = w * (i + shift)
            right = pltpu.roll(packs[pl_right], lax.rem(start - at + 128, 128), 1)
            left = pltpu.roll(packs[pl_left], lax.rem(256 - w - at, 128), 1)
            row = rim + row0 + i
            if OY[level] < 128:
                base = dest[row, :, last : last + 128]
            else:
                base = jnp.zeros((planes, 128), jnp.float32)
            tile = jnp.where((lane >= start) & (lane < start + w), right, base)
            dest[row, :, last : last + 128] = jnp.where(lane >= 128 - w, left, tile)
            return 0

        lax.fori_loop(0, count, body, 0, unroll=2 if count % 2 == 0 else 1)


def coefficients(level, c, e, y4, z, q, r, g, rows):
    scale = 0.25**level
    half, cross = 0.5 * scale, CROSS * scale
    lanes, rim = LN[level], RIM[level]
    first, count = rim - rows, OX[level] + 2 * rows
    sub = lax.broadcasted_iota(jnp.int32, (8, lanes), 0)
    e[first - 1] = half * (c[first - 1, 0:16, :] + c[first, 0:16, :])

    def body(n, _):
        i = first + n
        here = c[i, 0:16, :]
        north, south = roll(here, -1, 1), roll(here, 1, 1)
        east = half * (here + c[i + 1, 0:16, :])
        west = half * (here + c[i - 1, 0:16, :])
        nf, sf = half * (here + north), half * (here + south)
        e[i] = east
        y4[i, 0:16, :] = nf
        y4[i, 16:32, :] = sf
        y4[i, 32:48, :] = cross * north
        y4[i, 48:64, :] = cross * south
        even, odd = here[0:8], here[8:16]
        inner = 2.0 * (even + odd)
        upper = jnp.where(sub < 7, 2.0 * (odd + roll(even, -1, 0)), 0.0)
        lower = roll(upper, 1, 0)
        z[i, 0:8, :] = inner
        z[i, 8:16, :] = upper
        z[i, 16:24, :] = lower
        ice = c[i, 16:17, :]
        drag = jnp.where(sub == 0, c[i, 17:18, :], 0.0)
        vertical = jnp.concatenate([inner + lower + drag, inner + upper], 0)
        xs, ys = east + west, nf + sf
        for k, lateral in enumerate((4.0 * xs + ys, xs + 4.0 * ys)):
            diag = ice * (lateral + vertical) + (1.0 - ice)
            inv = OMEGA / diag
            if q is not None:
                q[i, 16 * k : 16 * k + 16, :] = inv
            r[i, 16 * k : 16 * k + 16, :] = ice * inv
            if g is not None:
                g[i, 16 * k : 16 * k + 16, :] = diag * (1.0 / OMEGA)
        return 0

    lax.fori_loop(0, count, body, 0)


def off_diagonal(w, e, y4, z, i):
    u0, u, u2 = w[i - 1, 0:16, :], w[i, 0:16, :], w[i + 1, 0:16, :]
    v0, v, v2 = w[i - 1, 16:32, :], w[i, 16:32, :], w[i + 1, 16:32, :]
    west, east = e[i - 1], e[i]
    nf, sf, mn, ms = (y4[i, 16 * k : 16 * k + 16, :] for k in range(4))
    inner, upper, lower = (z[i, 8 * k : 8 * k + 8, :] for k in range(3))
    du, dv, v4 = u2 - u0, v2 - v0, 4.0 * v
    xu = 4.0 * (east * u2 + west * u0)
    xv = east * v2 + west * v0
    yu = roll(sf * u + ms * dv, -1, 1) + roll(nf * u - mn * dv, 1, 1)
    yv = roll(sf * v4 + ms * du, -1, 1) + roll(nf * v4 - mn * du, 1, 1)

    def column(f):
        even, odd = f[0:8], f[8:16]
        return jnp.concatenate(
            [inner * odd + lower * roll(odd, 1, 0), inner * even + upper * roll(even, -1, 0)], 0
        )

    return (u, v), (xu + yu + column(u), xv + yv + column(v))


def sweep_row(src, dst, e, y4, z, r, tt, i):
    fields, sums = off_diagonal(src, e, y4, z, i)
    for k in range(2):
        at = slice(16 * k, 16 * k + 16)
        dst[i, at, :] = (1.0 - OMEGA) * fields[k] + (tt[i, at, :] + r[i, at, :] * sums[k])


def remainder_row(src, e, y4, z, r, tt, g, i, lanes):
    fields, sums = off_diagonal(src, e, y4, z, i)
    parts = []
    for k in range(2):
        at = slice(16 * k, 16 * k + 16)
        change = tt[i, at, :] + r[i, at, :] * sums[k] - OMEGA * fields[k]
        parts.append(change[:, 0:lanes] * g[i, at, 0:lanes])
    return jnp.concatenate(parts, 0)


def kernel(nx, ny, m_ref, v_ref, f_ref, i_ref, b_ref, o_ref, *scratch):
    names = iter(scratch)
    lv = []
    for level in range(4):
        keys = ["c", "e", "y4", "z", "r", "t", "a", "b"]
        keys += ["q"] if level > 0 else []
        keys += ["g"] if level < 3 else []
        keys += ["spc", "rpc", "spt", "rpt"] if level < 3 else []
        lv.append({key: next(names) for key in keys})
    rest, far_c, far_t, side_c, side_t, fr, ic, gr = (next(names) for _ in range(8))
    in_sem, out_sem, send_sem, recv_sem, l3c, l3t = (next(names) for _ in range(6))

    gx, gy = lax.axis_index("gx"), lax.axis_index("gy")
    place = (gx, gy, nx, ny)
    sems = (send_sem, recv_sem)
    count = iter(range(10**6))

    def message(src, dst, dx, dy):
        return Message(place, sems, next(count), src, dst, dx, dy)

    def rim_messages(level, array, packs, landed, reach):
        rim, own = RIM[level], OX[level]
        lanes = pl.ds(0, max(OY[level], 128))
        out = [
            message(
                array.at[pl.ds(rim, reach), :, lanes],
                array.at[pl.ds(rim + own, reach), :, lanes], -1, 0),
            message(
                array.at[pl.ds(rim + own - reach, reach), :, lanes],
                array.at[pl.ds(rim - reach, reach), :, lanes], 1, 0),
        ]
        for slot, (dx, dy) in enumerate(SIDES):
            out.append(message(packs.at[0 if dy > 0 else 1], landed.at[slot], -dx, -dy))
        return out

    def far_messages(own, far):
        return [
            message(far.at[REACH], far.at[REACH - d], d, 0)
            for d in [k * s for k in range(REACH, 0, -1) for s in (1, -1)]
        ]

    def side_messages(far, side):
        return [message(far, side.at[0], 0, 1), message(far, side.at[1], 0, -1)]

    msg_c = [rim_messages(n, lv[n]["c"], lv[n]["spc"], lv[n]["rpc"], RIM[n]) for n in range(3)]
    msg_t = [rim_messages(n, lv[n]["t"], lv[n]["spt"], lv[n]["rpt"], RIM[n] - 1) for n in range(3)]
    msg_fc, msg_ft = far_messages(None, far_c), far_messages(None, far_t)
    msg_sc, msg_st = side_messages(far_c, side_c), side_messages(far_t, side_t)
    every = sum(msg_c + msg_t, []) + msg_fc + msg_ft + msg_sc + msg_st

    own0 = pl.ds(RIM[0], OX[0])
    loads = []
    for k in range(16):
        kk = (k % 2) * 8 + k // 2
        loads.append((v_ref.at[k], lv[0]["c"].at[own0, kk, pl.ds(0, 256)]))
        for n in range(2):
            loads.append((m_ref.at[n, k], lv[0]["t"].at[own0, 16 * n + kk, pl.ds(0, 256)]))
    loads += [(f_ref, fr), (i_ref, ic), (b_ref, gr)]
    loads = [pltpu.make_async_copy(s, d, in_sem.at[n]) for n, (s, d) in enumerate(loads)]
    for load in loads:
        load.start()

    barrier = pltpu.get_barrier_semaphore()
    partners = [(d, 0) for d in range(-REACH, REACH + 1) if d != 0] + list(SIDES)
    arrivals = 0
    for dx, dy in partners:
        there = (gx + dx >= 0) & (gx + dx < nx) & (gy + dy >= 0) & (gy + dy < ny)
        arrivals = arrivals + there.astype(jnp.int32)

        @pl.when(there)
        def _(dx=dx, dy=dy):
            pl.semaphore_signal(
                barrier,
                inc=1,
                device_id=(jnp.clip(gx + dx, 0, nx - 1), jnp.clip(gy + dy, 0, ny - 1)),
                device_id_type=MESH,
            )

    for one in every:
        one.clear()
    for load in loads:
        load.wait()

    c0, t0 = lv[0]["c"], lv[0]["t"]
    ic_f = ic[...].astype(jnp.float32)
    ic_f = ic_f.reshape(OX[0], 1, 256)
    dr_f = (fr[...] * gr[...].astype(jnp.float32)).reshape(OX[0], 1, 256)
    sub = lax.broadcasted_iota(jnp.int32, (OX[0], 8, 256), 1)
    c0[own0, 16:24, 0:256] = jnp.where(sub == 0, ic_f, jnp.where(sub == 1, dr_f, 0.0))

    pl.semaphore_wait(barrier, arrivals)
    for one in msg_c[0][:2] + msg_t[0][:2]:
        one.start()
    pack_columns(0, c0, lv[0]["spc"], 24)
    pack_columns(0, t0, lv[0]["spt"], 32)
    for one in msg_c[0][2:] + msg_t[0][2:]:
        one.start()

    for level in range(3):
        rim, own, width = RIM[level], OX[level + 1], max(OY[level], 128)
        fine = lv[level]["c"]
        block = fine[rim : rim + 2 * own, :, 0:width].reshape(own, 2, 24, width)
        block = (block[:, 0] + block[:, 1]).reshape(own * 24, width)
        coarse = exact_dot(block, restrict_matrix(level)).reshape(own, 24, 128)
        if level < 2:
            target = lv[level + 1]["c"]
            target[RIM[level + 1] : RIM[level + 1] + own, :, 0:128] = coarse
            for one in msg_c[level + 1][:2]:
                one.start()
            pack_columns(level + 1, target, lv[level + 1]["spc"], 24)
            for one in msg_c[level + 1][2:]:
                one.start()
        else:
            far_c[REACH] = sum(roll(coarse[k], 32 * k, 1) for k in range(4))
            for one in msg_fc:
                one.start()

    def refs(level):
        return [lv[level][key] for key in ("e", "y4", "z", "r", "t")]

    def gather(level, kind, messages, landed, planes, reach):
        for one in messages:
            one.arrived()
        if OY[level] < 128:
            for one in messages[:2]:
                one.sent()
        unpack_columns(level, lv[level][kind], lv[level][landed], planes, reach)

    def first_sweep(level, rows, factor):
        t = lv[level]["t"]

        def body(n, _):
            i = RIM[level] - rows + n
            t[i] = t[i] * factor[i]
            return 0

        lax.fori_loop(0, OX[level] + 2 * rows, body, 0, unroll=2)

    def sweep(level, src, dst, rows):
        args = refs(level)

        def body(n, _):
            sweep_row(src, dst, *args, RIM[level] - rows + n)
            return 0

        lax.fori_loop(0, OX[level] + 2 * rows, body, 0, unroll=1 if level < 2 else 2)

    def restricted_remainder(level, src):
        args = refs(level)
        width, own = max(OY[level], 128), OX[level + 1]

        def body(n, _):
            i = RIM[level] + 2 * n
            pair = [remainder_row(src, *args, lv[level]["g"], i + k, width) for k in range(2)]
            rest[n, :, 0:width] = pair[0] + pair[1]
            return 0

        lax.fori_loop(0, own, body, 0)
        block = rest[0:own, :, 0:width].reshape(own * 32, width)
        return exact_dot(block, restrict_matrix(level)).reshape(own, 32, 128)

    def prolonged(level, src, dst, rows):
        low, high = RIM[level + 1] - rows, RIM[level + 1] + OX[level + 1] + rows
        n = high - low
        sel = prolong_matrix(level)
        spread = lv[level]["g"]
        block = src[low:high].reshape(n * 32, LN[level + 1])
        spread[0:n] = exact_dot(block, sel).reshape(n, 32, LN[level])

        def body(k, _):
            i = RIM[level] + 2 * (k - rows)
            extra = spread[k]
            dst[i] = dst[i] + extra
            dst[i + 1] = dst[i + 1] + extra
            return 0

        lax.fori_loop(0, n, body, 0)

    gather(0, "c", msg_c[0], "rpc", 24, RIM[0])
    coefficients(0, c0, *[lv[0][k] for k in ("e", "y4", "z")], None, lv[0]["r"], lv[0]["g"], 3)
    gather(0, "t", msg_t[0], "rpt", 32, RIM[0] - 1)
    for one in msg_t[0][:2]:
        one.sent()
    first_sweep(0, 3, lv[0]["r"])
    sweep(0, t0, lv[0]["a"], 2)
    t_next = restricted_remainder(0, lv[0]["a"])

    for level in (1, 2):
        t = lv[level]["t"]
        t[RIM[level] : RIM[level] + OX[level], :, 0:128] = t_next
        for one in msg_t[level][:2]:
            one.start()
        pack_columns(level, t, lv[level]["spt"], 32)
        for one in msg_t[level][2:]:
            one.start()
        gather(level, "c", msg_c[level], "rpc", 24, RIM[level])
        coefficients(
            level, *[lv[level][k] for k in ("c", "e", "y4", "z", "q", "r", "g")], RIM[level] - 1
        )
        if level == 1:
            for one in msg_fc:
                one.arrived()
            for one in msg_sc:
                one.start()
        gather(level, "t", msg_t[level], "rpt", 32, RIM[level] - 1)
        if OY[level] >= 128:
            for one in msg_t[level][:2]:
                one.sent()
        first_sweep(level, RIM[level] - 1, lv[level]["q"])
        sweep(level, t, lv[level]["a"], RIM[level] - 2)
        t_next = restricted_remainder(level, lv[level]["a"])

    far_t[REACH] = sum(roll(t_next[k], 32 * k, 1) for k in range(4))
    for one in msg_ft:
        one.start()

    def unpack_far(dest, far, side, planes):
        lane = lane_iota(planes)

        def body(b, _):
            own, left, right = far[b], side[0, b], side[1, b]
            for k in range(4):
                tile = jnp.where(lane < 32, roll(own, -32 * k, 1), 0.0)
                tile = jnp.where((lane >= 32) & (lane < 64), roll(right, 32 - 32 * k, 1), tile)
                tile = jnp.where(lane >= 96, roll(left, 96 - 32 * k, 1), tile)
                dest[4 * b + k] = tile
            return 0

        lax.fori_loop(0, FAR, body, 0)

    for one in msg_sc:
        one.arrived()
    unpack_far(lv[3]["c"], far_c, side_c, 24)
    coefficients(3, *[lv[3][k] for k in ("c", "e", "y4", "z", "q", "r")], None, RIM[3] - 1)
    for one in msg_ft:
        one.arrived()
    for one in msg_st:
        one.start()
    for one in msg_st:
        one.arrived()
    t3, a3, b3 = lv[3]["t"], lv[3]["a"], lv[3]["b"]
    unpack_far(t3, far_t, side_t, 32)
    first_sweep(3, RIM[3] - 1, lv[3]["q"])
    args3 = refs(3)

    def coarse_sweep(src, dst, s):
        first = s + 2

        def body(n, _):
            for k in range(4):
                sweep_row(src, dst, *args3, first + 4 * n + k)
            return 0

        lax.fori_loop(0, (51 - 2 * s) // 4, body, 0)

    coarse_sweep(t3, a3, 2)

    def coarse_pair(n, _):
        coarse_sweep(a3, b3, 2 * n + 3)
        coarse_sweep(b3, a3, 2 * n + 4)
        return 0

    lax.fori_loop(0, (ITERS - 2) // 2, coarse_pair, 0)

    prolonged(2, a3, lv[2]["a"], 2)
    sweep(2, lv[2]["a"], lv[2]["b"], 3)
    sweep(2, lv[2]["b"], lv[2]["a"], 2)
    prolonged(1, lv[2]["a"], lv[1]["a"], 2)
    sweep(1, lv[1]["a"], lv[1]["b"], 2)
    sweep(1, lv[1]["b"], lv[1]["a"], 1)
    prolonged(0, lv[1]["a"], lv[0]["a"], 1)
    a0, b0 = lv[0]["a"], lv[0]["b"]
    sweep(0, a0, b0, 1)
    args0 = refs(0)
    stores = []
    for part in range(2):
        first = RIM[0] + 16 * part

        def last_body(n, _, first=first):
            sweep_row(b0, a0, *args0, first + n)
            return 0

        lax.fori_loop(0, 16, last_body, 0)
        for n in range(2):
            for k in range(16):
                kk = (k % 2) * 8 + k // 2
                store = pltpu.make_async_copy(
                    a0.at[pl.ds(first, 16), 16 * n + kk, pl.ds(0, 256)],
                    o_ref.at[n, k, pl.ds(16 * part, 16), :],
                    out_sem.at[32 * part + 16 * n + k],
                )
                store.start()
                stores.append(store)
    waited = msg_t[0][:2] + msg_t[1][:2] + msg_t[2][:2] + msg_c[2][:2]
    for one in every:
        if one not in waited:
            one.sent()
    for store in stores:
        store.wait()


def solution(mesh):
    nx, ny = mesh.shape["gx"], mesh.shape["gy"]
    f32 = jnp.float32
    scratch = []
    for level in range(4):
        rows, lanes = TX[level], LN[level]
        planes = [24, 16, 64, 24, 32, 32, 32, 32]
        planes += [32] if level > 0 else []
        planes += [32] if level < 3 else []
        scratch += [pltpu.VMEM((rows, p, lanes), f32) for p in planes]
        if level < 3:
            scratch += [pltpu.VMEM((n, p, 128), f32) for p in (24, 32) for n in (2, 6)]
    scratch += [pltpu.VMEM((16, 32, 256), f32)]
    scratch += [pltpu.VMEM((FAR, 24, 128), f32), pltpu.VMEM((FAR, 32, 128), f32)]
    scratch += [pltpu.VMEM((2, FAR, 24, 128), f32), pltpu.VMEM((2, FAR, 32, 128), f32)]
    scratch += [
        pltpu.VMEM((32, 256), f32),
        pltpu.VMEM((32, 256), jnp.int32),
        pltpu.VMEM((32, 256), jnp.int32),
    ]
    messages = 6 * 8 + 4 * REACH + 4
    scratch += [pltpu.SemaphoreType.DMA((51,)), pltpu.SemaphoreType.DMA((64,))]
    scratch += [pltpu.SemaphoreType.DMA((messages,)), pltpu.SemaphoreType.DMA((messages,))]
    scratch += [pltpu.SemaphoreType.DMA((1,)), pltpu.SemaphoreType.DMA((1,))]

    def per_device(misfit, viscosity, friction, ice_mask, grounded):
        return pl.pallas_call(
            functools.partial(kernel, nx, ny),
            out_shape=jax.ShapeDtypeStruct(misfit.shape, f32),
            in_specs=[pl.BlockSpec(memory_space=HBM)] * 5,
            out_specs=pl.BlockSpec(memory_space=HBM),
            scratch_shapes=scratch,
            compiler_params=pltpu.CompilerParams(
                collective_id=0, has_side_effects=True, vmem_limit_bytes=62 * 2**20
            ),
        )(misfit, viscosity, friction, ice_mask, grounded)

    placed = (
        P(None, None, "gx", "gy"),
        P(None, "gx", "gy"),
        P("gx", "gy"),
        P("gx", "gy"),
        P("gx", "gy"),
    )
    return jax.shard_map(
        per_device, mesh=mesh, in_specs=placed, out_specs=P(None, None, "gx", "gy"), check_vma=False
    )
```

```python
import functools

import jax
import jax.numpy as jnp
from jax import lax
from jax.experimental import pallas as pl
from jax.experimental.pallas import tpu as pltpu
from jax.sharding import PartitionSpec as P

MESH = pl.DeviceIdType.MESH
HBM = pltpu.MemorySpace.HBM
OMEGA = 0.6
CROSS = 0.75
ITERS = 20

OX = (32, 16, 8, 4)
OY = (256, 128, 64, 32)
LN = (384, 256, 128, 128)
RIM = (4, 5, 6, 24)
PW = (4, 8, 16, 32)
TX = tuple(o + 2 * h for o, h in zip(OX[:3], RIM)) + (58,)
UNROLL = (2, 3, 6, 8)
UNROLL_C = (2, 3, 6, 5)
UNROLL_R = (1, 2, 4)
REACH = 6
FAR = 2 * REACH + 1
SIDES = ((0, -1), (0, 1), (-1, -1), (-1, 1), (1, -1), (1, 1))


def over_rows(first, count, body, unroll):
    steps = count // unroll

    def step(n, _):
        for k in range(unroll):
            body(first + n * unroll + k)
        return 0

    if steps > 0:
        lax.fori_loop(0, steps, step, 0)
    for k in range(steps * unroll, count):
        body(first + k)


def lane_iota(rows):
    return lax.broadcasted_iota(jnp.int32, (rows, 128), 1)


def roll(x, shift, axis):
    return pltpu.roll(x, shift % x.shape[axis], axis)


def exact_dot(x, sel):
    hi = x.astype(jnp.bfloat16)
    rest = x - hi.astype(jnp.float32)
    mid = rest.astype(jnp.bfloat16)
    low = (rest - mid.astype(jnp.float32)).astype(jnp.bfloat16)
    rows = x.shape[0]
    out = jnp.dot(
        jnp.concatenate([hi, mid, low], 0), sel, preferred_element_type=jnp.float32
    )
    return (out[:rows] + out[rows : 2 * rows]) + out[2 * rows :]


def restrict_matrix(level):
    width = min(LN[level], OY[level]) if OY[level] >= 128 else 128
    fine = lax.broadcasted_iota(jnp.int32, (width, 128), 0)
    coarse = lax.broadcasted_iota(jnp.int32, (width, 128), 1)
    hit = (fine // 2 == coarse) & (fine < OY[level])
    return jnp.where(hit, 0.25, 0.0).astype(jnp.bfloat16)


def prolong_matrix(level):
    lc, lf = LN[level + 1], LN[level]
    coarse = lax.broadcasted_iota(jnp.int32, (lc, lf), 0)
    fine = lax.broadcasted_iota(jnp.int32, (lc, lf), 1)
    middle = (OY[level] + lf) // 2
    source = jnp.where(fine < middle, fine // 2, lc - (lf - fine + 1) // 2)
    return jnp.where(source == coarse, 1.0, 0.0).astype(jnp.bfloat16)


class Message:
    def __init__(self, place, sems, index, src, dst, dx, dy):
        gx, gy, nx, ny = place
        self.to_there = (gx + dx >= 0) & (gx + dx < nx) & (gy + dy >= 0) & (gy + dy < ny)
        self.from_there = (gx - dx >= 0) & (gx - dx < nx) & (gy - dy >= 0) & (gy - dy < ny)
        target = (jnp.clip(gx + dx, 0, nx - 1), jnp.clip(gy + dy, 0, ny - 1))
        self.dst = dst
        self.copy = pltpu.make_async_remote_copy(
            src_ref=src,
            dst_ref=dst,
            send_sem=sems[0].at[index],
            recv_sem=sems[1].at[index],
            device_id=target,
            device_id_type=MESH,
        )

    def clear(self):
        @pl.when(jnp.logical_not(self.from_there))
        def _():
            self.dst[...] = jnp.zeros(self.dst.shape, self.dst.dtype)

    def start(self):
        @pl.when(self.to_there)
        def _():
            self.copy.start()

    def arrived(self):
        @pl.when(self.from_there)
        def _():
            self.copy.wait_recv()

    def sent(self):
        @pl.when(self.to_there)
        def _():
            self.copy.wait_send()


def pack_columns(level, source, dest, planes):
    w, rim = PW[level], RIM[level]
    lane = lane_iota(planes)
    tile = (OY[level] - 1) // 128
    edge = (OY[level] - w) % 128

    def body(i, acc):
        left, right = acc
        here = (lane >= w * i) & (lane < w * i + w)
        a = source[rim + i, :, 0:128]
        b = source[rim + i, :, tile * 128 : tile * 128 + 128]
        left = jnp.where(here, pltpu.roll(a, w * i, 1), left)
        right = jnp.where(here, pltpu.roll(b, lax.rem(w * i + 128 - edge, 128), 1), right)
        return left, right

    zero = jnp.zeros((planes, 128), jnp.float32)
    left, right = lax.fori_loop(0, OX[level], body, (zero, zero), unroll=4)
    dest[0] = left
    dest[1] = right


def unpack_columns(level, dest, packs, planes, reach):
    w, rim, own = PW[level], RIM[level], OX[level]
    lane = lane_iota(planes)
    last = LN[level] - 128
    start = OY[level] % 128
    for row0, count, shift, pl_left, pl_right in (
        (-reach, reach, own - reach, 2, 3),
        (0, own, 0, 0, 1),
        (own, reach, 0, 4, 5),
    ):

        for i in range(count):
            at = w * (i + shift)
            right = roll(packs[pl_right], start - at, 1)
            left = roll(packs[pl_left], -w - at, 1)
            row = rim + row0 + i
            if OY[level] < 128:
                base = dest[row, :, last : last + 128]
            else:
                base = jnp.zeros((planes, 128), jnp.float32)
            tile = jnp.where((lane >= start) & (lane < start + w), right, base)
            dest[row, :, last : last + 128] = jnp.where(lane >= 128 - w, left, tile)


def coefficients(level, c, e, y4, z, q, r, g, rows):
    scale = 0.25**level
    half, cross = 0.5 * scale, CROSS * scale
    lanes, rim = LN[level], RIM[level]
    first, count = rim - rows, OX[level] + 2 * rows
    sub = lax.broadcasted_iota(jnp.int32, (8, lanes), 0)
    e[first - 1] = half * (c[first - 1, 0:16, :] + c[first, 0:16, :])

    def body(i):
        here = c[i, 0:16, :]
        north, south = roll(here, -1, 1), roll(here, 1, 1)
        east = half * (here + c[i + 1, 0:16, :])
        west = half * (here + c[i - 1, 0:16, :])
        nf, sf = half * (here + north), half * (here + south)
        e[i] = east
        y4[i, 0:16, :] = nf
        y4[i, 16:32, :] = sf
        y4[i, 32:48, :] = cross * north
        y4[i, 48:64, :] = cross * south
        even, odd = here[0:8], here[8:16]
        inner = 2.0 * (even + odd)
        upper = jnp.where(sub < 7, 2.0 * (odd + roll(even, -1, 0)), 0.0)
        lower = roll(upper, 1, 0)
        z[i, 0:8, :] = inner
        z[i, 8:16, :] = upper
        z[i, 16:24, :] = lower
        ice = c[i, 16:17, :]
        drag = jnp.where(sub == 0, c[i, 17:18, :], 0.0)
        vertical = jnp.concatenate([inner + lower + drag, inner + upper], 0)
        xs, ys = east + west, nf + sf
        for k, lateral in enumerate((4.0 * xs + ys, xs + 4.0 * ys)):
            diag = ice * (lateral + vertical) + (1.0 - ice)
            inv = OMEGA / diag
            if q is not None:
                q[i, 16 * k : 16 * k + 16, :] = inv
            r[i, 16 * k : 16 * k + 16, :] = ice * inv
            if g is not None:
                g[i, 16 * k : 16 * k + 16, :] = diag * (1.0 / OMEGA)

    over_rows(first, count, body, UNROLL_C[level])


def off_diagonal(w, e, y4, z, i):
    u0, u, u2 = w[i - 1, 0:16, :], w[i, 0:16, :], w[i + 1, 0:16, :]
    v0, v, v2 = w[i - 1, 16:32, :], w[i, 16:32, :], w[i + 1, 16:32, :]
    west, east = e[i - 1], e[i]
    nf, sf, mn, ms = (y4[i, 16 * k : 16 * k + 16, :] for k in range(4))
    inner, upper, lower = (z[i, 8 * k : 8 * k + 8, :] for k in range(3))
    du, dv, v4 = u2 - u0, v2 - v0, 4.0 * v
    xu = 4.0 * (east * u2 + west * u0)
    xv = east * v2 + west * v0
    yu = roll(sf * u + ms * dv, -1, 1) + roll(nf * u - mn * dv, 1, 1)
    yv = roll(sf * v4 + ms * du, -1, 1) + roll(nf * v4 - mn * du, 1, 1)

    def column(f):
        even, odd = f[0:8], f[8:16]
        return jnp.concatenate(
            [inner * odd + lower * roll(odd, 1, 0), inner * even + upper * roll(even, -1, 0)], 0
        )

    return (u, v), (xu + yu + column(u), xv + yv + column(v))


def sweep_row(src, dst, e, y4, z, r, tt, i):
    fields, sums = off_diagonal(src, e, y4, z, i)
    for k in range(2):
        at = slice(16 * k, 16 * k + 16)
        dst[i, at, :] = (1.0 - OMEGA) * fields[k] + (tt[i, at, :] + r[i, at, :] * sums[k])


def remainder_row(src, e, y4, z, r, tt, g, i, lanes):
    fields, sums = off_diagonal(src, e, y4, z, i)
    parts = []
    for k in range(2):
        at = slice(16 * k, 16 * k + 16)
        change = tt[i, at, :] + r[i, at, :] * sums[k] - OMEGA * fields[k]
        parts.append(change[:, 0:lanes] * g[i, at, 0:lanes])
    return jnp.concatenate(parts, 0)


def kernel(nx, ny, m_ref, v_ref, f_ref, i_ref, b_ref, o_ref, *scratch):
    names = iter(scratch)
    lv = []
    for level in range(4):
        keys = ["c", "e", "y4", "z", "r", "t", "a", "b"]
        keys += ["q"] if level > 0 else []
        keys += ["g"] if level < 3 else []
        keys += ["spc", "rpc", "spt", "rpt"] if level < 3 else []
        lv.append({key: next(names) for key in keys})
    rest, far_c, far_t, side_c, side_t, fr, ic, gr = (next(names) for _ in range(8))
    in_sem, out_sem, send_sem, recv_sem = (next(names) for _ in range(4))

    gx, gy = lax.axis_index("gx"), lax.axis_index("gy")
    place = (gx, gy, nx, ny)
    sems = (send_sem, recv_sem)
    count = iter(range(10**6))

    def message(src, dst, dx, dy):
        return Message(place, sems, next(count), src, dst, dx, dy)

    def rim_messages(level, array, packs, landed, reach):
        rim, own = RIM[level], OX[level]
        lanes = pl.ds(0, max(OY[level], 128))
        out = [
            message(
                array.at[pl.ds(rim, reach), :, lanes],
                array.at[pl.ds(rim + own, reach), :, lanes], -1, 0),
            message(
                array.at[pl.ds(rim + own - reach, reach), :, lanes],
                array.at[pl.ds(rim - reach, reach), :, lanes], 1, 0),
        ]
        for slot, (dx, dy) in enumerate(SIDES):
            out.append(message(packs.at[0 if dy > 0 else 1], landed.at[slot], -dx, -dy))
        return out

    def far_messages(own, far):
        return [
            message(far.at[REACH], far.at[REACH - d], d, 0)
            for d in [k * s for k in range(REACH, 0, -1) for s in (1, -1)]
        ]

    def side_messages(far, side):
        return [message(far, side.at[0], 0, 1), message(far, side.at[1], 0, -1)]

    msg_c = [rim_messages(n, lv[n]["c"], lv[n]["spc"], lv[n]["rpc"], RIM[n]) for n in range(3)]
    msg_t = [rim_messages(n, lv[n]["t"], lv[n]["spt"], lv[n]["rpt"], RIM[n] - 1) for n in range(3)]
    msg_fc, msg_ft = far_messages(None, far_c), far_messages(None, far_t)
    msg_sc, msg_st = side_messages(far_c, side_c), side_messages(far_t, side_t)
    every = sum(msg_c + msg_t, []) + msg_fc + msg_ft + msg_sc + msg_st

    own0 = pl.ds(RIM[0], OX[0])
    loads = []
    for k in range(16):
        kk = (k % 2) * 8 + k // 2
        loads.append((v_ref.at[k], lv[0]["c"].at[own0, kk, pl.ds(0, 256)]))
        for n in range(2):
            loads.append((m_ref.at[n, k], lv[0]["t"].at[own0, 16 * n + kk, pl.ds(0, 256)]))
    loads += [(f_ref, fr), (i_ref, ic), (b_ref, gr)]
    loads = [pltpu.make_async_copy(s, d, in_sem.at[n]) for n, (s, d) in enumerate(loads)]
    for load in loads:
        load.start()

    barrier = pltpu.get_barrier_semaphore()
    partners = [(d, 0) for d in range(-REACH, REACH + 1) if d != 0] + list(SIDES)
    arrivals = 0
    for dx, dy in partners:
        there = (gx + dx >= 0) & (gx + dx < nx) & (gy + dy >= 0) & (gy + dy < ny)
        arrivals = arrivals + there.astype(jnp.int32)

        @pl.when(there)
        def _(dx=dx, dy=dy):
            pl.semaphore_signal(
                barrier,
                inc=1,
                device_id=(jnp.clip(gx + dx, 0, nx - 1), jnp.clip(gy + dy, 0, ny - 1)),
                device_id_type=MESH,
            )

    for one in every:
        one.clear()
    for load in loads:
        load.wait()

    c0, t0 = lv[0]["c"], lv[0]["t"]
    ic_f = ic[...].astype(jnp.float32)
    ic_f = ic_f.reshape(OX[0], 1, 256)
    dr_f = (fr[...] * gr[...].astype(jnp.float32)).reshape(OX[0], 1, 256)
    sub = lax.broadcasted_iota(jnp.int32, (OX[0], 8, 256), 1)
    c0[own0, 16:24, 0:256] = jnp.where(sub == 0, ic_f, jnp.where(sub == 1, dr_f, 0.0))

    pl.semaphore_wait(barrier, arrivals)
    for one in msg_c[0][:2] + msg_t[0][:2]:
        one.start()
    pack_columns(0, c0, lv[0]["spc"], 24)
    pack_columns(0, t0, lv[0]["spt"], 32)
    for one in msg_c[0][2:] + msg_t[0][2:]:
        one.start()

    for level in range(3):
        rim, own, width = RIM[level], OX[level + 1], max(OY[level], 128)
        fine = lv[level]["c"]
        block = fine[rim : rim + 2 * own, :, 0:width].reshape(own, 2, 24, width)
        block = (block[:, 0] + block[:, 1]).reshape(own * 24, width)
        coarse = exact_dot(block, restrict_matrix(level)).reshape(own, 24, 128)
        if level < 2:
            target = lv[level + 1]["c"]
            target[RIM[level + 1] : RIM[level + 1] + own, :, 0:128] = coarse
            for one in msg_c[level + 1][:2]:
                one.start()
            pack_columns(level + 1, target, lv[level + 1]["spc"], 24)
            for one in msg_c[level + 1][2:]:
                one.start()
        else:
            far_c[REACH] = sum(roll(coarse[k], 32 * k, 1) for k in range(4))
            for one in msg_fc:
                one.start()

    def refs(level):
        return [lv[level][key] for key in ("e", "y4", "z", "r", "t")]

    def gather(level, kind, messages, landed, planes, reach):
        for one in messages:
            one.arrived()
        if OY[level] < 128:
            for one in messages[:2]:
                one.sent()
        unpack_columns(level, lv[level][kind], lv[level][landed], planes, reach)

    def first_sweep(level, rows, factor):
        t = lv[level]["t"]

        def body(i):
            t[i] = t[i] * factor[i]

        over_rows(RIM[level] - rows, OX[level] + 2 * rows, body, 4)

    def sweep(level, src, dst, rows):
        args = refs(level)

        over_rows(
            RIM[level] - rows,
            OX[level] + 2 * rows,
            lambda i: sweep_row(src, dst, *args, i),
            UNROLL[level],
        )

    def restricted_remainder(level, src):
        args = refs(level)
        width, own = max(OY[level], 128), OX[level + 1]

        def body(n):
            i = RIM[level] + 2 * n
            pair = [remainder_row(src, *args, lv[level]["g"], i + k, width) for k in range(2)]
            rest[n, :, 0:width] = pair[0] + pair[1]

        over_rows(0, own, body, UNROLL_R[level])
        block = rest[0:own, :, 0:width].reshape(own * 32, width)
        return exact_dot(block, restrict_matrix(level)).reshape(own, 32, 128)

    def prolonged(level, src, dst, rows):
        low, high = RIM[level + 1] - rows, RIM[level + 1] + OX[level + 1] + rows
        n = high - low
        sel = prolong_matrix(level)
        spread = lv[level]["g"]
        block = src[low:high].reshape(n * 32, LN[level + 1])
        spread[0:n] = exact_dot(block, sel).reshape(n, 32, LN[level])

        def body(k):
            i = RIM[level] + 2 * (k - rows)
            extra = spread[k]
            dst[i] = dst[i] + extra
            dst[i + 1] = dst[i + 1] + extra

        over_rows(0, n, body, 2)

    gather(0, "c", msg_c[0], "rpc", 24, RIM[0])
    coefficients(0, c0, *[lv[0][k] for k in ("e", "y4", "z")], None, lv[0]["r"], lv[0]["g"], 3)
    gather(0, "t", msg_t[0], "rpt", 32, RIM[0] - 1)
    for one in msg_t[0][:2]:
        one.sent()
    first_sweep(0, 3, lv[0]["r"])
    sweep(0, t0, lv[0]["a"], 2)
    t_next = restricted_remainder(0, lv[0]["a"])

    for level in (1, 2):
        t = lv[level]["t"]
        t[RIM[level] : RIM[level] + OX[level], :, 0:128] = t_next
        for one in msg_t[level][:2]:
            one.start()
        pack_columns(level, t, lv[level]["spt"], 32)
        for one in msg_t[level][2:]:
            one.start()
        gather(level, "c", msg_c[level], "rpc", 24, RIM[level])
        coefficients(
            level, *[lv[level][k] for k in ("c", "e", "y4", "z", "q", "r", "g")], RIM[level] - 1
        )
        if level == 1:
            for one in msg_fc:
                one.arrived()
            for one in msg_sc:
                one.start()
        gather(level, "t", msg_t[level], "rpt", 32, RIM[level] - 1)
        if OY[level] >= 128:
            for one in msg_t[level][:2]:
                one.sent()
        first_sweep(level, RIM[level] - 1, lv[level]["q"])
        sweep(level, t, lv[level]["a"], RIM[level] - 2)
        t_next = restricted_remainder(level, lv[level]["a"])

    far_t[REACH] = sum(roll(t_next[k], 32 * k, 1) for k in range(4))
    for one in msg_ft:
        one.start()

    def unpack_far(dest, far, side, planes):
        lane = lane_iota(planes)

        def body(b, _):
            own, left, right = far[b], side[0, b], side[1, b]
            for k in range(4):
                tile = jnp.where(lane < 32, roll(own, -32 * k, 1), 0.0)
                tile = jnp.where((lane >= 32) & (lane < 64), roll(right, 32 - 32 * k, 1), tile)
                tile = jnp.where(lane >= 96, roll(left, 96 - 32 * k, 1), tile)
                dest[4 * b + k] = tile
            return 0

        lax.fori_loop(0, FAR, body, 0)

    for one in msg_sc:
        one.arrived()
    unpack_far(lv[3]["c"], far_c, side_c, 24)
    coefficients(3, *[lv[3][k] for k in ("c", "e", "y4", "z", "q", "r")], None, RIM[3] - 1)
    for one in msg_ft:
        one.arrived()
    for one in msg_st:
        one.start()
    for one in msg_st:
        one.arrived()
    t3, a3, b3 = lv[3]["t"], lv[3]["a"], lv[3]["b"]
    unpack_far(t3, far_t, side_t, 32)
    first_sweep(3, RIM[3] - 1, lv[3]["q"])
    args3 = refs(3)

    def coarse_sweep(src, dst, s):
        first = s + 2

        def body(n, _):
            for k in range(UNROLL[3]):
                sweep_row(src, dst, *args3, first + UNROLL[3] * n + k)
            return 0

        lax.fori_loop(0, (47 - 2 * s + UNROLL[3]) // UNROLL[3], body, 0)

    coarse_sweep(t3, a3, 2)

    def coarse_pair(n, _):
        coarse_sweep(a3, b3, 2 * n + 3)
        coarse_sweep(b3, a3, 2 * n + 4)
        return 0

    lax.fori_loop(0, (ITERS - 2) // 2, coarse_pair, 0)

    prolonged(2, a3, lv[2]["a"], 2)
    sweep(2, lv[2]["a"], lv[2]["b"], 3)
    sweep(2, lv[2]["b"], lv[2]["a"], 2)
    prolonged(1, lv[2]["a"], lv[1]["a"], 2)
    sweep(1, lv[1]["a"], lv[1]["b"], 2)
    sweep(1, lv[1]["b"], lv[1]["a"], 1)
    prolonged(0, lv[1]["a"], lv[0]["a"], 1)
    a0, b0 = lv[0]["a"], lv[0]["b"]
    sweep(0, a0, b0, 1)
    args0 = refs(0)
    stores = []
    for part in range(2):
        first = RIM[0] + 16 * part

        over_rows(first, 16, lambda i: sweep_row(b0, a0, *args0, i), UNROLL[0])
        for n in range(2):
            for k in range(16):
                kk = (k % 2) * 8 + k // 2
                store = pltpu.make_async_copy(
                    a0.at[pl.ds(first, 16), 16 * n + kk, pl.ds(0, 256)],
                    o_ref.at[n, k, pl.ds(16 * part, 16), :],
                    out_sem.at[32 * part + 16 * n + k],
                )
                store.start()
                stores.append(store)
    waited = msg_t[0][:2] + msg_t[1][:2] + msg_t[2][:2] + msg_c[2][:2]
    for one in every:
        if one not in waited:
            one.sent()
    for store in stores:
        store.wait()


def solution(mesh):
    nx, ny = mesh.shape["gx"], mesh.shape["gy"]
    f32 = jnp.float32
    scratch = []
    for level in range(4):
        rows, lanes = TX[level], LN[level]
        planes = [24, 16, 64, 24, 32, 32, 32, 32]
        planes += [32] if level > 0 else []
        planes += [32] if level < 3 else []
        scratch += [pltpu.VMEM((rows, p, lanes), f32) for p in planes]
        if level < 3:
            scratch += [pltpu.VMEM((n, p, 128), f32) for p in (24, 32) for n in (2, 6)]
    scratch += [pltpu.VMEM((16, 32, 256), f32)]
    scratch += [pltpu.VMEM((FAR, 24, 128), f32), pltpu.VMEM((FAR, 32, 128), f32)]
    scratch += [pltpu.VMEM((2, FAR, 24, 128), f32), pltpu.VMEM((2, FAR, 32, 128), f32)]
    scratch += [
        pltpu.VMEM((32, 256), f32),
        pltpu.VMEM((32, 256), jnp.int32),
        pltpu.VMEM((32, 256), jnp.int32),
    ]
    messages = 6 * 8 + 4 * REACH + 4
    scratch += [pltpu.SemaphoreType.DMA((51,)), pltpu.SemaphoreType.DMA((64,))]
    scratch += [pltpu.SemaphoreType.DMA((messages,)), pltpu.SemaphoreType.DMA((messages,))]

    def per_device(misfit, viscosity, friction, ice_mask, grounded):
        return pl.pallas_call(
            functools.partial(kernel, nx, ny),
            out_shape=jax.ShapeDtypeStruct(misfit.shape, f32),
            in_specs=[pl.BlockSpec(memory_space=HBM)] * 5,
            out_specs=pl.BlockSpec(memory_space=HBM),
            scratch_shapes=scratch,
            compiler_params=pltpu.CompilerParams(
                collective_id=0, has_side_effects=True, vmem_limit_bytes=62 * 2**20
            ),
        )(misfit, viscosity, friction, ice_mask, grounded)

    placed = (
        P(None, None, "gx", "gy"),
        P(None, "gx", "gy"),
        P("gx", "gy"),
        P("gx", "gy"),
        P("gx", "gy"),
    )
    return jax.shard_map(
        per_device, mesh=mesh, in_specs=placed, out_specs=P(None, None, "gx", "gy"), check_vma=False
    )
```

```python
import functools

import jax
import jax.numpy as jnp
from jax import lax
from jax.experimental import pallas as pl
from jax.experimental.pallas import tpu as pltpu
from jax.sharding import PartitionSpec as P

MESH = pl.DeviceIdType.MESH
HBM = pltpu.MemorySpace.HBM
OMEGA = 0.6
CROSS = 0.75
ITERS = 20

OX = (32, 16, 8, 4)
OY = (256, 128, 64, 32)
LN = (384, 256, 128, 128)
RIM = (4, 5, 6, 24)
PW = (4, 8, 16, 32)
TX = tuple(o + 2 * h for o, h in zip(OX[:3], RIM)) + (58,)
UNROLL = (2, 3, 6, 8)
UNROLL_C = (2, 3, 6, 5)
UNROLL_R = (1, 2, 4)
REACH = 6
FAR = 2 * REACH + 1
SIDES = ((0, -1), (0, 1), (-1, -1), (-1, 1), (1, -1), (1, 1))


def over_rows(first, count, body, unroll):
    steps = count // unroll

    def step(n, _):
        for k in range(unroll):
            body(first + n * unroll + k)
        return 0

    if steps > 0:
        lax.fori_loop(0, steps, step, 0)
    for k in range(steps * unroll, count):
        body(first + k)


def lane_iota(rows):
    return lax.broadcasted_iota(jnp.int32, (rows, 128), 1)


def roll(x, shift, axis):
    return pltpu.roll(x, shift % x.shape[axis], axis)


def exact_dot(x, sel):
    hi = x.astype(jnp.bfloat16)
    rest = x - hi.astype(jnp.float32)
    mid = rest.astype(jnp.bfloat16)
    low = (rest - mid.astype(jnp.float32)).astype(jnp.bfloat16)
    rows = x.shape[0]
    out = jnp.dot(
        jnp.concatenate([hi, mid, low], 0), sel, preferred_element_type=jnp.float32
    )
    return (out[:rows] + out[rows : 2 * rows]) + out[2 * rows :]


def restrict_matrix(level):
    width = min(LN[level], OY[level]) if OY[level] >= 128 else 128
    fine = lax.broadcasted_iota(jnp.int32, (width, 128), 0)
    coarse = lax.broadcasted_iota(jnp.int32, (width, 128), 1)
    hit = (fine // 2 == coarse) & (fine < OY[level])
    return jnp.where(hit, 0.25, 0.0).astype(jnp.bfloat16)


def prolong_matrix(level):
    lc, lf = LN[level + 1], LN[level]
    coarse = lax.broadcasted_iota(jnp.int32, (lc, lf), 0)
    fine = lax.broadcasted_iota(jnp.int32, (lc, lf), 1)
    middle = (OY[level] + lf) // 2
    source = jnp.where(fine < middle, fine // 2, lc - (lf - fine + 1) // 2)
    return jnp.where(source == coarse, 1.0, 0.0).astype(jnp.bfloat16)


class Message:
    def __init__(self, place, sems, index, src, dst, dx, dy):
        gx, gy, nx, ny = place
        self.to_there = (gx + dx >= 0) & (gx + dx < nx) & (gy + dy >= 0) & (gy + dy < ny)
        self.from_there = (gx - dx >= 0) & (gx - dx < nx) & (gy - dy >= 0) & (gy - dy < ny)
        target = (jnp.clip(gx + dx, 0, nx - 1), jnp.clip(gy + dy, 0, ny - 1))
        self.dst = dst
        self.copy = pltpu.make_async_remote_copy(
            src_ref=src,
            dst_ref=dst,
            send_sem=sems[0].at[index],
            recv_sem=sems[1].at[index],
            device_id=target,
            device_id_type=MESH,
        )

    def clear(self):
        @pl.when(jnp.logical_not(self.from_there))
        def _():
            self.dst[...] = jnp.zeros(self.dst.shape, self.dst.dtype)

    def start(self):
        @pl.when(self.to_there)
        def _():
            self.copy.start()

    def arrived(self):
        @pl.when(self.from_there)
        def _():
            self.copy.wait_recv()

    def sent(self):
        @pl.when(self.to_there)
        def _():
            self.copy.wait_send()


def pack_columns(level, source, dest, planes, rows, base, start=None):
    w, rim = PW[level], RIM[level]
    lane = lane_iota(planes)
    tile = (OY[level] - 1) // 128
    edge = (OY[level] - w) % 128
    zero = jnp.zeros((planes, 128), jnp.float32)
    left, right = (zero, zero) if start is None else (dest[start], dest[start + 1])
    for i in rows:
        here = (lane >= w * i) & (lane < w * i + w)
        a = source[rim + i, :, 0:128]
        b = source[rim + i, :, tile * 128 : tile * 128 + 128]
        left = jnp.where(here, roll(a, w * i, 1), left)
        right = jnp.where(here, roll(b, w * i - edge, 1), right)
    dest[base] = left
    dest[base + 1] = right


def unpack_columns(level, dest, packs, planes, reach, side):
    w, rim, own = PW[level], RIM[level], OX[level]
    lane = lane_iota(planes)
    last = LN[level] - 128
    start = OY[level] % 128
    row0, count, shift, slot = {
        -1: (-reach, reach, own - reach, 2),
        0: (0, own, 0, 0),
        1: (own, reach, 0, 4),
    }[side]
    for i in range(count):
        at = w * (i + shift)
        right = roll(packs[slot + 1], start - at, 1)
        left = roll(packs[slot], -w - at, 1)
        row = rim + row0 + i
        if OY[level] < 128:
            rest = dest[row, :, last : last + 128]
        else:
            rest = jnp.zeros((planes, 128), jnp.float32)
        tile = jnp.where((lane >= start) & (lane < start + w), right, rest)
        dest[row, :, last : last + 128] = jnp.where(lane >= 128 - w, left, tile)


def coefficients(level, c, e, y4, z, q, r, g, low, high):
    scale = 0.25**level
    half, cross = 0.5 * scale, CROSS * scale
    lanes, rim = LN[level], RIM[level]
    first, count = rim + low, high - low
    sub = lax.broadcasted_iota(jnp.int32, (8, lanes), 0)
    e[first - 1] = half * (c[first - 1, 0:16, :] + c[first, 0:16, :])

    def body(i):
        here = c[i, 0:16, :]
        north, south = roll(here, -1, 1), roll(here, 1, 1)
        east = half * (here + c[i + 1, 0:16, :])
        west = half * (here + c[i - 1, 0:16, :])
        nf, sf = half * (here + north), half * (here + south)
        e[i] = east
        y4[i, 0:16, :] = nf
        y4[i, 16:32, :] = sf
        y4[i, 32:48, :] = cross * north
        y4[i, 48:64, :] = cross * south
        even, odd = here[0:8], here[8:16]
        inner = 2.0 * (even + odd)
        upper = jnp.where(sub < 7, 2.0 * (odd + roll(even, -1, 0)), 0.0)
        lower = roll(upper, 1, 0)
        z[i, 0:8, :] = inner
        z[i, 8:16, :] = upper
        z[i, 16:24, :] = lower
        ice = c[i, 16:17, :]
        drag = jnp.where(sub == 0, c[i, 17:18, :], 0.0)
        vertical = jnp.concatenate([inner + lower + drag, inner + upper], 0)
        xs, ys = east + west, nf + sf
        for k, lateral in enumerate((4.0 * xs + ys, xs + 4.0 * ys)):
            diag = ice * (lateral + vertical) + (1.0 - ice)
            inv = OMEGA / diag
            if q is not None:
                q[i, 16 * k : 16 * k + 16, :] = inv
            r[i, 16 * k : 16 * k + 16, :] = ice * inv
            if g is not None:
                g[i, 16 * k : 16 * k + 16, :] = diag * (1.0 / OMEGA)

    over_rows(first, count, body, UNROLL_C[level])


def off_diagonal(w, e, y4, z, i):
    u0, u, u2 = w[i - 1, 0:16, :], w[i, 0:16, :], w[i + 1, 0:16, :]
    v0, v, v2 = w[i - 1, 16:32, :], w[i, 16:32, :], w[i + 1, 16:32, :]
    west, east = e[i - 1], e[i]
    nf, sf, mn, ms = (y4[i, 16 * k : 16 * k + 16, :] for k in range(4))
    inner, upper, lower = (z[i, 8 * k : 8 * k + 8, :] for k in range(3))
    du, dv, v4 = u2 - u0, v2 - v0, 4.0 * v
    xu = 4.0 * (east * u2 + west * u0)
    xv = east * v2 + west * v0
    yu = roll(sf * u + ms * dv, -1, 1) + roll(nf * u - mn * dv, 1, 1)
    yv = roll(sf * v4 + ms * du, -1, 1) + roll(nf * v4 - mn * du, 1, 1)

    def column(f):
        even, odd = f[0:8], f[8:16]
        return jnp.concatenate(
            [inner * odd + lower * roll(odd, 1, 0), inner * even + upper * roll(even, -1, 0)], 0
        )

    return (u, v), (xu + yu + column(u), xv + yv + column(v))


def sweep_row(src, dst, e, y4, z, r, tt, i):
    fields, sums = off_diagonal(src, e, y4, z, i)
    for k in range(2):
        at = slice(16 * k, 16 * k + 16)
        dst[i, at, :] = (1.0 - OMEGA) * fields[k] + (tt[i, at, :] + r[i, at, :] * sums[k])


def remainder_row(src, e, y4, z, r, tt, g, i, lanes):
    fields, sums = off_diagonal(src, e, y4, z, i)
    parts = []
    for k in range(2):
        at = slice(16 * k, 16 * k + 16)
        change = tt[i, at, :] + r[i, at, :] * sums[k] - OMEGA * fields[k]
        parts.append(change[:, 0:lanes] * g[i, at, 0:lanes])
    return jnp.concatenate(parts, 0)


def kernel(nx, ny, m_ref, v_ref, f_ref, i_ref, b_ref, o_ref, *scratch):
    names = iter(scratch)
    lv = []
    for level in range(4):
        keys = ["c", "e", "y4", "z", "r", "t", "a", "b"]
        keys += ["q"] if level > 0 else []
        keys += ["g"] if level < 3 else []
        keys += ["spc", "rpc", "spt", "rpt"] if level < 3 else []
        keys += ["raw"] if level == 0 else []
        lv.append({key: next(names) for key in keys})
    rest, far_c, far_t, side_c, side_t, fr, ic, gr = (next(names) for _ in range(8))
    in_sem, out_sem, send_sem, recv_sem = (next(names) for _ in range(4))

    gx, gy = lax.axis_index("gx"), lax.axis_index("gy")
    place = (gx, gy, nx, ny)
    sems = (send_sem, recv_sem)
    count = iter(range(10**6))

    def message(src, dst, dx, dy):
        return Message(place, sems, next(count), src, dst, dx, dy)

    def rim_messages(level, array, packs, landed, reach, corner):
        rim, own = RIM[level], OX[level]
        lanes = pl.ds(0, max(OY[level], 128))
        out = [
            message(
                array.at[pl.ds(rim, reach), :, lanes],
                array.at[pl.ds(rim + own, reach), :, lanes], -1, 0),
            message(
                array.at[pl.ds(rim + own - reach, reach), :, lanes],
                array.at[pl.ds(rim - reach, reach), :, lanes], 1, 0),
        ]
        for slot, (dx, dy) in enumerate(SIDES):
            pack = (0 if dy > 0 else 1) + (corner if dx != 0 else 0)
            out.append(message(packs.at[pack], landed.at[slot], -dx, -dy))
        return out

    def far_messages(far):
        order = [k * s for k in range(REACH, 0, -1) for s in (1, -1)]
        return {d: message(far.at[REACH], far.at[REACH - d], d, 0) for d in order}

    def side_messages(far, side):
        return [
            [message(far.at[b], side.at[0, b], 0, 1), message(far.at[b], side.at[1, b], 0, -1)]
            for b in range(FAR)
        ]

    c0, t0, raw = lv[0]["c"], lv[0]["t"], lv[0]["raw"]
    msg_c = [rim_messages(n, lv[n]["c"], lv[n]["spc"], lv[n]["rpc"], RIM[n], 0) for n in range(3)]
    msg_t = [
        rim_messages(
            n, lv[n]["t"] if n > 0 else raw, lv[n]["spt"], lv[n]["rpt"], RIM[n] - 1, 2 * (n == 1)
        )
        for n in range(3)
    ]
    msg_fc, msg_ft = far_messages(far_c), far_messages(far_t)
    msg_sc, msg_st = side_messages(far_c, side_c), side_messages(far_t, side_t)
    every = sum(msg_c + msg_t + msg_sc + msg_st, []) + list(msg_fc.values()) + list(msg_ft.values())

    own0 = pl.ds(RIM[0], OX[0])
    loads = []
    for k in range(16):
        kk = (k % 2) * 8 + k // 2
        loads.append((v_ref.at[k], lv[0]["c"].at[own0, kk, pl.ds(0, 256)]))
        for n in range(2):
            loads.append((m_ref.at[n, k], raw.at[own0, 16 * n + kk, pl.ds(0, 256)]))
    loads += [(f_ref, fr), (i_ref, ic), (b_ref, gr)]
    loads = [pltpu.make_async_copy(s, d, in_sem.at[n]) for n, (s, d) in enumerate(loads)]
    for load in loads:
        load.start()

    barrier = pltpu.get_barrier_semaphore()
    partners = [(d, 0) for d in range(-REACH, REACH + 1) if d != 0] + list(SIDES)
    arrivals = 0
    for dx, dy in partners:
        there = (gx + dx >= 0) & (gx + dx < nx) & (gy + dy >= 0) & (gy + dy < ny)
        arrivals = arrivals + there.astype(jnp.int32)

        @pl.when(there)
        def _(dx=dx, dy=dy):
            pl.semaphore_signal(
                barrier,
                inc=1,
                device_id=(jnp.clip(gx + dx, 0, nx - 1), jnp.clip(gy + dy, 0, ny - 1)),
                device_id_type=MESH,
            )

    for one in every:
        one.clear()
    for load in loads:
        load.wait()

    ic_f = ic[...].astype(jnp.float32)
    ic_f = ic_f.reshape(OX[0], 1, 256)
    dr_f = (fr[...] * gr[...].astype(jnp.float32)).reshape(OX[0], 1, 256)
    sub = lax.broadcasted_iota(jnp.int32, (OX[0], 8, 256), 1)
    c0[own0, 16:24, 0:256] = jnp.where(sub == 0, ic_f, jnp.where(sub == 1, dr_f, 0.0))

    pack_columns(0, c0, lv[0]["spc"], 24, range(OX[0]), 0)
    pack_columns(0, raw, lv[0]["spt"], 32, range(OX[0]), 0)

    for level in range(3):
        rim, own, width = RIM[level], OX[level + 1], max(OY[level], 128)
        fine = lv[level]["c"]
        block = fine[rim : rim + 2 * own, :, 0:width].reshape(own, 2, 24, width)
        block = (block[:, 0] + block[:, 1]).reshape(own * 24, width)
        coarse = exact_dot(block, restrict_matrix(level)).reshape(own, 24, 128)
        if level < 2:
            target = lv[level + 1]["c"]
            target[RIM[level + 1] : RIM[level + 1] + own, :, 0:128] = coarse
            pack_columns(level + 1, target, lv[level + 1]["spc"], 24, range(own), 0)
        else:
            far_c[REACH] = sum(roll(coarse[k], 32 * k, 1) for k in range(4))

    pl.semaphore_wait(barrier, arrivals)
    for one in msg_c[0][2:4] + msg_t[0][2:4] + msg_c[0][:2] + msg_t[0][:2]:
        one.start()
    for one in msg_c[0][4:] + msg_t[0][4:] + msg_c[1] + msg_c[2] + list(msg_fc.values()):
        one.start()
    for one in msg_sc[REACH]:
        one.start()

    def refs(level):
        return [lv[level][key] for key in ("e", "y4", "z", "r", "t")]

    def gather(level, kind, messages, planes, reach, sides):
        landed = lv[level]["rp" + kind]
        array = raw if (level, kind) == (0, "t") else lv[level][kind]
        for side in sides:
            which = {0: messages[2:4], -1: messages[1:2] + messages[4:6], 1: messages[0:1] + messages[6:8]}
            for one in which[side]:
                one.arrived()
        if OY[level] < 128 and 0 in sides:
            for one in messages[:2]:
                one.sent()
        for side in sides:
            unpack_columns(level, array, landed, planes, reach, side)

    def first_sweep(level, low, high):
        t = lv[level]["t"]
        source, factor = (raw, lv[0]["r"]) if level == 0 else (t, lv[level]["q"])

        def body(i):
            t[i] = source[i] * factor[i]

        over_rows(RIM[level] + low, high - low, body, min(4, high - low))

    def sweep_range(level, src, dst, low, high):
        args = refs(level)

        over_rows(
            RIM[level] + low,
            high - low,
            lambda i: sweep_row(src, dst, *args, i),
            UNROLL[level],
        )

    def sweep(level, src, dst, rows):
        sweep_range(level, src, dst, -rows, OX[level] + rows)

    def restricted_remainder(level, src, ranges):
        args = refs(level)
        width = max(OY[level], 128)

        def body(n):
            i = RIM[level] + 2 * n
            pair = [remainder_row(src, *args, lv[level]["g"], i + k, width) for k in range(2)]
            rest[n, :, 0:width] = pair[0] + pair[1]

        for low, high in ranges:
            over_rows(low, high - low, body, UNROLL_R[level])
        block = jnp.concatenate([rest[low:high, :, 0:width] for low, high in ranges], 0)
        own = block.shape[0]
        block = block.reshape(own * 32, width)
        return exact_dot(block, restrict_matrix(level)).reshape(own, 32, 128)

    def prolonged(level, src, dst, rows):
        low, high = RIM[level + 1] - rows, RIM[level + 1] + OX[level + 1] + rows
        n = high - low
        sel = prolong_matrix(level)
        spread = lv[level]["g"]
        block = src[low:high].reshape(n * 32, LN[level + 1])
        spread[0:n] = exact_dot(block, sel).reshape(n, 32, LN[level])

        def body(k):
            i = RIM[level] + 2 * (k - rows)
            extra = spread[k]
            dst[i] = dst[i] + extra
            dst[i + 1] = dst[i + 1] + extra

        over_rows(0, n, body, 2)

    def all_coefficients(level, low, high):
        refs_c = [lv[level].get(k) for k in ("c", "e", "y4", "z", "q", "r", "g")]
        coefficients(level, *refs_c, low, high)

    n0, h0 = OX[0], RIM[0] - 1
    gather(0, "c", msg_c[0], 24, RIM[0], (0,))
    gather(0, "t", msg_t[0], 32, h0, (0,))
    all_coefficients(0, 1, n0 - 1)
    first_sweep(0, 1, n0 - 1)
    sweep_range(0, t0, lv[0]["a"], 2, n0 - 2)
    gather(0, "c", msg_c[0], 24, RIM[0], (-1, 1))
    gather(0, "t", msg_t[0], 32, h0, (-1, 1))
    for low, high in ((-h0, 1), (n0 - 1, n0 + h0)):
        all_coefficients(0, low, high)
        first_sweep(0, low, high)
    for low, high in ((1 - h0, 2), (n0 - 2, n0 + h0 - 1)):
        sweep_range(0, t0, lv[0]["a"], low, high)

    t1, h1, n1 = lv[1]["t"], RIM[1] - 1, OX[1]
    own1 = restricted_remainder(0, lv[0]["a"], [(0, h1), (n1 - h1, n1)])
    t1[RIM[1] : RIM[1] + h1, :, 0:128] = own1[:h1]
    t1[RIM[1] + n1 - h1 : RIM[1] + n1, :, 0:128] = own1[h1:]
    for one in msg_t[1][:2]:
        one.start()
    ends = [*range(h1), *range(n1 - h1, n1)]
    pack_columns(1, t1, lv[1]["spt"], 32, ends, 2)
    for one in msg_t[1][4:]:
        one.start()
    t1[RIM[1] + h1 : RIM[1] + n1 - h1, :, 0:128] = restricted_remainder(
        0, lv[0]["a"], [(h1, n1 - h1)]
    )
    pack_columns(1, t1, lv[1]["spt"], 32, range(h1, n1 - h1), 0, 2)
    for one in msg_t[1][2:4]:
        one.start()

    for level in (1, 2):
        t, own, h = lv[level]["t"], OX[level], RIM[level] - 1
        if level == 2:
            t[RIM[2] : RIM[2] + own, :, 0:128] = restricted_remainder(1, lv[1]["a"], [(0, own)])
            for one in msg_t[2][:2]:
                one.start()
            pack_columns(2, t, lv[2]["spt"], 32, range(own), 0)
            for one in msg_t[2][4:] + msg_t[2][2:4]:
                one.start()
        gather(level, "c", msg_c[level], 24, RIM[level], (0, -1, 1))
        all_coefficients(level, -h, own + h)
        if level == 1:
            for d in range(1, REACH + 1):
                for s in (d, -d):
                    msg_fc[s].arrived()
                    for one in msg_sc[REACH - s]:
                        one.start()
        gather(level, "t", msg_t[level], 32, h, (0,))
        for one in [] if OY[level] < 128 else msg_t[level][:2]:
            one.sent()
        first_sweep(level, 0, own)
        sweep_range(level, t, lv[level]["a"], 1, own - 1)
        gather(level, "t", msg_t[level], 32, h, (-1, 1))
        first_sweep(level, -h, 0)
        first_sweep(level, own, own + h)
        sweep_range(level, t, lv[level]["a"], 1 - h, 1)
        sweep_range(level, t, lv[level]["a"], own - 1, own + h - 1)

    t_next = restricted_remainder(2, lv[2]["a"], [(0, OX[3])])
    far_t[REACH] = sum(roll(t_next[k], 32 * k, 1) for k in range(4))
    for one in list(msg_ft.values()) + msg_st[REACH]:
        one.start()

    def unpack_far(dest, far, side, planes, factor):
        lane = lane_iota(planes)

        def body(b):
            own, left, right = far[b], side[0, b], side[1, b]
            for k in range(4):
                tile = jnp.where(lane < 32, roll(own, -32 * k, 1), 0.0)
                tile = jnp.where((lane >= 32) & (lane < 64), roll(right, 32 - 32 * k, 1), tile)
                tile = jnp.where(lane >= 96, roll(left, 96 - 32 * k, 1), tile)
                dest[4 * b + k] = tile if factor is None else tile * factor[4 * b + k]

        over_rows(0, FAR, body, 2)

    for pair in msg_sc:
        for one in pair:
            one.arrived()
    q3 = lv[3]["q"]
    unpack_far(lv[3]["c"], far_c, side_c, 24, None)
    all_coefficients(3, 1 - RIM[3], OX[3] + RIM[3] - 1)
    q3[0] = q3[1]
    q3[OX[3] + 2 * RIM[3] - 1] = q3[1]
    for d in range(1, REACH + 1):
        for s in (d, -d):
            msg_ft[s].arrived()
            for one in msg_st[REACH - s]:
                one.start()
    for pair in msg_st:
        for one in pair:
            one.arrived()
    t3, a3, b3 = lv[3]["t"], lv[3]["a"], lv[3]["b"]
    unpack_far(t3, far_t, side_t, 32, q3)
    args3 = refs(3)

    def coarse_sweep(src, dst, s):
        first = s + 2

        def body(n, _):
            for k in range(UNROLL[3]):
                sweep_row(src, dst, *args3, first + UNROLL[3] * n + k)
            return 0

        lax.fori_loop(0, (47 - 2 * s + UNROLL[3]) // UNROLL[3], body, 0)

    coarse_sweep(t3, a3, 2)

    def coarse_pair(n, _):
        coarse_sweep(a3, b3, 2 * n + 3)
        coarse_sweep(b3, a3, 2 * n + 4)
        return 0

    lax.fori_loop(0, (ITERS - 2) // 2, coarse_pair, 0)

    prolonged(2, a3, lv[2]["a"], 2)
    sweep(2, lv[2]["a"], lv[2]["b"], 3)
    sweep(2, lv[2]["b"], lv[2]["a"], 2)
    prolonged(1, lv[2]["a"], lv[1]["a"], 2)
    sweep(1, lv[1]["a"], lv[1]["b"], 2)
    sweep(1, lv[1]["b"], lv[1]["a"], 1)
    prolonged(0, lv[1]["a"], lv[0]["a"], 1)
    a0, b0 = lv[0]["a"], lv[0]["b"]
    sweep(0, a0, b0, 1)
    args0 = refs(0)
    stores = []
    for part in range(2):
        first = RIM[0] + 16 * part

        over_rows(first, 16, lambda i: sweep_row(b0, a0, *args0, i), UNROLL[0])
        for n in range(2):
            for k in range(16):
                kk = (k % 2) * 8 + k // 2
                store = pltpu.make_async_copy(
                    a0.at[pl.ds(first, 16), 16 * n + kk, pl.ds(0, 256)],
                    o_ref.at[n, k, pl.ds(16 * part, 16), :],
                    out_sem.at[32 * part + 16 * n + k],
                )
                store.start()
                stores.append(store)
    waited = msg_t[1][:2] + msg_t[2][:2] + msg_c[2][:2]
    for one in every:
        if one not in waited:
            one.sent()
    for store in stores:
        store.wait()


def solution(mesh):
    nx, ny = mesh.shape["gx"], mesh.shape["gy"]
    f32 = jnp.float32
    scratch = []
    for level in range(4):
        rows, lanes = TX[level], LN[level]
        planes = [24, 16, 64, 24, 32, 32, 32, 32]
        planes += [32] if level > 0 else []
        planes += [32] if level < 3 else []
        scratch += [pltpu.VMEM((rows, p, lanes), f32) for p in planes]
        if level < 3:
            scratch += [pltpu.VMEM((n, p, 128), f32) for p in (24, 32) for n in (4, 6)]
        if level == 0:
            scratch += [pltpu.VMEM((rows, 32, lanes), f32)]
    scratch += [pltpu.VMEM((16, 32, 256), f32)]
    scratch += [pltpu.VMEM((FAR, 24, 128), f32), pltpu.VMEM((FAR, 32, 128), f32)]
    scratch += [pltpu.VMEM((2, FAR, 24, 128), f32), pltpu.VMEM((2, FAR, 32, 128), f32)]
    scratch += [
        pltpu.VMEM((32, 256), f32),
        pltpu.VMEM((32, 256), jnp.int32),
        pltpu.VMEM((32, 256), jnp.int32),
    ]
    messages = 6 * 8 + 4 * REACH + 4 * FAR
    scratch += [pltpu.SemaphoreType.DMA((51,)), pltpu.SemaphoreType.DMA((64,))]
    scratch += [pltpu.SemaphoreType.DMA((messages,)), pltpu.SemaphoreType.DMA((messages,))]

    def per_device(misfit, viscosity, friction, ice_mask, grounded):
        return pl.pallas_call(
            functools.partial(kernel, nx, ny),
            out_shape=jax.ShapeDtypeStruct(misfit.shape, f32),
            in_specs=[pl.BlockSpec(memory_space=HBM)] * 5,
            out_specs=pl.BlockSpec(memory_space=HBM),
            scratch_shapes=scratch,
            compiler_params=pltpu.CompilerParams(
                collective_id=0, has_side_effects=True, vmem_limit_bytes=62 * 2**20
            ),
        )(misfit, viscosity, friction, ice_mask, grounded)

    placed = (
        P(None, None, "gx", "gy"),
        P(None, "gx", "gy"),
        P("gx", "gy"),
        P("gx", "gy"),
        P("gx", "gy"),
    )
    return jax.shard_map(
        per_device, mesh=mesh, in_specs=placed, out_specs=P(None, None, "gx", "gy"), check_vma=False
    )
```

```python
import functools

import jax
import jax.numpy as jnp
from jax import lax
from jax.experimental import pallas as pl
from jax.experimental.pallas import tpu as pltpu
from jax.sharding import PartitionSpec as P

MESH = pl.DeviceIdType.MESH
HBM = pltpu.MemorySpace.HBM
OMEGA = 0.6
CROSS = 0.75
ITERS = 20

OX = (32, 16, 8, 4)
OY = (256, 128, 64, 32)
LN = (384, 256, 128, 128)
RIM = (4, 5, 6, 24)
PW = (4, 8, 16, 32)
TX = tuple(o + 2 * h for o, h in zip(OX[:3], RIM)) + (58,)
UNROLL = (2, 3, 6, 8)
UNROLL_C = (2, 3, 6, 5)
UNROLL_R = (1, 2, 4)
DIRECT = 6
REACH = 6
FAR = 2 * REACH + 1
SIDES = ((0, -1), (0, 1), (-1, -1), (-1, 1), (1, -1), (1, 1))


def over_rows(first, count, body, unroll):
    steps = count // unroll

    def step(n, _):
        for k in range(unroll):
            body(first + n * unroll + k)
        return 0

    if steps > 0:
        lax.fori_loop(0, steps, step, 0)
    for k in range(steps * unroll, count):
        body(first + k)


def lane_iota(rows):
    return lax.broadcasted_iota(jnp.int32, (rows, 128), 1)


def roll(x, shift, axis):
    return pltpu.roll(x, shift % x.shape[axis], axis)


def exact_dot(x, sel):
    hi = x.astype(jnp.bfloat16)
    rest = x - hi.astype(jnp.float32)
    mid = rest.astype(jnp.bfloat16)
    low = (rest - mid.astype(jnp.float32)).astype(jnp.bfloat16)
    rows = x.shape[0]
    out = jnp.dot(
        jnp.concatenate([hi, mid, low], 0), sel, preferred_element_type=jnp.float32
    )
    return (out[:rows] + out[rows : 2 * rows]) + out[2 * rows :]


def restrict_matrix(level):
    width = min(LN[level], OY[level]) if OY[level] >= 128 else 128
    fine = lax.broadcasted_iota(jnp.int32, (width, 128), 0)
    coarse = lax.broadcasted_iota(jnp.int32, (width, 128), 1)
    hit = (fine // 2 == coarse) & (fine < OY[level])
    return jnp.where(hit, 0.25, 0.0).astype(jnp.bfloat16)


def prolong_matrix(level):
    lc, lf = LN[level + 1], LN[level]
    coarse = lax.broadcasted_iota(jnp.int32, (lc, lf), 0)
    fine = lax.broadcasted_iota(jnp.int32, (lc, lf), 1)
    middle = (OY[level] + lf) // 2
    source = jnp.where(fine < middle, fine // 2, lc - (lf - fine + 1) // 2)
    return jnp.where(source == coarse, 1.0, 0.0).astype(jnp.bfloat16)


class Message:
    def __init__(self, place, sems, index, src, dst, dx, dy):
        gx, gy, nx, ny = place
        self.way = (dx, dy)
        self.to_there = (gx + dx >= 0) & (gx + dx < nx) & (gy + dy >= 0) & (gy + dy < ny)
        self.from_there = (gx - dx >= 0) & (gx - dx < nx) & (gy - dy >= 0) & (gy - dy < ny)
        target = (jnp.clip(gx + dx, 0, nx - 1), jnp.clip(gy + dy, 0, ny - 1))
        self.dst = dst
        self.pending = []
        self.copy = pltpu.make_async_remote_copy(
            src_ref=src,
            dst_ref=dst,
            send_sem=sems[0].at[index],
            recv_sem=sems[1].at[index],
            device_id=target,
            device_id_type=MESH,
        )


def by_way(messages):
    groups = {}
    for one in messages:
        groups.setdefault(one.way, []).append(one)
    return groups.values()


def clear(messages):
    for group in by_way(messages):

        @pl.when(jnp.logical_not(group[0].from_there))
        def _(group=group):
            for one in group:
                one.dst[...] = jnp.zeros(one.dst.shape, one.dst.dtype)


def start(messages):
    for group in by_way(messages):

        @pl.when(group[0].to_there)
        def _(group=group):
            for one in group:
                one.copy.start()

    for one in messages:
        one.pending = ["arrived", "sent"]


def arrived(messages):
    for group in by_way(messages):

        @pl.when(group[0].from_there)
        def _(group=group):
            for one in group:
                one.copy.wait_recv()

    for one in messages:
        one.pending.remove("arrived")


def sent(messages):
    for group in by_way(messages):

        @pl.when(group[0].to_there)
        def _(group=group):
            for one in group:
                one.copy.wait_send()

    for one in messages:
        one.pending.remove("sent")


def pack_columns(level, source, dest, planes):
    w, rim = PW[level], RIM[level]
    lane = lane_iota(planes)
    tile = (OY[level] - 1) // 128
    edge = (OY[level] - w) % 128
    zero = jnp.zeros((planes, 128), jnp.float32)
    left, right = zero, zero
    for i in range(OX[level]):
        here = (lane >= w * i) & (lane < w * i + w)
        a = source[rim + i, :, 0:128]
        b = source[rim + i, :, tile * 128 : tile * 128 + 128]
        left = jnp.where(here, roll(a, w * i, 1), left)
        right = jnp.where(here, roll(b, w * i - edge, 1), right)
    dest[0] = left
    dest[1] = right


def unpack_columns(level, dest, packs, planes, reach, side):
    w, rim, own = PW[level], RIM[level], OX[level]
    lane = lane_iota(planes)
    last = LN[level] - 128
    start = OY[level] % 128
    row0, count, shift, slot = {
        -1: (-reach, reach, own - reach, 2),
        0: (0, own, 0, 0),
        1: (own, reach, 0, 4),
    }[side]
    for i in range(count):
        at = w * (i + shift)
        right = roll(packs[slot + 1], start - at, 1)
        left = roll(packs[slot], -w - at, 1)
        row = rim + row0 + i
        if OY[level] < 128:
            rest = dest[row, :, last : last + 128]
        else:
            rest = jnp.zeros((planes, 128), jnp.float32)
        tile = jnp.where((lane >= start) & (lane < start + w), right, rest)
        dest[row, :, last : last + 128] = jnp.where(lane >= 128 - w, left, tile)


def coefficients(level, c, e, y4, z, q, r, g, low, high):
    scale = 0.25**level
    half, cross = 0.5 * scale, CROSS * scale
    lanes, rim = LN[level], RIM[level]
    first, count = rim + low, high - low
    sub = lax.broadcasted_iota(jnp.int32, (8, lanes), 0)
    e[first - 1] = half * (c[first - 1, 0:16, :] + c[first, 0:16, :])

    def body(i):
        here = c[i, 0:16, :]
        north, south = roll(here, -1, 1), roll(here, 1, 1)
        east = half * (here + c[i + 1, 0:16, :])
        west = half * (here + c[i - 1, 0:16, :])
        nf, sf = half * (here + north), half * (here + south)
        e[i] = east
        y4[i, 0:16, :] = nf
        y4[i, 16:32, :] = sf
        y4[i, 32:48, :] = cross * north
        y4[i, 48:64, :] = cross * south
        even, odd = here[0:8], here[8:16]
        inner = 2.0 * (even + odd)
        upper = jnp.where(sub < 7, 2.0 * (odd + roll(even, -1, 0)), 0.0)
        lower = roll(upper, 1, 0)
        z[i, 0:8, :] = inner
        z[i, 8:16, :] = upper
        z[i, 16:24, :] = lower
        ice = c[i, 16:17, :]
        drag = jnp.where(sub == 0, c[i, 17:18, :], 0.0)
        vertical = jnp.concatenate([inner + lower + drag, inner + upper], 0)
        xs, ys = east + west, nf + sf
        for k, lateral in enumerate((4.0 * xs + ys, xs + 4.0 * ys)):
            diag = ice * (lateral + vertical) + (1.0 - ice)
            inv = OMEGA / diag
            if q is not None:
                q[i, 16 * k : 16 * k + 16, :] = inv
            r[i, 16 * k : 16 * k + 16, :] = ice * inv
            if g is not None:
                g[i, 16 * k : 16 * k + 16, :] = diag * (1.0 / OMEGA)

    over_rows(first, count, body, UNROLL_C[level])


def off_diagonal(w, e, y4, z, i):
    u0, u, u2 = w[i - 1, 0:16, :], w[i, 0:16, :], w[i + 1, 0:16, :]
    v0, v, v2 = w[i - 1, 16:32, :], w[i, 16:32, :], w[i + 1, 16:32, :]
    west, east = e[i - 1], e[i]
    nf, sf, mn, ms = (y4[i, 16 * k : 16 * k + 16, :] for k in range(4))
    inner, upper, lower = (z[i, 8 * k : 8 * k + 8, :] for k in range(3))
    du, dv, v4 = u2 - u0, v2 - v0, 4.0 * v
    xu = 4.0 * (east * u2 + west * u0)
    xv = east * v2 + west * v0
    yu = roll(sf * u + ms * dv, -1, 1) + roll(nf * u - mn * dv, 1, 1)
    yv = roll(sf * v4 + ms * du, -1, 1) + roll(nf * v4 - mn * du, 1, 1)

    def column(f):
        even, odd = f[0:8], f[8:16]
        return jnp.concatenate(
            [inner * odd + lower * roll(odd, 1, 0), inner * even + upper * roll(even, -1, 0)], 0
        )

    return (u, v), (xu + yu + column(u), xv + yv + column(v))


def sweep_row(src, dst, e, y4, z, r, tt, i):
    fields, sums = off_diagonal(src, e, y4, z, i)
    for k in range(2):
        at = slice(16 * k, 16 * k + 16)
        dst[i, at, :] = (1.0 - OMEGA) * fields[k] + (tt[i, at, :] + r[i, at, :] * sums[k])


def remainder_row(src, e, y4, z, r, tt, g, i, lanes):
    fields, sums = off_diagonal(src, e, y4, z, i)
    parts = []
    for k in range(2):
        at = slice(16 * k, 16 * k + 16)
        change = tt[i, at, :] + r[i, at, :] * sums[k] - OMEGA * fields[k]
        parts.append(change[:, 0:lanes] * g[i, at, 0:lanes])
    return jnp.concatenate(parts, 0)


def kernel(nx, ny, m_ref, v_ref, f_ref, i_ref, b_ref, o_ref, *scratch):
    names = iter(scratch)
    lv = []
    for level in range(4):
        keys = ["c", "e", "y4", "z", "r", "t", "a", "b"]
        keys += ["q"] if level > 0 else []
        keys += ["g"] if level < 3 else []
        keys += ["spc", "rpc", "spt", "rpt"] if level < 3 else []
        keys += ["raw"] if level == 0 else []
        lv.append({key: next(names) for key in keys})
    rest, far_c, far_t, side_c, side_t, fr, ic, gr = (next(names) for _ in range(8))
    in_sem, out_sem, send_sem, recv_sem = (next(names) for _ in range(4))

    gx, gy = lax.axis_index("gx"), lax.axis_index("gy")
    place = (gx, gy, nx, ny)
    sems = (send_sem, recv_sem)
    count = iter(range(10**6))

    def message(src, dst, dx, dy):
        return Message(place, sems, next(count), src, dst, dx, dy)

    def rim_messages(level, array, packs, landed, reach):
        rim, own = RIM[level], OX[level]
        lanes = pl.ds(0, max(OY[level], 128))
        out = [
            message(
                array.at[pl.ds(rim, reach), :, lanes],
                array.at[pl.ds(rim + own, reach), :, lanes], -1, 0),
            message(
                array.at[pl.ds(rim + own - reach, reach), :, lanes],
                array.at[pl.ds(rim - reach, reach), :, lanes], 1, 0),
        ]
        for slot, (dx, dy) in enumerate(SIDES):
            out.append(message(packs.at[0 if dy > 0 else 1], landed.at[slot], -dx, -dy))
        return out

    def far_messages(far, side):
        out = []
        for d in [k * s for k in range(REACH, 0, -1) for s in (1, -1)]:
            out.append(message(far.at[REACH], far.at[REACH - d], d, 0))
            for n in range(2 if abs(d) > DIRECT else 0):
                out.append(message(far.at[REACH], side.at[n, REACH - d], d, 1 - 2 * n))
        return out

    def side_messages(far, side):
        near = pl.ds(REACH - DIRECT, 2 * DIRECT + 1)
        whole = [message(far.at[near], side.at[n, near], 0, 1 - 2 * n) for n in range(2)]
        first = next(count) - 2
        blocks = {
            b: [
                Message(place, sems, first + n, far.at[b], side.at[n, b], 0, 1 - 2 * n)
                for n in range(2)
            ]
            for b in range(REACH - DIRECT, REACH + DIRECT + 1)
        }
        return whole, blocks

    def pass_on(far, side):
        for d in range(1, DIRECT + 1):
            for s in (d, -d):
                arrived([one for one in far if one.way == (s, 0)])
                start(side[REACH - s])

    c0, t0, raw = lv[0]["c"], lv[0]["t"], lv[0]["raw"]
    msg_c = [rim_messages(n, lv[n]["c"], lv[n]["spc"], lv[n]["rpc"], RIM[n]) for n in range(3)]
    msg_t = [
        rim_messages(
            n, lv[n]["t"] if n > 0 else raw, lv[n]["spt"], lv[n]["rpt"], RIM[n] - 1
        )
        for n in range(3)
    ]
    msg_fc, msg_ft = far_messages(far_c, side_c), far_messages(far_t, side_t)
    all_sc, msg_sc = side_messages(far_c, side_c)
    all_st, msg_st = side_messages(far_t, side_t)
    every = sum(msg_c + msg_t, []) + msg_fc + msg_ft + all_sc + all_st

    barrier = pltpu.get_barrier_semaphore()
    far_away = [d for d in range(-REACH, REACH + 1) if abs(d) > DIRECT]
    partners = [(d, 0) for d in range(-REACH, REACH + 1) if d != 0] + list(SIDES)
    partners += [(d, s) for d in far_away for s in (-1, 1)]
    arrivals = 0
    for dx, dy in partners:
        there = (gx + dx >= 0) & (gx + dx < nx) & (gy + dy >= 0) & (gy + dy < ny)
        arrivals = arrivals + there.astype(jnp.int32)

        @pl.when(there)
        def _(dx=dx, dy=dy):
            pl.semaphore_signal(
                barrier,
                inc=1,
                device_id=(jnp.clip(gx + dx, 0, nx - 1), jnp.clip(gy + dy, 0, ny - 1)),
                device_id_type=MESH,
            )

    own0 = pl.ds(RIM[0], OX[0])
    loads = []
    for k in range(16):
        kk = (k % 2) * 8 + k // 2
        loads.append((v_ref.at[k], lv[0]["c"].at[own0, kk, pl.ds(0, 256)]))
        for n in range(2):
            loads.append((m_ref.at[n, k], raw.at[own0, 16 * n + kk, pl.ds(0, 256)]))
    loads += [(f_ref, fr), (i_ref, ic), (b_ref, gr)]
    loads = [pltpu.make_async_copy(s, d, in_sem.at[n]) for n, (s, d) in enumerate(loads)]
    for load in loads:
        load.start()

    clear(every)
    for load in loads:
        load.wait()

    ic_f = ic[...].astype(jnp.float32)
    ic_f = ic_f.reshape(OX[0], 1, 256)
    dr_f = (fr[...] * gr[...].astype(jnp.float32)).reshape(OX[0], 1, 256)
    sub = lax.broadcasted_iota(jnp.int32, (OX[0], 8, 256), 1)
    c0[own0, 16:24, 0:256] = jnp.where(sub == 0, ic_f, jnp.where(sub == 1, dr_f, 0.0))

    pack_columns(0, c0, lv[0]["spc"], 24)
    pack_columns(0, raw, lv[0]["spt"], 32)

    pl.semaphore_wait(barrier, arrivals)
    start(msg_c[0][2:4] + msg_t[0][2:4])
    start(msg_c[0][:2] + msg_t[0][:2] + msg_c[0][4:] + msg_t[0][4:])

    for level in range(3):
        rim, own, width = RIM[level], OX[level + 1], max(OY[level], 128)
        fine = lv[level]["c"]
        block = fine[rim : rim + 2 * own, :, 0:width].reshape(own, 2, 24, width)
        block = (block[:, 0] + block[:, 1]).reshape(own * 24, width)
        coarse = exact_dot(block, restrict_matrix(level)).reshape(own, 24, 128)
        if level < 2:
            target = lv[level + 1]["c"]
            target[RIM[level + 1] : RIM[level + 1] + own, :, 0:128] = coarse
            pack_columns(level + 1, target, lv[level + 1]["spc"], 24)
        else:
            far_c[REACH] = sum(roll(coarse[k], 32 * k, 1) for k in range(4))

    def refs(level):
        return [lv[level][key] for key in ("e", "y4", "z", "r", "t")]

    def gather(level, kind, messages, planes, reach, sides):
        landed = lv[level]["rp" + kind]
        array = raw if (level, kind) == (0, "t") else lv[level][kind]
        for side in sides:
            which = {0: messages[2:4], -1: messages[1:2] + messages[4:6], 1: messages[0:1] + messages[6:8]}
            arrived(which[side])
        if OY[level] < 128 and 0 in sides:
            sent(messages[:2])
        for side in sides:
            unpack_columns(level, array, landed, planes, reach, side)

    def first_sweep(level, low, high):
        t = lv[level]["t"]
        source, factor = (raw, lv[0]["r"]) if level == 0 else (t, lv[level]["q"])

        def body(i):
            t[i] = source[i] * factor[i]

        over_rows(RIM[level] + low, high - low, body, min(4, high - low))

    def sweep_range(level, src, dst, low, high):
        args = refs(level)

        over_rows(
            RIM[level] + low,
            high - low,
            lambda i: sweep_row(src, dst, *args, i),
            UNROLL[level],
        )

    def sweep(level, src, dst, rows):
        sweep_range(level, src, dst, -rows, OX[level] + rows)

    def remainder_rows(level, src, low, high):
        args = refs(level)
        width = max(OY[level], 128)

        def body(n):
            i = RIM[level] + 2 * n
            pair = [remainder_row(src, *args, lv[level]["g"], i + k, width) for k in range(2)]
            rest[n, :, 0:width] = pair[0] + pair[1]

        over_rows(low, high - low, body, min(UNROLL_R[level], high - low))

    def restricted(level):
        width, own = max(OY[level], 128), OX[level + 1]
        block = rest[0:own, :, 0:width].reshape(own * 32, width)
        return exact_dot(block, restrict_matrix(level)).reshape(own, 32, 128)

    def prolonged(level, src, dst, rows):
        low, high = RIM[level + 1] - rows, RIM[level + 1] + OX[level + 1] + rows
        n = high - low
        sel = prolong_matrix(level)
        spread = lv[level]["g"]
        block = src[low:high].reshape(n * 32, LN[level + 1])
        spread[0:n] = exact_dot(block, sel).reshape(n, 32, LN[level])

        def body(k):
            i = RIM[level] + 2 * (k - rows)
            extra = spread[k]
            dst[i] = dst[i] + extra
            dst[i + 1] = dst[i + 1] + extra

        over_rows(0, n, body, 2)

    def all_coefficients(level, low, high):
        refs_c = [lv[level].get(k) for k in ("c", "e", "y4", "z", "q", "r", "g")]
        coefficients(level, *refs_c, low, high)

    n0, h0 = OX[0], RIM[0] - 1
    gather(0, "c", msg_c[0], 24, RIM[0], (0,))
    gather(0, "t", msg_t[0], 32, h0, (0,))
    all_coefficients(0, 1, n0 - 1)
    start(msg_c[1] + msg_c[2])
    first_sweep(0, 1, n0 - 1)
    sweep_range(0, t0, lv[0]["a"], 2, n0 - 2)
    remainder_rows(0, lv[0]["a"], 2, OX[1] - 2)
    gather(0, "c", msg_c[0], 24, RIM[0], (-1, 1))
    gather(0, "t", msg_t[0], 32, h0, (-1, 1))
    for low, high in ((-h0, 1), (n0 - 1, n0 + h0)):
        all_coefficients(0, low, high)
        first_sweep(0, low, high)
    for low, high in ((1 - h0, 2), (n0 - 2, n0 + h0 - 1)):
        sweep_range(0, t0, lv[0]["a"], low, high)
    for low, high in ((0, 2), (OX[1] - 2, OX[1])):
        remainder_rows(0, lv[0]["a"], low, high)

    for level in (1, 2):
        t, own, h = lv[level]["t"], OX[level], RIM[level] - 1
        if level == 2:
            remainder_rows(1, lv[1]["a"], 0, own)
        t[RIM[level] : RIM[level] + own, :, 0:128] = restricted(level - 1)
        start(msg_t[level][:2])
        pack_columns(level, t, lv[level]["spt"], 32)
        start(msg_t[level][4:] + msg_t[level][2:4])
        if level == 2:
            pass_on(msg_fc, msg_sc)
        gather(level, "c", msg_c[level], 24, RIM[level], (0, -1, 1))
        all_coefficients(level, -h, own + h)
        gather(level, "t", msg_t[level], 32, h, (0,))
        if OY[level] >= 128:
            sent(msg_t[level][:2])
            start(msg_fc + msg_sc[REACH])
        first_sweep(level, 0, own)
        sweep_range(level, t, lv[level]["a"], 1, own - 1)
        gather(level, "t", msg_t[level], 32, h, (-1, 1))
        first_sweep(level, -h, 0)
        first_sweep(level, own, own + h)
        sweep_range(level, t, lv[level]["a"], 1 - h, 1)
        sweep_range(level, t, lv[level]["a"], own - 1, own + h - 1)

    remainder_rows(2, lv[2]["a"], 0, OX[3])
    t_next = restricted(2)
    far_t[REACH] = sum(roll(t_next[k], 32 * k, 1) for k in range(4))
    start(msg_ft + msg_st[REACH])

    def unpack_far(dest, far, side, planes, factor):
        lane = lane_iota(planes)

        def body(b):
            own, left, right = far[b], side[0, b], side[1, b]
            for k in range(4):
                tile = jnp.where(lane < 32, roll(own, -32 * k, 1), 0.0)
                tile = jnp.where((lane >= 32) & (lane < 64), roll(right, 32 - 32 * k, 1), tile)
                tile = jnp.where(lane >= 96, roll(left, 96 - 32 * k, 1), tile)
                dest[4 * b + k] = tile if factor is None else tile * factor[4 * b + k]

        over_rows(0, FAR, body, 2)

    for one in all_sc + all_st:
        one.pending = ["arrived", "sent"]
    arrived(all_sc + [one for one in msg_fc if "arrived" in one.pending])
    q3 = lv[3]["q"]
    unpack_far(lv[3]["c"], far_c, side_c, 24, None)
    all_coefficients(3, 1 - RIM[3], OX[3] + RIM[3] - 1)
    q3[0] = q3[1]
    q3[OX[3] + 2 * RIM[3] - 1] = q3[1]
    pass_on(msg_ft, msg_st)
    sent([one for one in every if one.pending == ["sent"]])
    arrived([one for one in msg_ft if "arrived" in one.pending] + all_st)
    t3, a3, b3 = lv[3]["t"], lv[3]["a"], lv[3]["b"]
    unpack_far(t3, far_t, side_t, 32, q3)
    args3 = refs(3)

    def coarse_sweep(src, dst, s):
        first = s + 2

        def body(n, _):
            for k in range(UNROLL[3]):
                sweep_row(src, dst, *args3, first + UNROLL[3] * n + k)
            return 0

        lax.fori_loop(0, (47 - 2 * s + UNROLL[3]) // UNROLL[3], body, 0)

    coarse_sweep(t3, a3, 2)

    def coarse_pair(n, _):
        coarse_sweep(a3, b3, 2 * n + 3)
        coarse_sweep(b3, a3, 2 * n + 4)
        return 0

    lax.fori_loop(0, (ITERS - 2) // 2, coarse_pair, 0)

    prolonged(2, a3, lv[2]["a"], 2)
    sweep(2, lv[2]["a"], lv[2]["b"], 3)
    sweep(2, lv[2]["b"], lv[2]["a"], 2)
    prolonged(1, lv[2]["a"], lv[1]["a"], 2)
    sweep(1, lv[1]["a"], lv[1]["b"], 2)
    sweep(1, lv[1]["b"], lv[1]["a"], 1)
    prolonged(0, lv[1]["a"], lv[0]["a"], 1)
    a0, b0 = lv[0]["a"], lv[0]["b"]
    sweep(0, a0, b0, 1)
    args0 = refs(0)
    stores = []
    for part in range(2):
        first = RIM[0] + 16 * part

        over_rows(first, 16, lambda i: sweep_row(b0, a0, *args0, i), UNROLL[0])
        for n in range(2):
            for k in range(16):
                kk = (k % 2) * 8 + k // 2
                store = pltpu.make_async_copy(
                    a0.at[pl.ds(first, 16), 16 * n + kk, pl.ds(0, 256)],
                    o_ref.at[n, k, pl.ds(16 * part, 16), :],
                    out_sem.at[32 * part + 16 * n + k],
                )
                store.start()
                stores.append(store)
    sent([one for one in every if one.pending])
    for store in stores:
        store.wait()


def solution(mesh):
    nx, ny = mesh.shape["gx"], mesh.shape["gy"]
    f32 = jnp.float32
    scratch = []
    for level in range(4):
        rows, lanes = TX[level], LN[level]
        planes = [24, 16, 64, 24, 32, 32, 32, 32]
        planes += [32] if level > 0 else []
        planes += [32] if level < 3 else []
        scratch += [pltpu.VMEM((rows, p, lanes), f32) for p in planes]
        if level < 3:
            scratch += [pltpu.VMEM((n, p, 128), f32) for p in (24, 32) for n in (2, 6)]
        if level == 0:
            scratch += [pltpu.VMEM((rows, 32, lanes), f32)]
    scratch += [pltpu.VMEM((16, 32, 256), f32)]
    scratch += [pltpu.VMEM((FAR, 24, 128), f32), pltpu.VMEM((FAR, 32, 128), f32)]
    scratch += [pltpu.VMEM((2, FAR, 24, 128), f32), pltpu.VMEM((2, FAR, 32, 128), f32)]
    scratch += [
        pltpu.VMEM((32, 256), f32),
        pltpu.VMEM((32, 256), jnp.int32),
        pltpu.VMEM((32, 256), jnp.int32),
    ]
    messages = 6 * 8 + 4 * REACH + 8 * (REACH - DIRECT) + 8
    scratch += [pltpu.SemaphoreType.DMA((51,)), pltpu.SemaphoreType.DMA((64,))]
    scratch += [pltpu.SemaphoreType.DMA((messages,)), pltpu.SemaphoreType.DMA((messages,))]

    def per_device(misfit, viscosity, friction, ice_mask, grounded):
        return pl.pallas_call(
            functools.partial(kernel, nx, ny),
            out_shape=jax.ShapeDtypeStruct(misfit.shape, f32),
            in_specs=[pl.BlockSpec(memory_space=HBM)] * 5,
            out_specs=pl.BlockSpec(memory_space=HBM),
            scratch_shapes=scratch,
            compiler_params=pltpu.CompilerParams(
                collective_id=0, has_side_effects=True, vmem_limit_bytes=62 * 2**20
            ),
        )(misfit, viscosity, friction, ice_mask, grounded)

    placed = (
        P(None, None, "gx", "gy"),
        P(None, "gx", "gy"),
        P("gx", "gy"),
        P("gx", "gy"),
        P("gx", "gy"),
    )
    return jax.shard_map(
        per_device, mesh=mesh, in_specs=placed, out_specs=P(None, None, "gx", "gy"), check_vma=False
    )
```

```python
import functools

import jax
import jax.numpy as jnp
from jax import lax
from jax.experimental import pallas as pl
from jax.experimental.pallas import tpu as pltpu
from jax.sharding import PartitionSpec as P

MESH = pl.DeviceIdType.MESH
HBM = pltpu.MemorySpace.HBM
OMEGA = 0.6
CROSS = 0.75
ITERS = 20

OX = (32, 16, 8, 4)
OY = (256, 128, 64, 32)
LN = (384, 256, 128, 128)
RIM = (4, 5, 6, 24)
PW = (4, 8, 16, 32)
TX = tuple(o + 2 * h for o, h in zip(OX[:3], RIM)) + (64,)
UNROLL = (4, 6, 8, 16)
UNROLL_C = (4, 4, 6, 10)
UNROLL_R = (2, 4, 4)
DIRECT = 6
REACH = 6
FAR = 2 * REACH + 1
SIDES = ((0, -1), (0, 1), (-1, -1), (-1, 1), (1, -1), (1, 1))


def over_rows(first, count, body, unroll):
    steps = count // unroll

    def step(n, _):
        for k in range(unroll):
            body(first + n * unroll + k)
        return 0

    if steps > 0:
        lax.fori_loop(0, steps, step, 0)
    for k in range(steps * unroll, count):
        body(first + k)


def lane_iota(rows):
    return lax.broadcasted_iota(jnp.int32, (rows, 128), 1)


def roll(x, shift, axis):
    return pltpu.roll(x, shift % x.shape[axis], axis)


def exact_dot(x, sel):
    hi = x.astype(jnp.bfloat16)
    rest = x - hi.astype(jnp.float32)
    mid = rest.astype(jnp.bfloat16)
    low = (rest - mid.astype(jnp.float32)).astype(jnp.bfloat16)
    rows = x.shape[0]
    out = jnp.dot(
        jnp.concatenate([hi, mid, low], 0), sel, preferred_element_type=jnp.float32
    )
    return (out[:rows] + out[rows : 2 * rows]) + out[2 * rows :]


def restrict_matrix(level):
    width = min(LN[level], OY[level]) if OY[level] >= 128 else 128
    fine = lax.broadcasted_iota(jnp.int32, (width, 128), 0)
    coarse = lax.broadcasted_iota(jnp.int32, (width, 128), 1)
    hit = (fine // 2 == coarse) & (fine < OY[level])
    return jnp.where(hit, 0.25, 0.0).astype(jnp.bfloat16)


def prolong_matrix(level):
    lc, lf = LN[level + 1], LN[level]
    coarse = lax.broadcasted_iota(jnp.int32, (lc, lf), 0)
    fine = lax.broadcasted_iota(jnp.int32, (lc, lf), 1)
    middle = (OY[level] + lf) // 2
    source = jnp.where(fine < middle, fine // 2, lc - (lf - fine + 1) // 2)
    return jnp.where(source == coarse, 1.0, 0.0).astype(jnp.bfloat16)


class Message:
    def __init__(self, place, sems, index, src, dst, dx, dy):
        gx, gy, nx, ny = place
        self.way = (dx, dy)
        self.to_there = (gx + dx >= 0) & (gx + dx < nx) & (gy + dy >= 0) & (gy + dy < ny)
        self.from_there = (gx - dx >= 0) & (gx - dx < nx) & (gy - dy >= 0) & (gy - dy < ny)
        target = (jnp.clip(gx + dx, 0, nx - 1), jnp.clip(gy + dy, 0, ny - 1))
        self.dst = dst
        self.pending = []
        self.copy = pltpu.make_async_remote_copy(
            src_ref=src,
            dst_ref=dst,
            send_sem=sems[0].at[index],
            recv_sem=sems[1].at[index],
            device_id=target,
            device_id_type=MESH,
        )


def by_way(messages):
    groups = {}
    for one in messages:
        groups.setdefault(one.way, []).append(one)
    return groups.values()


def clear(messages):
    for group in by_way(messages):

        @pl.when(jnp.logical_not(group[0].from_there))
        def _(group=group):
            for one in group:
                one.dst[...] = jnp.zeros(one.dst.shape, one.dst.dtype)


def start(messages):
    for group in by_way(messages):

        @pl.when(group[0].to_there)
        def _(group=group):
            for one in group:
                one.copy.start()

    for one in messages:
        one.pending = ["arrived", "sent"]


def arrived(messages):
    for group in by_way(messages):

        @pl.when(group[0].from_there)
        def _(group=group):
            for one in group:
                one.copy.wait_recv()

    for one in messages:
        one.pending.remove("arrived")


def sent(messages):
    for group in by_way(messages):

        @pl.when(group[0].to_there)
        def _(group=group):
            for one in group:
                one.copy.wait_send()

    for one in messages:
        one.pending.remove("sent")


def pack_columns(level, source, dest, planes):
    w, rim = PW[level], RIM[level]
    lane = lane_iota(planes)
    tile = (OY[level] - 1) // 128
    edge = (OY[level] - w) % 128
    zero = jnp.zeros((planes, 128), jnp.float32)
    left, right = zero, zero
    for i in range(OX[level]):
        here = (lane >= w * i) & (lane < w * i + w)
        a = source[rim + i, :, 0:128]
        b = source[rim + i, :, tile * 128 : tile * 128 + 128]
        left = jnp.where(here, roll(a, w * i, 1), left)
        right = jnp.where(here, roll(b, w * i - edge, 1), right)
    dest[0] = left
    dest[1] = right


def unpack_columns(level, dest, packs, planes, reach, side):
    w, rim, own = PW[level], RIM[level], OX[level]
    lane = lane_iota(planes)
    last = LN[level] - 128
    start = OY[level] % 128
    row0, count, shift, slot = {
        -1: (-reach, reach, own - reach, 2),
        0: (0, own, 0, 0),
        1: (own, reach, 0, 4),
    }[side]
    for i in range(count):
        at = w * (i + shift)
        right = roll(packs[slot + 1], start - at, 1)
        left = roll(packs[slot], -w - at, 1)
        row = rim + row0 + i
        if OY[level] < 128:
            rest = dest[row, :, last : last + 128]
        else:
            rest = jnp.zeros((planes, 128), jnp.float32)
        tile = jnp.where((lane >= start) & (lane < start + w), right, rest)
        dest[row, :, last : last + 128] = jnp.where(lane >= 128 - w, left, tile)


def coefficients(level, c, e, y4, z, q, r, g, low, high):
    scale = 0.25**level
    half, cross = 0.5 * scale, CROSS * scale
    lanes, rim = LN[level], RIM[level]
    first, count = rim + low, high - low
    sub = lax.broadcasted_iota(jnp.int32, (8, lanes), 0)
    e[first - 1] = half * (c[first - 1, 0:16, :] + c[first, 0:16, :])

    def body(i):
        here = c[i, 0:16, :]
        north, south = roll(here, -1, 1), roll(here, 1, 1)
        east = half * (here + c[i + 1, 0:16, :])
        west = half * (here + c[i - 1, 0:16, :])
        nf, sf = half * (here + north), half * (here + south)
        e[i] = east
        y4[i, 0:16, :] = nf
        y4[i, 16:32, :] = sf
        y4[i, 32:48, :] = cross * north
        y4[i, 48:64, :] = cross * south
        even, odd = here[0:8], here[8:16]
        inner = 2.0 * (even + odd)
        upper = jnp.where(sub < 7, 2.0 * (odd + roll(even, -1, 0)), 0.0)
        lower = roll(upper, 1, 0)
        z[i, 0:8, :] = inner
        z[i, 8:16, :] = upper
        z[i, 16:24, :] = lower
        ice = c[i, 16:17, :]
        drag = jnp.where(sub == 0, c[i, 17:18, :], 0.0)
        vertical = jnp.concatenate([inner + lower + drag, inner + upper], 0)
        xs, ys = east + west, nf + sf
        for k, lateral in enumerate((4.0 * xs + ys, xs + 4.0 * ys)):
            diag = ice * (lateral + vertical) + (1.0 - ice)
            inv = OMEGA / diag
            if q is not None:
                q[i, 16 * k : 16 * k + 16, :] = inv
            r[i, 16 * k : 16 * k + 16, :] = ice * inv
            if g is not None:
                g[i, 16 * k : 16 * k + 16, :] = diag * (1.0 / OMEGA)

    over_rows(first, count, body, UNROLL_C[level])


def off_diagonal(w, e, y4, z, i):
    u0, u, u2 = w[i - 1, 0:16, :], w[i, 0:16, :], w[i + 1, 0:16, :]
    v0, v, v2 = w[i - 1, 16:32, :], w[i, 16:32, :], w[i + 1, 16:32, :]
    west, east = e[i - 1], e[i]
    nf, sf, mn, ms = (y4[i, 16 * k : 16 * k + 16, :] for k in range(4))
    inner, upper, lower = (z[i, 8 * k : 8 * k + 8, :] for k in range(3))
    du, dv, v4 = u2 - u0, v2 - v0, 4.0 * v
    xu = 4.0 * (east * u2 + west * u0)
    xv = east * v2 + west * v0
    yu = roll(sf * u + ms * dv, -1, 1) + roll(nf * u - mn * dv, 1, 1)
    yv = roll(sf * v4 + ms * du, -1, 1) + roll(nf * v4 - mn * du, 1, 1)

    def column(f):
        even, odd = f[0:8], f[8:16]
        return jnp.concatenate(
            [inner * odd + lower * roll(odd, 1, 0), inner * even + upper * roll(even, -1, 0)], 0
        )

    return (u, v), (xu + yu + column(u), xv + yv + column(v))


def sweep_row(src, dst, e, y4, z, r, tt, i):
    fields, sums = off_diagonal(src, e, y4, z, i)
    for k in range(2):
        at = slice(16 * k, 16 * k + 16)
        dst[i, at, :] = (1.0 - OMEGA) * fields[k] + (tt[i, at, :] + r[i, at, :] * sums[k])


def remainder_row(src, e, y4, z, r, tt, g, i, lanes):
    fields, sums = off_diagonal(src, e, y4, z, i)
    parts = []
    for k in range(2):
        at = slice(16 * k, 16 * k + 16)
        change = tt[i, at, :] + r[i, at, :] * sums[k] - OMEGA * fields[k]
        parts.append(change[:, 0:lanes] * g[i, at, 0:lanes])
    return jnp.concatenate(parts, 0)


def kernel(nx, ny, m_ref, v_ref, f_ref, i_ref, b_ref, o_ref, *scratch):
    names = iter(scratch)
    lv = []
    for level in range(4):
        keys = ["c", "e", "y4", "z", "r", "t", "a", "b"]
        keys += ["q"] if level > 0 else []
        keys += ["g"] if level < 3 else []
        keys += ["spc", "rpc", "spt", "rpt"] if level < 3 else []
        keys += ["raw"] if level == 0 else []
        lv.append({key: next(names) for key in keys})
    rest, far_c, far_t, side_c, side_t, fr, ic, gr = (next(names) for _ in range(8))
    in_sem, out_sem, send_sem, recv_sem = (next(names) for _ in range(4))

    gx, gy = lax.axis_index("gx"), lax.axis_index("gy")
    place = (gx, gy, nx, ny)
    sems = (send_sem, recv_sem)
    count = iter(range(10**6))

    def message(src, dst, dx, dy):
        return Message(place, sems, next(count), src, dst, dx, dy)

    def rim_messages(level, array, packs, landed, reach):
        rim, own = RIM[level], OX[level]
        lanes = pl.ds(0, max(OY[level], 128))
        out = [
            message(
                array.at[pl.ds(rim, reach), :, lanes],
                array.at[pl.ds(rim + own, reach), :, lanes], -1, 0),
            message(
                array.at[pl.ds(rim + own - reach, reach), :, lanes],
                array.at[pl.ds(rim - reach, reach), :, lanes], 1, 0),
        ]
        for slot, (dx, dy) in enumerate(SIDES):
            out.append(message(packs.at[0 if dy > 0 else 1], landed.at[slot], -dx, -dy))
        return out

    def far_messages(far, side):
        out = []
        for d in [k * s for k in range(REACH, 0, -1) for s in (1, -1)]:
            out.append(message(far.at[REACH], far.at[REACH - d], d, 0))
            for n in range(2 if abs(d) > DIRECT else 0):
                out.append(message(far.at[REACH], side.at[n, REACH - d], d, 1 - 2 * n))
        return out

    def side_messages(far, side):
        near = pl.ds(REACH - DIRECT, 2 * DIRECT + 1)
        whole = [message(far.at[near], side.at[n, near], 0, 1 - 2 * n) for n in range(2)]
        first = next(count) - 2
        blocks = {
            b: [
                Message(place, sems, first + n, far.at[b], side.at[n, b], 0, 1 - 2 * n)
                for n in range(2)
            ]
            for b in range(REACH - DIRECT, REACH + DIRECT + 1)
        }
        return whole, blocks

    def pass_on(far, side):
        for d in range(1, DIRECT + 1):
            for s in (d, -d):
                arrived([one for one in far if one.way == (s, 0)])
                start(side[REACH - s])

    c0, t0, raw = lv[0]["c"], lv[0]["t"], lv[0]["raw"]
    msg_c = [rim_messages(n, lv[n]["c"], lv[n]["spc"], lv[n]["rpc"], RIM[n]) for n in range(3)]
    msg_t = [
        rim_messages(
            n, lv[n]["t"] if n > 0 else raw, lv[n]["spt"], lv[n]["rpt"], RIM[n] - 1
        )
        for n in range(3)
    ]
    msg_fc, msg_ft = far_messages(far_c, side_c), far_messages(far_t, side_t)
    all_sc, msg_sc = side_messages(far_c, side_c)
    all_st, msg_st = side_messages(far_t, side_t)
    every = sum(msg_c + msg_t, []) + msg_fc + msg_ft + all_sc + all_st

    barrier = pltpu.get_barrier_semaphore()
    far_away = [d for d in range(-REACH, REACH + 1) if abs(d) > DIRECT]
    partners = [(d, 0) for d in range(-REACH, REACH + 1) if d != 0] + list(SIDES)
    partners += [(d, s) for d in far_away for s in (-1, 1)]
    arrivals = 0
    for dx, dy in partners:
        there = (gx + dx >= 0) & (gx + dx < nx) & (gy + dy >= 0) & (gy + dy < ny)
        arrivals = arrivals + there.astype(jnp.int32)

        @pl.when(there)
        def _(dx=dx, dy=dy):
            pl.semaphore_signal(
                barrier,
                inc=1,
                device_id=(jnp.clip(gx + dx, 0, nx - 1), jnp.clip(gy + dy, 0, ny - 1)),
                device_id_type=MESH,
            )

    own0 = pl.ds(RIM[0], OX[0])
    loads = []
    for k in range(16):
        kk = (k % 2) * 8 + k // 2
        loads.append((v_ref.at[k], lv[0]["c"].at[own0, kk, pl.ds(0, 256)]))
        for n in range(2):
            loads.append((m_ref.at[n, k], raw.at[own0, 16 * n + kk, pl.ds(0, 256)]))
    loads += [(f_ref, fr), (i_ref, ic), (b_ref, gr)]
    loads = [pltpu.make_async_copy(s, d, in_sem.at[n]) for n, (s, d) in enumerate(loads)]
    for load in loads:
        load.start()

    clear(every)
    for load in loads:
        load.wait()

    ic_f = ic[...].astype(jnp.float32)
    ic_f = ic_f.reshape(OX[0], 1, 256)
    dr_f = (fr[...] * gr[...].astype(jnp.float32)).reshape(OX[0], 1, 256)
    sub = lax.broadcasted_iota(jnp.int32, (OX[0], 8, 256), 1)
    c0[own0, 16:24, 0:256] = jnp.where(sub == 0, ic_f, jnp.where(sub == 1, dr_f, 0.0))

    pack_columns(0, c0, lv[0]["spc"], 24)
    pack_columns(0, raw, lv[0]["spt"], 32)

    pl.semaphore_wait(barrier, arrivals)
    start(msg_c[0][2:4] + msg_t[0][2:4])
    start(msg_c[0][:2] + msg_t[0][:2] + msg_c[0][4:] + msg_t[0][4:])

    for level in range(3):
        rim, own, width = RIM[level], OX[level + 1], max(OY[level], 128)
        fine = lv[level]["c"]
        block = fine[rim : rim + 2 * own, :, 0:width].reshape(own, 2, 24, width)
        block = (block[:, 0] + block[:, 1]).reshape(own * 24, width)
        coarse = exact_dot(block, restrict_matrix(level)).reshape(own, 24, 128)
        if level < 2:
            target = lv[level + 1]["c"]
            target[RIM[level + 1] : RIM[level + 1] + own, :, 0:128] = coarse
            pack_columns(level + 1, target, lv[level + 1]["spc"], 24)
        else:
            far_c[REACH] = sum(roll(coarse[k], 32 * k, 1) for k in range(4))

    def refs(level):
        return [lv[level][key] for key in ("e", "y4", "z", "r", "t")]

    def gather(level, kind, messages, planes, reach, sides):
        landed = lv[level]["rp" + kind]
        array = raw if (level, kind) == (0, "t") else lv[level][kind]
        for side in sides:
            which = {0: messages[2:4], -1: messages[1:2] + messages[4:6], 1: messages[0:1] + messages[6:8]}
            arrived(which[side])
        if OY[level] < 128 and 0 in sides:
            sent(messages[:2])
        for side in sides:
            unpack_columns(level, array, landed, planes, reach, side)

    def first_sweep(level, low, high):
        t = lv[level]["t"]
        source, factor = (raw, lv[0]["r"]) if level == 0 else (t, lv[level]["q"])

        def body(i):
            t[i] = source[i] * factor[i]

        over_rows(RIM[level] + low, high - low, body, min(4, high - low))

    def sweep_range(level, src, dst, low, high):
        args = refs(level)

        over_rows(
            RIM[level] + low,
            high - low,
            lambda i: sweep_row(src, dst, *args, i),
            UNROLL[level],
        )

    def sweep(level, src, dst, rows):
        sweep_range(level, src, dst, -rows, OX[level] + rows)

    def remainder_rows(level, src, low, high):
        args = refs(level)
        width = max(OY[level], 128)

        def body(n):
            i = RIM[level] + 2 * n
            pair = [remainder_row(src, *args, lv[level]["g"], i + k, width) for k in range(2)]
            rest[n, :, 0:width] = pair[0] + pair[1]

        over_rows(low, high - low, body, min(UNROLL_R[level], high - low))

    def restricted(level):
        width, own = max(OY[level], 128), OX[level + 1]
        block = rest[0:own, :, 0:width].reshape(own * 32, width)
        return exact_dot(block, restrict_matrix(level)).reshape(own, 32, 128)

    def prolonged(level, src, dst, rows):
        low, high = RIM[level + 1] - rows, RIM[level + 1] + OX[level + 1] + rows
        n = high - low
        sel = prolong_matrix(level)
        spread = lv[level]["g"]
        block = src[low:high].reshape(n * 32, LN[level + 1])
        spread[0:n] = exact_dot(block, sel).reshape(n, 32, LN[level])

        def body(k):
            i = RIM[level] + 2 * (k - rows)
            extra = spread[k]
            dst[i] = dst[i] + extra
            dst[i + 1] = dst[i + 1] + extra

        over_rows(0, n, body, 2)

    def all_coefficients(level, low, high):
        refs_c = [lv[level].get(k) for k in ("c", "e", "y4", "z", "q", "r", "g")]
        coefficients(level, *refs_c, low, high)

    n0, h0 = OX[0], RIM[0] - 1
    gather(0, "c", msg_c[0], 24, RIM[0], (0,))
    gather(0, "t", msg_t[0], 32, h0, (0,))
    all_coefficients(0, 1, n0 - 1)
    start(msg_c[1] + msg_c[2])
    first_sweep(0, 1, n0 - 1)
    sweep_range(0, t0, lv[0]["a"], 2, n0 - 2)
    remainder_rows(0, lv[0]["a"], 2, OX[1] - 2)
    gather(0, "c", msg_c[0], 24, RIM[0], (-1, 1))
    gather(0, "t", msg_t[0], 32, h0, (-1, 1))
    for low, high in ((-h0, 1), (n0 - 1, n0 + h0)):
        all_coefficients(0, low, high)
        first_sweep(0, low, high)
    for low, high in ((1 - h0, 2), (n0 - 2, n0 + h0 - 1)):
        sweep_range(0, t0, lv[0]["a"], low, high)
    for low, high in ((0, 2), (OX[1] - 2, OX[1])):
        remainder_rows(0, lv[0]["a"], low, high)

    for level in (1, 2):
        t, own, h = lv[level]["t"], OX[level], RIM[level] - 1
        if level == 2:
            remainder_rows(1, lv[1]["a"], 0, own)
        t[RIM[level] : RIM[level] + own, :, 0:128] = restricted(level - 1)
        start(msg_t[level][:2])
        pack_columns(level, t, lv[level]["spt"], 32)
        start(msg_t[level][4:] + msg_t[level][2:4])
        if level == 2:
            pass_on(msg_fc, msg_sc)
        gather(level, "c", msg_c[level], 24, RIM[level], (0, -1, 1))
        all_coefficients(level, -h, own + h)
        gather(level, "t", msg_t[level], 32, h, (0,))
        if OY[level] >= 128:
            sent(msg_t[level][:2])
            start(msg_fc + msg_sc[REACH])
        first_sweep(level, 0, own)
        sweep_range(level, t, lv[level]["a"], 1, own - 1)
        gather(level, "t", msg_t[level], 32, h, (-1, 1))
        first_sweep(level, -h, 0)
        first_sweep(level, own, own + h)
        sweep_range(level, t, lv[level]["a"], 1 - h, 1)
        sweep_range(level, t, lv[level]["a"], own - 1, own + h - 1)

    remainder_rows(2, lv[2]["a"], 0, OX[3])
    t_next = restricted(2)
    far_t[REACH] = sum(roll(t_next[k], 32 * k, 1) for k in range(4))
    start(msg_ft + msg_st[REACH])

    def unpack_far(dest, far, side, planes, factor):
        lane = lane_iota(planes)

        def body(b):
            own, left, right = far[b], side[0, b], side[1, b]
            for k in range(4):
                tile = jnp.where(lane < 32, roll(own, -32 * k, 1), 0.0)
                tile = jnp.where((lane >= 32) & (lane < 64), roll(right, 32 - 32 * k, 1), tile)
                tile = jnp.where(lane >= 96, roll(left, 96 - 32 * k, 1), tile)
                dest[4 * b + k] = tile if factor is None else tile * factor[4 * b + k]

        over_rows(0, FAR, body, 2)

    for one in all_sc + all_st:
        one.pending = ["arrived", "sent"]
    arrived(all_sc + [one for one in msg_fc if "arrived" in one.pending])
    q3 = lv[3]["q"]
    unpack_far(lv[3]["c"], far_c, side_c, 24, None)
    all_coefficients(3, 1 - RIM[3], OX[3] + RIM[3] - 1)
    q3[0] = q3[1]
    q3[OX[3] + 2 * RIM[3] - 1] = q3[1]
    pass_on(msg_ft, msg_st)
    sent([one for one in every if one.pending == ["sent"]])
    arrived([one for one in msg_ft if "arrived" in one.pending] + all_st)
    t3, a3, b3 = lv[3]["t"], lv[3]["a"], lv[3]["b"]
    unpack_far(t3, far_t, side_t, 32, q3)
    args3 = refs(3)

    def coarse_sweep(src, dst, s):
        first = s + 2

        def body(n, _):
            for k in range(UNROLL[3]):
                sweep_row(src, dst, *args3, first + UNROLL[3] * n + k)
            return 0

        lax.fori_loop(0, (47 - 2 * s + UNROLL[3]) // UNROLL[3], body, 0)

    coarse_sweep(t3, a3, 2)

    def coarse_pair(n, _):
        coarse_sweep(a3, b3, 2 * n + 3)
        coarse_sweep(b3, a3, 2 * n + 4)
        return 0

    lax.fori_loop(0, (ITERS - 2) // 2, coarse_pair, 0)

    prolonged(2, a3, lv[2]["a"], 2)
    sweep(2, lv[2]["a"], lv[2]["b"], 3)
    sweep(2, lv[2]["b"], lv[2]["a"], 2)
    prolonged(1, lv[2]["a"], lv[1]["a"], 2)
    sweep(1, lv[1]["a"], lv[1]["b"], 2)
    sweep(1, lv[1]["b"], lv[1]["a"], 1)
    prolonged(0, lv[1]["a"], lv[0]["a"], 1)
    a0, b0 = lv[0]["a"], lv[0]["b"]
    sweep(0, a0, b0, 1)
    args0 = refs(0)
    stores = []
    for part in range(2):
        first = RIM[0] + 16 * part

        over_rows(first, 16, lambda i: sweep_row(b0, a0, *args0, i), UNROLL[0])
        for n in range(2):
            for k in range(16):
                kk = (k % 2) * 8 + k // 2
                store = pltpu.make_async_copy(
                    a0.at[pl.ds(first, 16), 16 * n + kk, pl.ds(0, 256)],
                    o_ref.at[n, k, pl.ds(16 * part, 16), :],
                    out_sem.at[32 * part + 16 * n + k],
                )
                store.start()
                stores.append(store)
    sent([one for one in every if one.pending])
    for store in stores:
        store.wait()


def solution(mesh):
    nx, ny = mesh.shape["gx"], mesh.shape["gy"]
    f32 = jnp.float32
    scratch = []
    for level in range(4):
        rows, lanes = TX[level], LN[level]
        planes = [24, 16, 64, 24, 32, 32, 32, 32]
        planes += [32] if level > 0 else []
        planes += [32] if level < 3 else []
        scratch += [pltpu.VMEM((rows, p, lanes), f32) for p in planes]
        if level < 3:
            scratch += [pltpu.VMEM((n, p, 128), f32) for p in (24, 32) for n in (2, 6)]
        if level == 0:
            scratch += [pltpu.VMEM((rows, 32, lanes), f32)]
    scratch += [pltpu.VMEM((16, 32, 256), f32)]
    scratch += [pltpu.VMEM((FAR, 24, 128), f32), pltpu.VMEM((FAR, 32, 128), f32)]
    scratch += [pltpu.VMEM((2, FAR, 24, 128), f32), pltpu.VMEM((2, FAR, 32, 128), f32)]
    scratch += [
        pltpu.VMEM((32, 256), f32),
        pltpu.VMEM((32, 256), jnp.int32),
        pltpu.VMEM((32, 256), jnp.int32),
    ]
    messages = 6 * 8 + 4 * REACH + 8 * (REACH - DIRECT) + 8
    scratch += [pltpu.SemaphoreType.DMA((51,)), pltpu.SemaphoreType.DMA((64,))]
    scratch += [pltpu.SemaphoreType.DMA((messages,)), pltpu.SemaphoreType.DMA((messages,))]

    def per_device(misfit, viscosity, friction, ice_mask, grounded):
        return pl.pallas_call(
            functools.partial(kernel, nx, ny),
            out_shape=jax.ShapeDtypeStruct(misfit.shape, f32),
            in_specs=[pl.BlockSpec(memory_space=HBM)] * 5,
            out_specs=pl.BlockSpec(memory_space=HBM),
            scratch_shapes=scratch,
            compiler_params=pltpu.CompilerParams(
                collective_id=0, has_side_effects=True, vmem_limit_bytes=62 * 2**20
            ),
        )(misfit, viscosity, friction, ice_mask, grounded)

    placed = (
        P(None, None, "gx", "gy"),
        P(None, "gx", "gy"),
        P("gx", "gy"),
        P("gx", "gy"),
        P("gx", "gy"),
    )
    return jax.shard_map(
        per_device, mesh=mesh, in_specs=placed, out_specs=P(None, None, "gx", "gy"), check_vma=False
    )
```

```python
import functools

import jax
import jax.numpy as jnp
from jax import lax
from jax.experimental import pallas as pl
from jax.experimental.pallas import tpu as pltpu
from jax.sharding import PartitionSpec as P

MESH = pl.DeviceIdType.MESH
HBM = pltpu.MemorySpace.HBM
OMEGA = 0.6
CROSS = 0.75
ITERS = 20

OX = (32, 16, 8, 4)
OY = (256, 128, 64, 32)
LN = (384, 256, 128, 128)
RIM = (4, 5, 6, 24)
PW = (4, 8, 16, 32)
TX = tuple(o + 2 * h for o, h in zip(OX[:3], RIM)) + (64,)
UNROLL = (4, 6, 8, 16)
UNROLL_C = (4, 4, 6, 10)
UNROLL_R = (2, 4, 4)
DIRECT = 6
REACH = 6
FAR = 2 * REACH + 1
SIDES = ((0, -1), (0, 1), (-1, -1), (-1, 1), (1, -1), (1, 1))


def over_rows(first, count, body, unroll):
    steps = count // unroll

    def step(n, _):
        for k in range(unroll):
            body(first + n * unroll + k)
        return 0

    if steps > 0:
        lax.fori_loop(0, steps, step, 0)
    for k in range(steps * unroll, count):
        body(first + k)


def lane_iota(rows):
    return lax.broadcasted_iota(jnp.int32, (rows, 128), 1)


def roll(x, shift, axis):
    return pltpu.roll(x, shift % x.shape[axis], axis)


def exact_dot(x, sel):
    hi = x.astype(jnp.bfloat16)
    rest = x - hi.astype(jnp.float32)
    mid = rest.astype(jnp.bfloat16)
    low = (rest - mid.astype(jnp.float32)).astype(jnp.bfloat16)
    rows = x.shape[0]
    out = jnp.dot(
        jnp.concatenate([hi, mid, low], 0), sel, preferred_element_type=jnp.float32
    )
    return (out[:rows] + out[rows : 2 * rows]) + out[2 * rows :]


def restrict_matrix(level):
    width = min(LN[level], OY[level]) if OY[level] >= 128 else 128
    fine = lax.broadcasted_iota(jnp.int32, (width, 128), 0)
    coarse = lax.broadcasted_iota(jnp.int32, (width, 128), 1)
    hit = (fine // 2 == coarse) & (fine < OY[level])
    return jnp.where(hit, 0.25, 0.0).astype(jnp.bfloat16)


def prolong_matrix(level):
    lc, lf = LN[level + 1], LN[level]
    coarse = lax.broadcasted_iota(jnp.int32, (lc, lf), 0)
    fine = lax.broadcasted_iota(jnp.int32, (lc, lf), 1)
    middle = (OY[level] + lf) // 2
    source = jnp.where(fine < middle, fine // 2, lc - (lf - fine + 1) // 2)
    return jnp.where(source == coarse, 1.0, 0.0).astype(jnp.bfloat16)


class Message:
    def __init__(self, place, sems, index, src, dst, dx, dy):
        gx, gy, nx, ny = place
        self.way = (dx, dy)
        self.to_there = (gx + dx >= 0) & (gx + dx < nx) & (gy + dy >= 0) & (gy + dy < ny)
        self.from_there = (gx - dx >= 0) & (gx - dx < nx) & (gy - dy >= 0) & (gy - dy < ny)
        target = (jnp.clip(gx + dx, 0, nx - 1), jnp.clip(gy + dy, 0, ny - 1))
        self.dst = dst
        self.pending = []
        self.copy = pltpu.make_async_remote_copy(
            src_ref=src,
            dst_ref=dst,
            send_sem=sems[0].at[index],
            recv_sem=sems[1].at[index],
            device_id=target,
            device_id_type=MESH,
        )


def by_way(messages):
    groups = {}
    for one in messages:
        groups.setdefault(one.way, []).append(one)
    return groups.values()


def clear(messages):
    for group in by_way(messages):

        @pl.when(jnp.logical_not(group[0].from_there))
        def _(group=group):
            for one in group:
                one.dst[...] = jnp.zeros(one.dst.shape, one.dst.dtype)


def start(messages):
    for group in by_way(messages):

        @pl.when(group[0].to_there)
        def _(group=group):
            for one in group:
                one.copy.start()

    for one in messages:
        one.pending = ["arrived", "sent"]


def arrived(messages):
    for group in by_way(messages):

        @pl.when(group[0].from_there)
        def _(group=group):
            for one in group:
                one.copy.wait_recv()

    for one in messages:
        one.pending.remove("arrived")


def sent(messages):
    for group in by_way(messages):

        @pl.when(group[0].to_there)
        def _(group=group):
            for one in group:
                one.copy.wait_send()

    for one in messages:
        one.pending.remove("sent")


def pack_columns(level, source, dest, planes):
    w, rim = PW[level], RIM[level]
    lane = lane_iota(planes)
    tile = (OY[level] - 1) // 128
    edge = (OY[level] - w) % 128
    zero = jnp.zeros((planes, 128), jnp.float32)
    left, right = zero, zero
    for i in range(OX[level]):
        here = (lane >= w * i) & (lane < w * i + w)
        a = source[rim + i, :, 0:128]
        b = source[rim + i, :, tile * 128 : tile * 128 + 128]
        left = jnp.where(here, roll(a, w * i, 1), left)
        right = jnp.where(here, roll(b, w * i - edge, 1), right)
    dest[0] = left
    dest[1] = right


def unpack_columns(level, dest, packs, planes, reach, side, skip=0):
    w, rim, own = PW[level], RIM[level], OX[level]
    lane = lane_iota(planes)
    last = LN[level] - 128
    start = OY[level] % 128
    row0, count, shift, slot = {
        -1: (-reach, reach - skip, own - reach, 2),
        0: (0, own, 0, 0),
        1: (own + skip, reach - skip, skip, 4),
    }[side]
    for i in range(count):
        at = w * (i + shift)
        right = roll(packs[slot + 1], start - at, 1)
        left = roll(packs[slot], -w - at, 1)
        row = rim + row0 + i
        if OY[level] < 128:
            rest = dest[row, :, last : last + 128]
        else:
            rest = jnp.zeros((planes, 128), jnp.float32)
        tile = jnp.where((lane >= start) & (lane < start + w), right, rest)
        dest[row, :, last : last + 128] = jnp.where(lane >= 128 - w, left, tile)


def coefficients(level, c, e, y4, z, q, r, g, low, high):
    scale = 0.25**level
    half, cross = 0.5 * scale, CROSS * scale
    lanes, rim = LN[level], RIM[level]
    first, count = rim + low, high - low
    sub = lax.broadcasted_iota(jnp.int32, (8, lanes), 0)
    e[first - 1] = half * (c[first - 1, 0:16, :] + c[first, 0:16, :])

    def body(i):
        here = c[i, 0:16, :]
        north, south = roll(here, -1, 1), roll(here, 1, 1)
        east = half * (here + c[i + 1, 0:16, :])
        west = half * (here + c[i - 1, 0:16, :])
        nf, sf = half * (here + north), half * (here + south)
        e[i] = east
        y4[i, 0:16, :] = nf
        y4[i, 16:32, :] = sf
        y4[i, 32:48, :] = cross * north
        y4[i, 48:64, :] = cross * south
        even, odd = here[0:8], here[8:16]
        inner = 2.0 * (even + odd)
        upper = jnp.where(sub < 7, 2.0 * (odd + roll(even, -1, 0)), 0.0)
        lower = roll(upper, 1, 0)
        z[i, 0:8, :] = inner
        z[i, 8:16, :] = upper
        z[i, 16:24, :] = lower
        ice = c[i, 16:17, :]
        drag = jnp.where(sub == 0, c[i, 17:18, :], 0.0)
        vertical = jnp.concatenate([inner + lower + drag, inner + upper], 0)
        xs, ys = east + west, nf + sf
        for k, lateral in enumerate((4.0 * xs + ys, xs + 4.0 * ys)):
            diag = ice * (lateral + vertical) + (1.0 - ice)
            inv = OMEGA / diag
            if q is not None:
                q[i, 16 * k : 16 * k + 16, :] = inv
            r[i, 16 * k : 16 * k + 16, :] = ice * inv
            if g is not None:
                g[i, 16 * k : 16 * k + 16, :] = diag * (1.0 / OMEGA)

    over_rows(first, count, body, UNROLL_C[level])


def off_diagonal(w, e, y4, z, i):
    u0, u, u2 = w[i - 1, 0:16, :], w[i, 0:16, :], w[i + 1, 0:16, :]
    v0, v, v2 = w[i - 1, 16:32, :], w[i, 16:32, :], w[i + 1, 16:32, :]
    west, east = e[i - 1], e[i]
    nf, sf, mn, ms = (y4[i, 16 * k : 16 * k + 16, :] for k in range(4))
    inner, upper, lower = (z[i, 8 * k : 8 * k + 8, :] for k in range(3))
    du, dv, v4 = u2 - u0, v2 - v0, 4.0 * v
    xu = 4.0 * (east * u2 + west * u0)
    xv = east * v2 + west * v0
    yu = roll(sf * u + ms * dv, -1, 1) + roll(nf * u - mn * dv, 1, 1)
    yv = roll(sf * v4 + ms * du, -1, 1) + roll(nf * v4 - mn * du, 1, 1)

    def column(f):
        even, odd = f[0:8], f[8:16]
        return jnp.concatenate(
            [inner * odd + lower * roll(odd, 1, 0), inner * even + upper * roll(even, -1, 0)], 0
        )

    return (u, v), (xu + yu + column(u), xv + yv + column(v))


def sweep_row(src, dst, e, y4, z, r, tt, i):
    fields, sums = off_diagonal(src, e, y4, z, i)
    for k in range(2):
        at = slice(16 * k, 16 * k + 16)
        dst[i, at, :] = (1.0 - OMEGA) * fields[k] + (tt[i, at, :] + r[i, at, :] * sums[k])


def remainder_row(src, e, y4, z, r, tt, g, i, lanes):
    fields, sums = off_diagonal(src, e, y4, z, i)
    parts = []
    for k in range(2):
        at = slice(16 * k, 16 * k + 16)
        change = tt[i, at, :] + r[i, at, :] * sums[k] - OMEGA * fields[k]
        parts.append(change[:, 0:lanes] * g[i, at, 0:lanes])
    return jnp.concatenate(parts, 0)


def kernel(nx, ny, m_ref, v_ref, f_ref, i_ref, b_ref, o_ref, *scratch):
    names = iter(scratch)
    lv = []
    for level in range(4):
        keys = ["c", "e", "y4", "z", "r", "t", "a", "b"]
        keys += ["q"] if level > 0 else []
        keys += ["g"] if level < 3 else []
        keys += ["spc", "rpc", "spt", "rpt"] if level < 3 else []
        keys += ["raw"] if level == 0 else []
        lv.append({key: next(names) for key in keys})
    rest, far_c, far_t, side_c, side_t, fr, ic, gr = (next(names) for _ in range(8))
    in_sem, out_sem, send_sem, recv_sem = (next(names) for _ in range(4))

    gx, gy = lax.axis_index("gx"), lax.axis_index("gy")
    place = (gx, gy, nx, ny)
    sems = (send_sem, recv_sem)
    count = iter(range(10**6))

    def message(src, dst, dx, dy):
        return Message(place, sems, next(count), src, dst, dx, dy)

    def rim_messages(level, array, packs, landed, reach):
        rim, own = RIM[level], OX[level]
        lanes = pl.ds(0, max(OY[level], 128))
        out = [
            message(
                array.at[pl.ds(rim, reach), :, lanes],
                array.at[pl.ds(rim + own, reach), :, lanes], -1, 0),
            message(
                array.at[pl.ds(rim + own - reach, reach), :, lanes],
                array.at[pl.ds(rim - reach, reach), :, lanes], 1, 0),
        ]
        for slot, (dx, dy) in enumerate(SIDES):
            out.append(message(packs.at[0 if dy > 0 else 1], landed.at[slot], -dx, -dy))
        return out

    def far_messages(far, side):
        out = []
        for d in [k * s for k in range(REACH, 0, -1) for s in (1, -1)]:
            out.append(message(far.at[REACH], far.at[REACH - d], d, 0))
            for n in range(2 if abs(d) > DIRECT else 0):
                out.append(message(far.at[REACH], side.at[n, REACH - d], d, 1 - 2 * n))
        return out

    def side_messages(far, side):
        near = pl.ds(REACH - DIRECT, 2 * DIRECT + 1)
        whole = [message(far.at[near], side.at[n, near], 0, 1 - 2 * n) for n in range(2)]
        first = next(count) - 2
        blocks = {
            b: [
                Message(place, sems, first + n, far.at[b], side.at[n, b], 0, 1 - 2 * n)
                for n in range(2)
            ]
            for b in range(REACH - DIRECT, REACH + DIRECT + 1)
        }
        return whole, blocks

    def pass_on(far, side):
        for d in range(1, DIRECT + 1):
            for s in (d, -d):
                arrived([one for one in far if one.way == (s, 0)])
                start(side[REACH - s])

    c0, t0, raw = lv[0]["c"], lv[0]["t"], lv[0]["raw"]
    msg_c = [rim_messages(n, lv[n]["c"], lv[n]["spc"], lv[n]["rpc"], RIM[n] - (n == 0)) for n in range(3)]
    msg_t = [
        rim_messages(
            n, lv[n]["t"] if n > 0 else raw, lv[n]["spt"], lv[n]["rpt"], RIM[n] - 1 - (n == 0)
        )
        for n in range(3)
    ]
    late = []
    for array, reach in ((c0, RIM[0] - 1), (raw, RIM[0] - 2)):
        rim, own, lanes = RIM[0], OX[0], pl.ds(0, 256)
        for dx, source, target in (
            (-1, rim + reach, rim + own + reach),
            (1, rim + own - reach - 1, rim - reach - 1),
        ):
            src, dst = (array.at[pl.ds(row, 1), :, lanes] for row in (source, target))
            late.append(message(src, dst, dx, 0))
    msg_fc, msg_ft = far_messages(far_c, side_c), far_messages(far_t, side_t)
    all_sc, msg_sc = side_messages(far_c, side_c)
    all_st, msg_st = side_messages(far_t, side_t)
    every = sum(msg_c + msg_t, late) + msg_fc + msg_ft + all_sc + all_st

    barrier = pltpu.get_barrier_semaphore()
    far_away = [d for d in range(-REACH, REACH + 1) if abs(d) > DIRECT]
    partners = [(d, 0) for d in range(-REACH, REACH + 1) if d != 0] + list(SIDES)
    partners += [(d, s) for d in far_away for s in (-1, 1)]
    arrivals = 0
    for dx, dy in partners:
        there = (gx + dx >= 0) & (gx + dx < nx) & (gy + dy >= 0) & (gy + dy < ny)
        arrivals = arrivals + there.astype(jnp.int32)

        @pl.when(there)
        def _(dx=dx, dy=dy):
            pl.semaphore_signal(
                barrier,
                inc=1,
                device_id=(jnp.clip(gx + dx, 0, nx - 1), jnp.clip(gy + dy, 0, ny - 1)),
                device_id_type=MESH,
            )

    own0 = pl.ds(RIM[0], OX[0])
    loads = []
    for k in range(16):
        kk = (k % 2) * 8 + k // 2
        loads.append((v_ref.at[k], lv[0]["c"].at[own0, kk, pl.ds(0, 256)]))
        for n in range(2):
            loads.append((m_ref.at[n, k], raw.at[own0, 16 * n + kk, pl.ds(0, 256)]))
    loads += [(f_ref, fr), (i_ref, ic), (b_ref, gr)]
    loads = [pltpu.make_async_copy(s, d, in_sem.at[n]) for n, (s, d) in enumerate(loads)]
    for load in loads:
        load.start()

    clear(every)
    for load in loads:
        load.wait()

    ic_f = ic[...].astype(jnp.float32)
    ic_f = ic_f.reshape(OX[0], 1, 256)
    dr_f = (fr[...] * gr[...].astype(jnp.float32)).reshape(OX[0], 1, 256)
    sub = lax.broadcasted_iota(jnp.int32, (OX[0], 8, 256), 1)
    c0[own0, 16:24, 0:256] = jnp.where(sub == 0, ic_f, jnp.where(sub == 1, dr_f, 0.0))

    pack_columns(0, c0, lv[0]["spc"], 24)
    pack_columns(0, raw, lv[0]["spt"], 32)

    pl.semaphore_wait(barrier, arrivals)
    start(msg_c[0][2:4] + msg_t[0][2:4])
    start(msg_c[0][:2] + msg_t[0][:2] + msg_c[0][4:] + msg_t[0][4:])

    for level in range(3):
        rim, own, width = RIM[level], OX[level + 1], max(OY[level], 128)
        fine = lv[level]["c"]
        block = fine[rim : rim + 2 * own, :, 0:width].reshape(own, 2, 24, width)
        block = (block[:, 0] + block[:, 1]).reshape(own * 24, width)
        coarse = exact_dot(block, restrict_matrix(level)).reshape(own, 24, 128)
        if level < 2:
            target = lv[level + 1]["c"]
            target[RIM[level + 1] : RIM[level + 1] + own, :, 0:128] = coarse
            pack_columns(level + 1, target, lv[level + 1]["spc"], 24)
        else:
            far_c[REACH] = sum(roll(coarse[k], 32 * k, 1) for k in range(4))

    def refs(level):
        return [lv[level][key] for key in ("e", "y4", "z", "r", "t")]

    def gather(level, kind, messages, planes, reach, sides):
        landed = lv[level]["rp" + kind]
        array = raw if (level, kind) == (0, "t") else lv[level][kind]
        for side in sides:
            which = {0: messages[2:4], -1: messages[1:2] + messages[4:6], 1: messages[0:1] + messages[6:8]}
            arrived(which[side])
        if OY[level] < 128 and 0 in sides:
            sent(messages[:2])
        for side in sides:
            unpack_columns(level, array, landed, planes, reach, side)

    def first_sweep(level, low, high):
        t = lv[level]["t"]
        source, factor = (raw, lv[0]["r"]) if level == 0 else (t, lv[level]["q"])

        def body(i):
            t[i] = source[i] * factor[i]

        over_rows(RIM[level] + low, high - low, body, min(4, high - low))

    def sweep_range(level, src, dst, low, high):
        args = refs(level)

        over_rows(
            RIM[level] + low,
            high - low,
            lambda i: sweep_row(src, dst, *args, i),
            UNROLL[level],
        )

    def sweep(level, src, dst, rows):
        sweep_range(level, src, dst, -rows, OX[level] + rows)

    def remainder_rows(level, src, low, high):
        args = refs(level)
        width = max(OY[level], 128)

        def body(n):
            i = RIM[level] + 2 * n
            pair = [remainder_row(src, *args, lv[level]["g"], i + k, width) for k in range(2)]
            rest[n, :, 0:width] = pair[0] + pair[1]

        over_rows(low, high - low, body, min(UNROLL_R[level], high - low))

    def restricted(level):
        width, own = max(OY[level], 128), OX[level + 1]
        block = rest[0:own, :, 0:width].reshape(own * 32, width)
        return exact_dot(block, restrict_matrix(level)).reshape(own, 32, 128)

    def prolonged(level, src, dst, rows):
        low, high = RIM[level + 1] - rows, RIM[level + 1] + OX[level + 1] + rows
        n = high - low
        sel = prolong_matrix(level)
        spread = lv[level]["g"]
        block = src[low:high].reshape(n * 32, LN[level + 1])
        spread[0:n] = exact_dot(block, sel).reshape(n, 32, LN[level])

        def body(k):
            i = RIM[level] + 2 * (k - rows)
            extra = spread[k]
            dst[i] = dst[i] + extra
            dst[i + 1] = dst[i + 1] + extra

        over_rows(0, n, body, 6)

    def all_coefficients(level, low, high):
        refs_c = [lv[level].get(k) for k in ("c", "e", "y4", "z", "q", "r", "g")]
        coefficients(level, *refs_c, low, high)

    n0, h0 = OX[0], RIM[0] - 2
    gather(0, "c", msg_c[0], 24, h0 + 1, (0,))
    gather(0, "t", msg_t[0], 32, h0, (0,))
    all_coefficients(0, 1, n0 - 1)
    start(msg_c[1] + late + msg_c[2])
    first_sweep(0, 1, n0 - 1)
    sweep_range(0, t0, lv[0]["a"], 2, n0 - 2)
    remainder_rows(0, lv[0]["a"], 2, OX[1] - 2)
    gather(0, "c", msg_c[0], 24, h0 + 1, (-1, 1))
    gather(0, "t", msg_t[0], 32, h0, (-1, 1))
    for low, high in ((-h0, 1), (n0 - 1, n0 + h0)):
        all_coefficients(0, low, high)
        first_sweep(0, low, high)
    for low, high in ((1 - h0, 2), (n0 - 2, n0 + h0 - 1)):
        sweep_range(0, t0, lv[0]["a"], low, high)
    for low, high in ((0, 2), (OX[1] - 2, OX[1])):
        remainder_rows(0, lv[0]["a"], low, high)

    for level in (1, 2):
        t, own, h = lv[level]["t"], OX[level], RIM[level] - 1
        if level == 2:
            remainder_rows(1, lv[1]["a"], 0, own)
        t[RIM[level] : RIM[level] + own, :, 0:128] = restricted(level - 1)
        start(msg_t[level][:2])
        pack_columns(level, t, lv[level]["spt"], 32)
        start(msg_t[level][4:] + msg_t[level][2:4])
        if level == 2:
            pass_on(msg_fc, msg_sc)
        if level == 1:
            arrived(late)
            for side in (-1, 1):
                unpack_columns(0, c0, lv[0]["rpc"], 24, h0 + 2, side, h0 + 1)
                unpack_columns(0, raw, lv[0]["rpt"], 32, h0 + 1, side, h0)
            for row, inward in ((-h0 - 1, -h0), (n0 + h0, n0 + h0 - 1)):
                all_coefficients(0, row, row + 1)
                first_sweep(0, row, row + 1)
                sweep_range(0, t0, lv[0]["a"], inward, inward + 1)
        gather(level, "c", msg_c[level], 24, RIM[level], (0, -1, 1))
        all_coefficients(level, -h, own + h)
        gather(level, "t", msg_t[level], 32, h, (0,))
        if OY[level] >= 128:
            sent(msg_t[level][:2])
            start(msg_fc + msg_sc[REACH])
        first_sweep(level, 0, own)
        sweep_range(level, t, lv[level]["a"], 1, own - 1)
        gather(level, "t", msg_t[level], 32, h, (-1, 1))
        first_sweep(level, -h, 0)
        first_sweep(level, own, own + h)
        sweep_range(level, t, lv[level]["a"], 1 - h, 1)
        sweep_range(level, t, lv[level]["a"], own - 1, own + h - 1)

    remainder_rows(2, lv[2]["a"], 0, OX[3])
    t_next = restricted(2)
    far_t[REACH] = sum(roll(t_next[k], 32 * k, 1) for k in range(4))
    start(msg_ft + msg_st[REACH])

    def unpack_far(dest, far, side, planes, factor):
        lane = lane_iota(planes)

        def body(b):
            own, left, right = far[b], side[0, b], side[1, b]
            for k in range(4):
                tile = jnp.where(lane < 32, roll(own, -32 * k, 1), 0.0)
                tile = jnp.where((lane >= 32) & (lane < 64), roll(right, 32 - 32 * k, 1), tile)
                tile = jnp.where(lane >= 96, roll(left, 96 - 32 * k, 1), tile)
                dest[4 * b + k] = tile if factor is None else tile * factor[4 * b + k]

        over_rows(0, FAR, body, FAR)

    for one in all_sc + all_st:
        one.pending = ["arrived", "sent"]
    arrived(all_sc + [one for one in msg_fc if "arrived" in one.pending])
    q3 = lv[3]["q"]
    unpack_far(lv[3]["c"], far_c, side_c, 24, None)
    all_coefficients(3, 1 - RIM[3], OX[3] + RIM[3] - 1)
    q3[0] = q3[1]
    q3[OX[3] + 2 * RIM[3] - 1] = q3[1]
    pass_on(msg_ft, msg_st)
    sent([one for one in every if one.pending == ["sent"]])
    arrived([one for one in msg_ft if "arrived" in one.pending] + all_st)
    t3, a3, b3 = lv[3]["t"], lv[3]["a"], lv[3]["b"]
    unpack_far(t3, far_t, side_t, 32, q3)
    args3 = refs(3)

    def coarse_sweep(src, dst, s):
        first = s + 2

        def body(n, _):
            for k in range(UNROLL[3]):
                sweep_row(src, dst, *args3, first + UNROLL[3] * n + k)
            return 0

        lax.fori_loop(0, (47 - 2 * s + UNROLL[3]) // UNROLL[3], body, 0)

    coarse_sweep(t3, a3, 2)

    def coarse_pair(n, _):
        coarse_sweep(a3, b3, 2 * n + 3)
        coarse_sweep(b3, a3, 2 * n + 4)
        return 0

    lax.fori_loop(0, (ITERS - 2) // 2, coarse_pair, 0)

    prolonged(2, a3, lv[2]["a"], 2)
    sweep(2, lv[2]["a"], lv[2]["b"], 3)
    sweep(2, lv[2]["b"], lv[2]["a"], 2)
    prolonged(1, lv[2]["a"], lv[1]["a"], 2)
    sweep(1, lv[1]["a"], lv[1]["b"], 2)
    sweep(1, lv[1]["b"], lv[1]["a"], 1)
    prolonged(0, lv[1]["a"], lv[0]["a"], 1)
    a0, b0 = lv[0]["a"], lv[0]["b"]
    sweep(0, a0, b0, 1)
    args0 = refs(0)
    stores = []
    for part, (low, rows) in enumerate(((0, 16), (16, 8), (24, 8))):
        first = RIM[0] + low

        over_rows(first, rows, lambda i: sweep_row(b0, a0, *args0, i), UNROLL[0])
        for n in range(2):
            for k in range(16):
                kk = (k % 2) * 8 + k // 2
                store = pltpu.make_async_copy(
                    a0.at[pl.ds(first, rows), 16 * n + kk, pl.ds(0, 256)],
                    o_ref.at[n, k, pl.ds(low, rows), :],
                    out_sem.at[32 * part + 16 * n + k],
                )
                store.start()
                stores.append(store)
    sent([one for one in every if one.pending])
    for store in stores:
        store.wait()


def solution(mesh):
    nx, ny = mesh.shape["gx"], mesh.shape["gy"]
    f32 = jnp.float32
    scratch = []
    for level in range(4):
        rows, lanes = TX[level], LN[level]
        planes = [24, 16, 64, 24, 32, 32, 32, 32]
        planes += [32] if level > 0 else []
        planes += [32] if level < 3 else []
        scratch += [pltpu.VMEM((rows, p, lanes), f32) for p in planes]
        if level < 3:
            scratch += [pltpu.VMEM((n, p, 128), f32) for p in (24, 32) for n in (2, 6)]
        if level == 0:
            scratch += [pltpu.VMEM((rows, 32, lanes), f32)]
    scratch += [pltpu.VMEM((16, 32, 256), f32)]
    scratch += [pltpu.VMEM((FAR, 24, 128), f32), pltpu.VMEM((FAR, 32, 128), f32)]
    scratch += [pltpu.VMEM((2, FAR, 24, 128), f32), pltpu.VMEM((2, FAR, 32, 128), f32)]
    scratch += [
        pltpu.VMEM((32, 256), f32),
        pltpu.VMEM((32, 256), jnp.int32),
        pltpu.VMEM((32, 256), jnp.int32),
    ]
    messages = 4 + 6 * 8 + 4 * REACH + 8 * (REACH - DIRECT) + 8
    scratch += [pltpu.SemaphoreType.DMA((51,)), pltpu.SemaphoreType.DMA((96,))]
    scratch += [pltpu.SemaphoreType.DMA((messages,)), pltpu.SemaphoreType.DMA((messages,))]

    def per_device(misfit, viscosity, friction, ice_mask, grounded):
        return pl.pallas_call(
            functools.partial(kernel, nx, ny),
            out_shape=jax.ShapeDtypeStruct(misfit.shape, f32),
            in_specs=[pl.BlockSpec(memory_space=HBM)] * 5,
            out_specs=pl.BlockSpec(memory_space=HBM),
            scratch_shapes=scratch,
            compiler_params=pltpu.CompilerParams(
                collective_id=0, has_side_effects=True, vmem_limit_bytes=62 * 2**20
            ),
        )(misfit, viscosity, friction, ice_mask, grounded)

    placed = (
        P(None, None, "gx", "gy"),
        P(None, "gx", "gy"),
        P("gx", "gy"),
        P("gx", "gy"),
        P("gx", "gy"),
    )
    return jax.shard_map(
        per_device, mesh=mesh, in_specs=placed, out_specs=P(None, None, "gx", "gy"), check_vma=False
    )
```

```python
import functools

import jax
import jax.numpy as jnp
from jax import lax
from jax.experimental import pallas as pl
from jax.experimental.pallas import tpu as pltpu
from jax.sharding import PartitionSpec as P

MESH = pl.DeviceIdType.MESH
HBM = pltpu.MemorySpace.HBM
OMEGA = 0.6
CROSS = 0.75
ITERS = 20

OX = (32, 16, 8, 4)
OY = (256, 128, 64, 32)
LN = (384, 256, 128, 128)
RIM = (4, 5, 6, 24)
PW = (4, 8, 16, 32)
TX = tuple(o + 2 * h for o, h in zip(OX[:3], RIM)) + (64,)
UNROLL = (4, 6, 8, 16)
UNROLL_C = (4, 4, 6, 10)
UNROLL_R = (2, 4, 4)
DIRECT = 6
REACH = 6
FAR = 2 * REACH + 1
SIDES = ((0, -1), (0, 1), (-1, -1), (-1, 1), (1, -1), (1, 1))


def over_rows(first, count, body, unroll):
    steps = count // unroll

    def step(n, _):
        for k in range(unroll):
            body(first + n * unroll + k)
        return 0

    if steps > 0:
        lax.fori_loop(0, steps, step, 0)
    for k in range(steps * unroll, count):
        body(first + k)


def lane_iota(rows):
    return lax.broadcasted_iota(jnp.int32, (rows, 128), 1)


def roll(x, shift, axis):
    return pltpu.roll(x, shift % x.shape[axis], axis)


def exact_dot(x, sel):
    hi = x.astype(jnp.bfloat16)
    rest = x - hi.astype(jnp.float32)
    mid = rest.astype(jnp.bfloat16)
    low = (rest - mid.astype(jnp.float32)).astype(jnp.bfloat16)
    rows = x.shape[0]
    out = jnp.dot(
        jnp.concatenate([hi, mid, low], 0), sel, preferred_element_type=jnp.float32
    )
    return (out[:rows] + out[rows : 2 * rows]) + out[2 * rows :]


def restrict_matrix(level):
    width = min(LN[level], OY[level]) if OY[level] >= 128 else 128
    fine = lax.broadcasted_iota(jnp.int32, (width, 128), 0)
    coarse = lax.broadcasted_iota(jnp.int32, (width, 128), 1)
    hit = (fine // 2 == coarse) & (fine < OY[level])
    return jnp.where(hit, 0.25, 0.0).astype(jnp.bfloat16)


def prolong_matrix(level):
    lc, lf = LN[level + 1], LN[level]
    coarse = lax.broadcasted_iota(jnp.int32, (lc, lf), 0)
    fine = lax.broadcasted_iota(jnp.int32, (lc, lf), 1)
    middle = (OY[level] + lf) // 2
    source = jnp.where(fine < middle, fine // 2, lc - (lf - fine + 1) // 2)
    return jnp.where(source == coarse, 1.0, 0.0).astype(jnp.bfloat16)


class Message:
    def __init__(self, place, sems, index, src, dst, dx, dy):
        gx, gy, nx, ny = place
        self.way = (dx, dy)
        self.to_there = (gx + dx >= 0) & (gx + dx < nx) & (gy + dy >= 0) & (gy + dy < ny)
        self.from_there = (gx - dx >= 0) & (gx - dx < nx) & (gy - dy >= 0) & (gy - dy < ny)
        target = (jnp.clip(gx + dx, 0, nx - 1), jnp.clip(gy + dy, 0, ny - 1))
        self.dst = dst
        self.pending = []
        self.copy = pltpu.make_async_remote_copy(
            src_ref=src,
            dst_ref=dst,
            send_sem=sems[0].at[index],
            recv_sem=sems[1].at[index],
            device_id=target,
            device_id_type=MESH,
        )


def by_way(messages):
    groups = {}
    for one in messages:
        groups.setdefault(one.way, []).append(one)
    return groups.values()


def clear(messages):
    for group in by_way(messages):

        @pl.when(jnp.logical_not(group[0].from_there))
        def _(group=group):
            for one in group:
                one.dst[...] = jnp.zeros(one.dst.shape, one.dst.dtype)


def start(messages):
    for group in by_way(messages):

        @pl.when(group[0].to_there)
        def _(group=group):
            for one in group:
                one.copy.start()

    for one in messages:
        one.pending = ["arrived", "sent"]


def arrived(messages):
    for group in by_way(messages):

        @pl.when(group[0].from_there)
        def _(group=group):
            for one in group:
                one.copy.wait_recv()

    for one in messages:
        one.pending.remove("arrived")


def sent(messages):
    for group in by_way(messages):

        @pl.when(group[0].to_there)
        def _(group=group):
            for one in group:
                one.copy.wait_send()

    for one in messages:
        one.pending.remove("sent")


def pack_columns(level, source, dest, planes):
    w, rim = PW[level], RIM[level]
    lane = lane_iota(planes)
    tile = (OY[level] - 1) // 128
    edge = (OY[level] - w) % 128
    zero = jnp.zeros((planes, 128), jnp.float32)
    left, right = zero, zero
    for i in range(OX[level]):
        here = (lane >= w * i) & (lane < w * i + w)
        a = source[rim + i, :, 0:128]
        b = source[rim + i, :, tile * 128 : tile * 128 + 128]
        left = jnp.where(here, roll(a, w * i, 1), left)
        right = jnp.where(here, roll(b, w * i - edge, 1), right)
    dest[0] = left
    dest[1] = right


def unpack_columns(level, dest, packs, planes, reach, side, skip=0):
    w, rim, own = PW[level], RIM[level], OX[level]
    lane = lane_iota(planes)
    last = LN[level] - 128
    start = OY[level] % 128
    row0, count, shift, slot = {
        -1: (-reach, reach - skip, own - reach, 2),
        0: (0, own, 0, 0),
        1: (own + skip, reach - skip, skip, 4),
    }[side]
    for i in range(count):
        at = w * (i + shift)
        right = roll(packs[slot + 1], start - at, 1)
        left = roll(packs[slot], -w - at, 1)
        row = rim + row0 + i
        if OY[level] < 128:
            rest = dest[row, :, last : last + 128]
        else:
            rest = jnp.zeros((planes, 128), jnp.float32)
        tile = jnp.where((lane >= start) & (lane < start + w), right, rest)
        dest[row, :, last : last + 128] = jnp.where(lane >= 128 - w, left, tile)


def coefficients(level, c, e, y4, z, q, r, g, low, high):
    scale = 0.25**level
    half, cross = 0.5 * scale, CROSS * scale
    lanes, rim = LN[level], RIM[level]
    first, count = rim + low, high - low
    sub = lax.broadcasted_iota(jnp.int32, (8, lanes), 0)
    e[first - 1] = half * (c[first - 1, 0:16, :] + c[first, 0:16, :])

    def body(i):
        here = c[i, 0:16, :]
        north, south = roll(here, -1, 1), roll(here, 1, 1)
        east = half * (here + c[i + 1, 0:16, :])
        west = half * (here + c[i - 1, 0:16, :])
        nf, sf = half * (here + north), half * (here + south)
        e[i] = east
        y4[i, 0:16, :] = nf
        y4[i, 16:32, :] = sf
        y4[i, 32:48, :] = cross * north
        y4[i, 48:64, :] = cross * south
        even, odd = here[0:8], here[8:16]
        inner = 2.0 * (even + odd)
        upper = jnp.where(sub < 7, 2.0 * (odd + roll(even, -1, 0)), 0.0)
        lower = roll(upper, 1, 0)
        z[i, 0:8, :] = inner
        z[i, 8:16, :] = upper
        z[i, 16:24, :] = lower
        ice = c[i, 16:17, :]
        drag = jnp.where(sub == 0, c[i, 17:18, :], 0.0)
        vertical = jnp.concatenate([inner + lower + drag, inner + upper], 0)
        xs, ys = east + west, nf + sf
        for k, lateral in enumerate((4.0 * xs + ys, xs + 4.0 * ys)):
            diag = ice * (lateral + vertical) + (1.0 - ice)
            inv = OMEGA / diag
            if q is not None:
                q[i, 16 * k : 16 * k + 16, :] = inv
            r[i, 16 * k : 16 * k + 16, :] = ice * inv
            if g is not None:
                g[i, 16 * k : 16 * k + 16, :] = diag * (1.0 / OMEGA)

    over_rows(first, count, body, UNROLL_C[level])


def off_diagonal(w, e, y4, z, i):
    u0, u, u2 = w[i - 1, 0:16, :], w[i, 0:16, :], w[i + 1, 0:16, :]
    v0, v, v2 = w[i - 1, 16:32, :], w[i, 16:32, :], w[i + 1, 16:32, :]
    west, east = e[i - 1], e[i]
    nf, sf, mn, ms = (y4[i, 16 * k : 16 * k + 16, :] for k in range(4))
    inner, upper, lower = (z[i, 8 * k : 8 * k + 8, :] for k in range(3))
    du, dv, v4 = u2 - u0, v2 - v0, 4.0 * v
    xu = 4.0 * (east * u2 + west * u0)
    xv = east * v2 + west * v0
    yu = roll(sf * u + ms * dv, -1, 1) + roll(nf * u - mn * dv, 1, 1)
    yv = roll(sf * v4 + ms * du, -1, 1) + roll(nf * v4 - mn * du, 1, 1)

    def column(f):
        even, odd = f[0:8], f[8:16]
        return jnp.concatenate(
            [inner * odd + lower * roll(odd, 1, 0), inner * even + upper * roll(even, -1, 0)], 0
        )

    return (u, v), (xu + yu + column(u), xv + yv + column(v))


def sweep_row(src, dst, e, y4, z, r, tt, i):
    fields, sums = off_diagonal(src, e, y4, z, i)
    for k in range(2):
        at = slice(16 * k, 16 * k + 16)
        dst[i, at, :] = (1.0 - OMEGA) * fields[k] + (tt[i, at, :] + r[i, at, :] * sums[k])


def remainder_row(src, e, y4, z, r, tt, g, i, lanes):
    fields, sums = off_diagonal(src, e, y4, z, i)
    parts = []
    for k in range(2):
        at = slice(16 * k, 16 * k + 16)
        change = tt[i, at, :] + r[i, at, :] * sums[k] - OMEGA * fields[k]
        parts.append(change[:, 0:lanes] * g[i, at, 0:lanes])
    return jnp.concatenate(parts, 0)


def kernel(nx, ny, m_ref, v_ref, f_ref, i_ref, b_ref, o_ref, *scratch):
    names = iter(scratch)
    lv = []
    for level in range(4):
        keys = ["c", "e", "y4", "z", "r", "t", "a", "b"]
        keys += ["q"] if level > 0 else []
        keys += ["g"] if level < 3 else []
        keys += ["spc", "rpc", "spt", "rpt"] if level < 3 else []
        keys += ["raw"] if level == 0 else []
        lv.append({key: next(names) for key in keys})
    rest, far_c, far_t, side_c, side_t, fr, ic, gr = (next(names) for _ in range(8))
    in_sem, out_sem, send_sem, recv_sem = (next(names) for _ in range(4))

    gx, gy = lax.axis_index("gx"), lax.axis_index("gy")
    place = (gx, gy, nx, ny)
    sems = (send_sem, recv_sem)
    count = iter(range(10**6))

    def message(src, dst, dx, dy):
        return Message(place, sems, next(count), src, dst, dx, dy)

    def rim_messages(level, array, packs, landed, reach):
        rim, own = RIM[level], OX[level]
        lanes = pl.ds(0, max(OY[level], 128))
        out = [
            message(
                array.at[pl.ds(rim, reach), :, lanes],
                array.at[pl.ds(rim + own, reach), :, lanes], -1, 0),
            message(
                array.at[pl.ds(rim + own - reach, reach), :, lanes],
                array.at[pl.ds(rim - reach, reach), :, lanes], 1, 0),
        ]
        for slot, (dx, dy) in enumerate(SIDES):
            out.append(message(packs.at[0 if dy > 0 else 1], landed.at[slot], -dx, -dy))
        return out

    def far_messages(far, side):
        out = []
        for d in [k * s for k in range(REACH, 0, -1) for s in (1, -1)]:
            out.append(message(far.at[REACH], far.at[REACH - d], d, 0))
            for n in range(2 if abs(d) > DIRECT else 0):
                out.append(message(far.at[REACH], side.at[n, REACH - d], d, 1 - 2 * n))
        return out

    def side_messages(far, side):
        near = pl.ds(REACH - DIRECT, 2 * DIRECT + 1)
        whole = [message(far.at[near], side.at[n, near], 0, 1 - 2 * n) for n in range(2)]
        first = next(count) - 2
        blocks = {
            b: [
                Message(place, sems, first + n, far.at[b], side.at[n, b], 0, 1 - 2 * n)
                for n in range(2)
            ]
            for b in range(REACH - DIRECT, REACH + DIRECT + 1)
        }
        return whole, blocks

    def pass_on(far, side):
        for d in range(1, DIRECT + 1):
            for s in (d, -d):
                arrived([one for one in far if one.way == (s, 0)])
                start(side[REACH - s])

    c0, t0, raw = lv[0]["c"], lv[0]["t"], lv[0]["raw"]
    msg_c = [rim_messages(n, lv[n]["c"], lv[n]["spc"], lv[n]["rpc"], RIM[n] - (n == 0)) for n in range(3)]
    msg_t = [
        rim_messages(
            n, lv[n]["t"] if n > 0 else raw, lv[n]["spt"], lv[n]["rpt"], 2
        )
        for n in range(3)
    ]
    def late_messages(level, array, near, far):
        rim, own, lanes = RIM[level], OX[level], pl.ds(0, max(OY[level], 128))
        return [
            message(
                array.at[pl.ds(source, far - near), :, lanes],
                array.at[pl.ds(target, far - near), :, lanes], dx, 0)
            for dx, source, target in (
                (-1, rim + near, rim + own + near),
                (1, rim + own - far, rim - far),
            )
        ]

    late = late_messages(0, c0, RIM[0] - 1, RIM[0]) + late_messages(0, raw, 2, RIM[0] - 1)
    late_t = {n: late_messages(n, lv[n]["t"], 2, RIM[n] - 1) for n in (1, 2)}
    msg_fc, msg_ft = far_messages(far_c, side_c), far_messages(far_t, side_t)
    all_sc, msg_sc = side_messages(far_c, side_c)
    all_st, msg_st = side_messages(far_t, side_t)
    every = sum(msg_c + msg_t, late + late_t[1] + late_t[2]) + msg_fc + msg_ft + all_sc + all_st

    barrier = pltpu.get_barrier_semaphore()
    far_away = [d for d in range(-REACH, REACH + 1) if abs(d) > DIRECT]
    partners = [(d, 0) for d in range(-REACH, REACH + 1) if d != 0] + list(SIDES)
    partners += [(d, s) for d in far_away for s in (-1, 1)]
    arrivals = 0
    for dx, dy in partners:
        there = (gx + dx >= 0) & (gx + dx < nx) & (gy + dy >= 0) & (gy + dy < ny)
        arrivals = arrivals + there.astype(jnp.int32)

        @pl.when(there)
        def _(dx=dx, dy=dy):
            pl.semaphore_signal(
                barrier,
                inc=1,
                device_id=(jnp.clip(gx + dx, 0, nx - 1), jnp.clip(gy + dy, 0, ny - 1)),
                device_id_type=MESH,
            )

    own0 = pl.ds(RIM[0], OX[0])
    loads = []
    for k in range(16):
        kk = (k % 2) * 8 + k // 2
        loads.append((v_ref.at[k], lv[0]["c"].at[own0, kk, pl.ds(0, 256)]))
        for n in range(2):
            loads.append((m_ref.at[n, k], raw.at[own0, 16 * n + kk, pl.ds(0, 256)]))
    loads += [(f_ref, fr), (i_ref, ic), (b_ref, gr)]
    loads = [pltpu.make_async_copy(s, d, in_sem.at[n]) for n, (s, d) in enumerate(loads)]
    for load in loads:
        load.start()

    clear(every)
    for load in loads:
        load.wait()

    ic_f = ic[...].astype(jnp.float32)
    ic_f = ic_f.reshape(OX[0], 1, 256)
    dr_f = (fr[...] * gr[...].astype(jnp.float32)).reshape(OX[0], 1, 256)
    sub = lax.broadcasted_iota(jnp.int32, (OX[0], 8, 256), 1)
    c0[own0, 16:24, 0:256] = jnp.where(sub == 0, ic_f, jnp.where(sub == 1, dr_f, 0.0))

    pack_columns(0, c0, lv[0]["spc"], 24)
    pack_columns(0, raw, lv[0]["spt"], 32)

    pl.semaphore_wait(barrier, arrivals)
    start(msg_c[0][2:4] + msg_t[0][2:4])
    start(msg_c[0][:2] + msg_t[0][:2] + msg_c[0][4:] + msg_t[0][4:])

    for level in range(3):
        rim, own, width = RIM[level], OX[level + 1], max(OY[level], 128)
        fine = lv[level]["c"]
        block = fine[rim : rim + 2 * own, :, 0:width].reshape(own, 2, 24, width)
        block = (block[:, 0] + block[:, 1]).reshape(own * 24, width)
        coarse = exact_dot(block, restrict_matrix(level)).reshape(own, 24, 128)
        if level < 2:
            target = lv[level + 1]["c"]
            target[RIM[level + 1] : RIM[level + 1] + own, :, 0:128] = coarse
            pack_columns(level + 1, target, lv[level + 1]["spc"], 24)
        else:
            far_c[REACH] = sum(roll(coarse[k], 32 * k, 1) for k in range(4))

    def refs(level):
        return [lv[level][key] for key in ("e", "y4", "z", "r", "t")]

    def gather(level, kind, messages, planes, reach, sides):
        landed = lv[level]["rp" + kind]
        array = raw if (level, kind) == (0, "t") else lv[level][kind]
        for side in sides:
            which = {0: messages[2:4], -1: messages[1:2] + messages[4:6], 1: messages[0:1] + messages[6:8]}
            arrived(which[side])
        if OY[level] < 128 and 0 in sides:
            sent(messages[:2] + (late_t[level] if kind == "t" else []))
        for side in sides:
            unpack_columns(level, array, landed, planes, reach, side)

    def first_sweep(level, low, high):
        t = lv[level]["t"]
        source, factor = (raw, lv[0]["r"]) if level == 0 else (t, lv[level]["q"])

        def body(i):
            t[i] = source[i] * factor[i]

        over_rows(RIM[level] + low, high - low, body, min(4, high - low))

    def sweep_range(level, src, dst, low, high):
        args = refs(level)

        over_rows(
            RIM[level] + low,
            high - low,
            lambda i: sweep_row(src, dst, *args, i),
            UNROLL[level],
        )

    def sweep(level, src, dst, rows):
        sweep_range(level, src, dst, -rows, OX[level] + rows)

    def remainder_rows(level, src, low, high):
        args = refs(level)
        width = max(OY[level], 128)

        def body(n):
            i = RIM[level] + 2 * n
            pair = [remainder_row(src, *args, lv[level]["g"], i + k, width) for k in range(2)]
            rest[n, :, 0:width] = pair[0] + pair[1]

        over_rows(low, high - low, body, min(UNROLL_R[level], high - low))

    def restricted(level):
        width, own = max(OY[level], 128), OX[level + 1]
        block = rest[0:own, :, 0:width].reshape(own * 32, width)
        return exact_dot(block, restrict_matrix(level)).reshape(own, 32, 128)

    def prolonged(level, src, dst, rows):
        low, high = RIM[level + 1] - rows, RIM[level + 1] + OX[level + 1] + rows
        n = high - low
        sel = prolong_matrix(level)
        spread = lv[level]["g"]
        block = src[low:high].reshape(n * 32, LN[level + 1])
        spread[0:n] = exact_dot(block, sel).reshape(n, 32, LN[level])

        def body(k):
            i = RIM[level] + 2 * (k - rows)
            extra = spread[k]
            dst[i] = dst[i] + extra
            dst[i + 1] = dst[i + 1] + extra

        over_rows(0, n, body, 6)

    def all_coefficients(level, low, high):
        refs_c = [lv[level].get(k) for k in ("c", "e", "y4", "z", "q", "r", "g")]
        coefficients(level, *refs_c, low, high)

    n0, h0 = OX[0], RIM[0] - 2
    gather(0, "c", msg_c[0], 24, h0 + 1, (0,))
    gather(0, "t", msg_t[0], 32, h0, (0,))
    all_coefficients(0, 1, n0 - 1)
    start(msg_c[1] + late + msg_c[2])
    first_sweep(0, 1, n0 - 1)
    sweep_range(0, t0, lv[0]["a"], 2, n0 - 2)
    remainder_rows(0, lv[0]["a"], 2, OX[1] - 2)
    gather(0, "c", msg_c[0], 24, h0 + 1, (-1, 1))
    gather(0, "t", msg_t[0], 32, h0, (-1, 1))
    for low, high in ((-h0, 1), (n0 - 1, n0 + h0)):
        all_coefficients(0, low, high)
        first_sweep(0, low, high)
    for low, high in ((1 - h0, 2), (n0 - 2, n0 + h0 - 1)):
        sweep_range(0, t0, lv[0]["a"], low, high)
    for low, high in ((0, 2), (OX[1] - 2, OX[1])):
        remainder_rows(0, lv[0]["a"], low, high)

    def outer_rows(level):
        own, h = OX[level], RIM[level] - 1
        arrived(late_t[level])
        for side in (-1, 1):
            unpack_columns(level, lv[level]["t"], lv[level]["rpt"], 32, h, side, 2)
        for low, high in ((-h, -2), (own + 2, own + h)):
            first_sweep(level, low, high)
        for low, high in ((1 - h, -1), (own + 1, own + h - 1)):
            sweep_range(level, lv[level]["t"], lv[level]["a"], low, high)

    for level in (1, 2):
        t, own, h = lv[level]["t"], OX[level], RIM[level] - 1
        if level == 2:
            remainder_rows(1, lv[1]["a"], 0, own)
        t[RIM[level] : RIM[level] + own, :, 0:128] = restricted(level - 1)
        start(msg_t[level][:2])
        pack_columns(level, t, lv[level]["spt"], 32)
        start(msg_t[level][4:] + msg_t[level][2:4] + late_t[level])
        if level == 2:
            outer_rows(1)
            pass_on(msg_fc, msg_sc)
        if level == 1:
            arrived(late)
            for side in (-1, 1):
                unpack_columns(0, c0, lv[0]["rpc"], 24, h0 + 2, side, h0 + 1)
                unpack_columns(0, raw, lv[0]["rpt"], 32, h0 + 1, side, h0)
            for row, inward in ((-h0 - 1, -h0), (n0 + h0, n0 + h0 - 1)):
                all_coefficients(0, row, row + 1)
                first_sweep(0, row, row + 1)
                sweep_range(0, t0, lv[0]["a"], inward, inward + 1)
        gather(level, "c", msg_c[level], 24, RIM[level], (0, -1, 1))
        all_coefficients(level, -h, own + h)
        gather(level, "t", msg_t[level], 32, 2, (0,))
        if OY[level] >= 128:
            sent(msg_t[level][:2] + late_t[level])
            start(msg_fc + msg_sc[REACH])
        first_sweep(level, 0, own)
        sweep_range(level, t, lv[level]["a"], 1, own - 1)
        gather(level, "t", msg_t[level], 32, 2, (-1, 1))
        first_sweep(level, -2, 0)
        first_sweep(level, own, own + 2)
        sweep_range(level, t, lv[level]["a"], -1, 1)
        sweep_range(level, t, lv[level]["a"], own - 1, own + 1)

    remainder_rows(2, lv[2]["a"], 0, OX[3])
    t_next = restricted(2)
    far_t[REACH] = sum(roll(t_next[k], 32 * k, 1) for k in range(4))
    start(msg_ft + msg_st[REACH])
    outer_rows(2)

    def unpack_far(dest, far, side, planes, factor):
        lane = lane_iota(planes)

        def body(b):
            own, left, right = far[b], side[0, b], side[1, b]
            for k in range(4):
                tile = jnp.where(lane < 32, roll(own, -32 * k, 1), 0.0)
                tile = jnp.where((lane >= 32) & (lane < 64), roll(right, 32 - 32 * k, 1), tile)
                tile = jnp.where(lane >= 96, roll(left, 96 - 32 * k, 1), tile)
                dest[4 * b + k] = tile if factor is None else tile * factor[4 * b + k]

        over_rows(0, FAR, body, FAR)

    for one in all_sc + all_st:
        one.pending = ["arrived", "sent"]
    arrived(all_sc + [one for one in msg_fc if "arrived" in one.pending])
    q3 = lv[3]["q"]
    unpack_far(lv[3]["c"], far_c, side_c, 24, None)
    all_coefficients(3, 1 - RIM[3], OX[3] + RIM[3] - 1)
    q3[0] = q3[1]
    q3[OX[3] + 2 * RIM[3] - 1] = q3[1]
    pass_on(msg_ft, msg_st)
    sent([one for one in every if one.pending == ["sent"]])
    arrived([one for one in msg_ft if "arrived" in one.pending] + all_st)
    t3, a3, b3 = lv[3]["t"], lv[3]["a"], lv[3]["b"]
    unpack_far(t3, far_t, side_t, 32, q3)
    args3 = refs(3)

    def coarse_sweep(src, dst, s):
        first = s + 2

        def body(n, _):
            for k in range(UNROLL[3]):
                sweep_row(src, dst, *args3, first + UNROLL[3] * n + k)
            return 0

        lax.fori_loop(0, (47 - 2 * s + UNROLL[3]) // UNROLL[3], body, 0)

    coarse_sweep(t3, a3, 2)

    def coarse_pair(n, _):
        coarse_sweep(a3, b3, 2 * n + 3)
        coarse_sweep(b3, a3, 2 * n + 4)
        return 0

    lax.fori_loop(0, (ITERS - 2) // 2, coarse_pair, 0)

    prolonged(2, a3, lv[2]["a"], 2)
    sweep(2, lv[2]["a"], lv[2]["b"], 3)
    sweep(2, lv[2]["b"], lv[2]["a"], 2)
    prolonged(1, lv[2]["a"], lv[1]["a"], 2)
    sweep(1, lv[1]["a"], lv[1]["b"], 2)
    sweep(1, lv[1]["b"], lv[1]["a"], 1)
    prolonged(0, lv[1]["a"], lv[0]["a"], 1)
    a0, b0 = lv[0]["a"], lv[0]["b"]
    sweep(0, a0, b0, 1)
    args0 = refs(0)
    stores = []
    for part, (low, rows) in enumerate(((0, 16), (16, 8), (24, 8))):
        first = RIM[0] + low

        over_rows(first, rows, lambda i: sweep_row(b0, a0, *args0, i), UNROLL[0])
        for n in range(2):
            for k in range(16):
                kk = (k % 2) * 8 + k // 2
                store = pltpu.make_async_copy(
                    a0.at[pl.ds(first, rows), 16 * n + kk, pl.ds(0, 256)],
                    o_ref.at[n, k, pl.ds(low, rows), :],
                    out_sem.at[32 * part + 16 * n + k],
                )
                store.start()
                stores.append(store)
    sent([one for one in every if one.pending])
    for store in stores:
        store.wait()


def solution(mesh):
    nx, ny = mesh.shape["gx"], mesh.shape["gy"]
    f32 = jnp.float32
    scratch = []
    for level in range(4):
        rows, lanes = TX[level], LN[level]
        planes = [24, 16, 64, 24, 32, 32, 32, 32]
        planes += [32] if level > 0 else []
        planes += [32] if level < 3 else []
        scratch += [pltpu.VMEM((rows, p, lanes), f32) for p in planes]
        if level < 3:
            scratch += [pltpu.VMEM((n, p, 128), f32) for p in (24, 32) for n in (2, 6)]
        if level == 0:
            scratch += [pltpu.VMEM((rows, 32, lanes), f32)]
    scratch += [pltpu.VMEM((16, 32, 256), f32)]
    scratch += [pltpu.VMEM((FAR, 24, 128), f32), pltpu.VMEM((FAR, 32, 128), f32)]
    scratch += [pltpu.VMEM((2, FAR, 24, 128), f32), pltpu.VMEM((2, FAR, 32, 128), f32)]
    scratch += [
        pltpu.VMEM((32, 256), f32),
        pltpu.VMEM((32, 256), jnp.int32),
        pltpu.VMEM((32, 256), jnp.int32),
    ]
    messages = 8 + 6 * 8 + 4 * REACH + 8 * (REACH - DIRECT) + 8
    scratch += [pltpu.SemaphoreType.DMA((51,)), pltpu.SemaphoreType.DMA((96,))]
    scratch += [pltpu.SemaphoreType.DMA((messages,)), pltpu.SemaphoreType.DMA((messages,))]

    def per_device(misfit, viscosity, friction, ice_mask, grounded):
        return pl.pallas_call(
            functools.partial(kernel, nx, ny),
            out_shape=jax.ShapeDtypeStruct(misfit.shape, f32),
            in_specs=[pl.BlockSpec(memory_space=HBM)] * 5,
            out_specs=pl.BlockSpec(memory_space=HBM),
            scratch_shapes=scratch,
            compiler_params=pltpu.CompilerParams(
                collective_id=0, has_side_effects=True, vmem_limit_bytes=62 * 2**20
            ),
        )(misfit, viscosity, friction, ice_mask, grounded)

    placed = (
        P(None, None, "gx", "gy"),
        P(None, "gx", "gy"),
        P("gx", "gy"),
        P("gx", "gy"),
        P("gx", "gy"),
    )
    return jax.shard_map(
        per_device, mesh=mesh, in_specs=placed, out_specs=P(None, None, "gx", "gy"), check_vma=False
    )
```

```python
import functools

import jax
import jax.numpy as jnp
from jax import lax
from jax.experimental import pallas as pl
from jax.experimental.pallas import tpu as pltpu
from jax.sharding import PartitionSpec as P

MESH = pl.DeviceIdType.MESH
HBM = pltpu.MemorySpace.HBM
OMEGA = 0.6
CROSS = 0.75
ITERS = 20

OX = (32, 16, 8, 4)
OY = (256, 128, 64, 32)
LN = (384, 256, 128, 128)
RIM = (4, 5, 6, 24)
PW = (4, 8, 16, 32)
TX = tuple(o + 2 * h for o, h in zip(OX[:3], RIM)) + (64,)
UNROLL = (4, 10, 9, 16)
UNROLL_C = (4, 4, 6, 10)
UNROLL_R = (2, 4, 4)
DIRECT = 6
REACH = 6
FAR = 2 * REACH + 1
SIDES = ((0, -1), (0, 1), (-1, -1), (-1, 1), (1, -1), (1, 1))


def over_rows(first, count, body, unroll):
    steps = count // unroll

    def step(n, _):
        for k in range(unroll):
            body(first + n * unroll + k)
        return 0

    if steps > 0:
        lax.fori_loop(0, steps, step, 0)
    for k in range(steps * unroll, count):
        body(first + k)


def lane_iota(rows):
    return lax.broadcasted_iota(jnp.int32, (rows, 128), 1)


def roll(x, shift, axis):
    return pltpu.roll(x, shift % x.shape[axis], axis)


def exact_dot(x, sel):
    hi = x.astype(jnp.bfloat16)
    rest = x - hi.astype(jnp.float32)
    mid = rest.astype(jnp.bfloat16)
    low = (rest - mid.astype(jnp.float32)).astype(jnp.bfloat16)
    rows = x.shape[0]
    out = jnp.dot(
        jnp.concatenate([hi, mid, low], 0), sel, preferred_element_type=jnp.float32
    )
    return (out[:rows] + out[rows : 2 * rows]) + out[2 * rows :]


def restrict_matrix(level):
    width = min(LN[level], OY[level]) if OY[level] >= 128 else 128
    fine = lax.broadcasted_iota(jnp.int32, (width, 128), 0)
    coarse = lax.broadcasted_iota(jnp.int32, (width, 128), 1)
    hit = (fine // 2 == coarse) & (fine < OY[level])
    return jnp.where(hit, 0.25, 0.0).astype(jnp.bfloat16)


def prolong_matrix(level):
    lc, lf = LN[level + 1], LN[level]
    coarse = lax.broadcasted_iota(jnp.int32, (lc, lf), 0)
    fine = lax.broadcasted_iota(jnp.int32, (lc, lf), 1)
    middle = (OY[level] + lf) // 2
    source = jnp.where(fine < middle, fine // 2, lc - (lf - fine + 1) // 2)
    return jnp.where(source == coarse, 1.0, 0.0).astype(jnp.bfloat16)


class Message:
    def __init__(self, place, sems, index, src, dst, dx, dy):
        gx, gy, nx, ny = place
        self.way = (dx, dy)
        self.to_there = (gx + dx >= 0) & (gx + dx < nx) & (gy + dy >= 0) & (gy + dy < ny)
        self.from_there = (gx - dx >= 0) & (gx - dx < nx) & (gy - dy >= 0) & (gy - dy < ny)
        target = (jnp.clip(gx + dx, 0, nx - 1), jnp.clip(gy + dy, 0, ny - 1))
        self.dst = dst
        self.pending = []
        self.copy = pltpu.make_async_remote_copy(
            src_ref=src,
            dst_ref=dst,
            send_sem=sems[0].at[index],
            recv_sem=sems[1].at[index],
            device_id=target,
            device_id_type=MESH,
        )


def by_way(messages):
    groups = {}
    for one in messages:
        groups.setdefault(one.way, []).append(one)
    return groups.values()


def clear(messages):
    for group in by_way(messages):

        @pl.when(jnp.logical_not(group[0].from_there))
        def _(group=group):
            for one in group:
                one.dst[...] = jnp.zeros(one.dst.shape, one.dst.dtype)


def start(messages):
    for group in by_way(messages):

        @pl.when(group[0].to_there)
        def _(group=group):
            for one in group:
                one.copy.start()

    for one in messages:
        one.pending = ["arrived", "sent"]


def arrived(messages):
    for group in by_way(messages):

        @pl.when(group[0].from_there)
        def _(group=group):
            for one in group:
                one.copy.wait_recv()

    for one in messages:
        one.pending.remove("arrived")


def sent(messages):
    for group in by_way(messages):

        @pl.when(group[0].to_there)
        def _(group=group):
            for one in group:
                one.copy.wait_send()

    for one in messages:
        one.pending.remove("sent")


def pack_columns(level, source, dest, planes):
    w, rim = PW[level], RIM[level]
    lane = lane_iota(planes)
    tile = (OY[level] - 1) // 128
    edge = (OY[level] - w) % 128
    zero = jnp.zeros((planes, 128), jnp.float32)
    left, right = zero, zero
    for i in range(OX[level]):
        here = (lane >= w * i) & (lane < w * i + w)
        a = source[rim + i, :, 0:128]
        b = source[rim + i, :, tile * 128 : tile * 128 + 128]
        left = jnp.where(here, roll(a, w * i, 1), left)
        right = jnp.where(here, roll(b, w * i - edge, 1), right)
    dest[0] = left
    dest[1] = right


def unpack_columns(level, dest, packs, planes, reach, side, skip=0):
    w, rim, own = PW[level], RIM[level], OX[level]
    lane = lane_iota(planes)
    last = LN[level] - 128
    start = OY[level] % 128
    row0, count, shift, slot = {
        -1: (-reach, reach - skip, own - reach, 2),
        0: (0, own, 0, 0),
        1: (own + skip, reach - skip, skip, 4),
    }[side]
    for i in range(count):
        at = w * (i + shift)
        right = roll(packs[slot + 1], start - at, 1)
        left = roll(packs[slot], -w - at, 1)
        row = rim + row0 + i
        if OY[level] < 128:
            rest = dest[row, :, last : last + 128]
        else:
            rest = jnp.zeros((planes, 128), jnp.float32)
        tile = jnp.where((lane >= start) & (lane < start + w), right, rest)
        dest[row, :, last : last + 128] = jnp.where(lane >= 128 - w, left, tile)


def coefficients(level, c, e, y4, z, q, r, g, low, high):
    scale = 0.25**level
    half, cross = 0.5 * scale, CROSS * scale
    lanes, rim = LN[level], RIM[level]
    first, count = rim + low, high - low
    sub = lax.broadcasted_iota(jnp.int32, (8, lanes), 0)
    e[first - 1] = half * (c[first - 1, 0:16, :] + c[first, 0:16, :])

    def body(i):
        here = c[i, 0:16, :]
        north, south = roll(here, -1, 1), roll(here, 1, 1)
        east = half * (here + c[i + 1, 0:16, :])
        west = half * (here + c[i - 1, 0:16, :])
        nf, sf = half * (here + north), half * (here + south)
        e[i] = east
        y4[i, 0:16, :] = nf
        y4[i, 16:32, :] = sf
        y4[i, 32:48, :] = cross * north
        y4[i, 48:64, :] = cross * south
        even, odd = here[0:8], here[8:16]
        inner = 2.0 * (even + odd)
        upper = jnp.where(sub < 7, 2.0 * (odd + roll(even, -1, 0)), 0.0)
        lower = roll(upper, 1, 0)
        z[i, 0:8, :] = inner
        z[i, 8:16, :] = upper
        z[i, 16:24, :] = lower
        ice = c[i, 16:17, :]
        drag = jnp.where(sub == 0, c[i, 17:18, :], 0.0)
        vertical = jnp.concatenate([inner + lower + drag, inner + upper], 0)
        xs, ys = east + west, nf + sf
        for k, lateral in enumerate((4.0 * xs + ys, xs + 4.0 * ys)):
            diag = ice * (lateral + vertical) + (1.0 - ice)
            inv = OMEGA / diag
            if q is not None:
                q[i, 16 * k : 16 * k + 16, :] = inv
            r[i, 16 * k : 16 * k + 16, :] = ice * inv
            if g is not None:
                g[i, 16 * k : 16 * k + 16, :] = diag * (1.0 / OMEGA)

    over_rows(first, count, body, UNROLL_C[level])


def off_diagonal(w, e, y4, z, i):
    u0, u, u2 = w[i - 1, 0:16, :], w[i, 0:16, :], w[i + 1, 0:16, :]
    v0, v, v2 = w[i - 1, 16:32, :], w[i, 16:32, :], w[i + 1, 16:32, :]
    west, east = e[i - 1], e[i]
    nf, sf, mn, ms = (y4[i, 16 * k : 16 * k + 16, :] for k in range(4))
    inner, upper, lower = (z[i, 8 * k : 8 * k + 8, :] for k in range(3))
    du, dv, v4 = u2 - u0, v2 - v0, 4.0 * v
    xu = 4.0 * (east * u2 + west * u0)
    xv = east * v2 + west * v0
    yu = roll(sf * u + ms * dv, -1, 1) + roll(nf * u - mn * dv, 1, 1)
    yv = roll(sf * v4 + ms * du, -1, 1) + roll(nf * v4 - mn * du, 1, 1)

    def column(f):
        even, odd = f[0:8], f[8:16]
        return jnp.concatenate(
            [inner * odd + lower * roll(odd, 1, 0), inner * even + upper * roll(even, -1, 0)], 0
        )

    return (u, v), (xu + yu + column(u), xv + yv + column(v))


def sweep_row(src, dst, e, y4, z, r, tt, i):
    fields, sums = off_diagonal(src, e, y4, z, i)
    for k in range(2):
        at = slice(16 * k, 16 * k + 16)
        dst[i, at, :] = (1.0 - OMEGA) * fields[k] + (tt[i, at, :] + r[i, at, :] * sums[k])


def remainder_row(src, e, y4, z, r, tt, g, i, lanes):
    fields, sums = off_diagonal(src, e, y4, z, i)
    parts = []
    for k in range(2):
        at = slice(16 * k, 16 * k + 16)
        change = tt[i, at, :] + r[i, at, :] * sums[k] - OMEGA * fields[k]
        parts.append(change[:, 0:lanes] * g[i, at, 0:lanes])
    return jnp.concatenate(parts, 0)


def kernel(nx, ny, m_ref, v_ref, f_ref, i_ref, b_ref, o_ref, *scratch):
    names = iter(scratch)
    lv = []
    for level in range(4):
        keys = ["c", "e", "y4", "z", "r", "t", "a", "b"]
        keys += ["q"] if level > 0 else []
        keys += ["g"] if level < 3 else []
        keys += ["spc", "rpc", "spt", "rpt"] if level < 3 else []
        keys += ["raw"] if level == 0 else []
        lv.append({key: next(names) for key in keys})
    rest, far_c, far_t, side_c, side_t, fr, ic, gr = (next(names) for _ in range(8))
    in_sem, out_sem, send_sem, recv_sem = (next(names) for _ in range(4))

    gx, gy = lax.axis_index("gx"), lax.axis_index("gy")
    place = (gx, gy, nx, ny)
    sems = (send_sem, recv_sem)
    count = iter(range(10**6))

    def message(src, dst, dx, dy):
        return Message(place, sems, next(count), src, dst, dx, dy)

    def rim_messages(level, array, packs, landed, reach):
        rim, own = RIM[level], OX[level]
        lanes = pl.ds(0, max(OY[level], 128))
        out = [
            message(
                array.at[pl.ds(rim, reach), :, lanes],
                array.at[pl.ds(rim + own, reach), :, lanes], -1, 0),
            message(
                array.at[pl.ds(rim + own - reach, reach), :, lanes],
                array.at[pl.ds(rim - reach, reach), :, lanes], 1, 0),
        ]
        for slot, (dx, dy) in enumerate(SIDES):
            out.append(message(packs.at[0 if dy > 0 else 1], landed.at[slot], -dx, -dy))
        return out

    def far_messages(far, side):
        out = []
        for d in [k * s for k in range(REACH, 0, -1) for s in (1, -1)]:
            out.append(message(far.at[REACH], far.at[REACH - d], d, 0))
            for n in range(2 if abs(d) > DIRECT else 0):
                out.append(message(far.at[REACH], side.at[n, REACH - d], d, 1 - 2 * n))
        return out

    def side_messages(far, side):
        near = pl.ds(REACH - DIRECT, 2 * DIRECT + 1)
        whole = [message(far.at[near], side.at[n, near], 0, 1 - 2 * n) for n in range(2)]
        first = next(count) - 2
        blocks = {
            b: [
                Message(place, sems, first + n, far.at[b], side.at[n, b], 0, 1 - 2 * n)
                for n in range(2)
            ]
            for b in range(REACH - DIRECT, REACH + DIRECT + 1)
        }
        return whole, blocks

    def pass_on(far, side):
        for d in range(1, DIRECT + 1):
            for s in (d, -d):
                arrived([one for one in far if one.way == (s, 0)])
                start(side[REACH - s])

    c0, t0, raw = lv[0]["c"], lv[0]["t"], lv[0]["raw"]
    msg_c = [rim_messages(n, lv[n]["c"], lv[n]["spc"], lv[n]["rpc"], RIM[n] - (n == 0)) for n in range(3)]
    msg_t = [
        rim_messages(
            n, lv[n]["t"] if n > 0 else raw, lv[n]["spt"], lv[n]["rpt"], 2
        )
        for n in range(3)
    ]
    def late_messages(level, array, near, far):
        rim, own, lanes = RIM[level], OX[level], pl.ds(0, max(OY[level], 128))
        return [
            message(
                array.at[pl.ds(source, far - near), :, lanes],
                array.at[pl.ds(target, far - near), :, lanes], dx, 0)
            for dx, source, target in (
                (-1, rim + near, rim + own + near),
                (1, rim + own - far, rim - far),
            )
        ]

    late = late_messages(0, c0, RIM[0] - 1, RIM[0]) + late_messages(0, raw, 2, RIM[0] - 1)
    late_t = {n: late_messages(n, lv[n]["t"], 2, RIM[n] - 1) for n in (1, 2)}
    msg_fc, msg_ft = far_messages(far_c, side_c), far_messages(far_t, side_t)
    all_sc, msg_sc = side_messages(far_c, side_c)
    all_st, msg_st = side_messages(far_t, side_t)
    every = sum(msg_c + msg_t, late + late_t[1] + late_t[2]) + msg_fc + msg_ft + all_sc + all_st

    barrier = pltpu.get_barrier_semaphore()
    far_away = [d for d in range(-REACH, REACH + 1) if abs(d) > DIRECT]
    partners = [(d, 0) for d in range(-REACH, REACH + 1) if d != 0] + list(SIDES)
    partners += [(d, s) for d in far_away for s in (-1, 1)]
    arrivals = 0
    for dx, dy in partners:
        there = (gx + dx >= 0) & (gx + dx < nx) & (gy + dy >= 0) & (gy + dy < ny)
        arrivals = arrivals + there.astype(jnp.int32)

        @pl.when(there)
        def _(dx=dx, dy=dy):
            pl.semaphore_signal(
                barrier,
                inc=1,
                device_id=(jnp.clip(gx + dx, 0, nx - 1), jnp.clip(gy + dy, 0, ny - 1)),
                device_id_type=MESH,
            )

    own0 = pl.ds(RIM[0], OX[0])
    loads = []
    for k in range(16):
        kk = (k % 2) * 8 + k // 2
        loads.append((v_ref.at[k], c0.at[own0, kk, pl.ds(0, 256)], 0))
        for n in range(2):
            loads.append((m_ref.at[n, k], raw.at[own0, 16 * n + kk, pl.ds(0, 256)], 1))
    loads += [(f_ref, fr, 2), (i_ref, ic, 3), (b_ref, gr, 4)]
    for source, target, n in loads:
        pltpu.make_async_copy(source, target, in_sem.at[n]).start()
    landed = [c0.at[own0, pl.ds(0, 16), pl.ds(0, 256)], raw.at[own0, :, pl.ds(0, 256)], fr, ic, gr]

    clear(every)
    for n, target in enumerate(landed):
        pltpu.make_async_copy(target, target, in_sem.at[n]).wait()

    ic_f = ic[...].astype(jnp.float32)
    ic_f = ic_f.reshape(OX[0], 1, 256)
    dr_f = (fr[...] * gr[...].astype(jnp.float32)).reshape(OX[0], 1, 256)
    sub = lax.broadcasted_iota(jnp.int32, (OX[0], 8, 256), 1)
    c0[own0, 16:24, 0:256] = jnp.where(sub == 0, ic_f, jnp.where(sub == 1, dr_f, 0.0))

    pack_columns(0, c0, lv[0]["spc"], 24)
    pack_columns(0, raw, lv[0]["spt"], 32)

    pl.semaphore_wait(barrier, arrivals)
    start(msg_c[0][2:4] + msg_t[0][2:4])
    start(msg_c[0][:2] + msg_t[0][:2] + msg_c[0][4:] + msg_t[0][4:])

    for level in range(3):
        rim, own, width = RIM[level], OX[level + 1], max(OY[level], 128)
        fine = lv[level]["c"]
        block = fine[rim : rim + 2 * own, :, 0:width].reshape(own, 2, 24, width)
        block = (block[:, 0] + block[:, 1]).reshape(own * 24, width)
        coarse = exact_dot(block, restrict_matrix(level)).reshape(own, 24, 128)
        if level < 2:
            target = lv[level + 1]["c"]
            target[RIM[level + 1] : RIM[level + 1] + own, :, 0:128] = coarse
            pack_columns(level + 1, target, lv[level + 1]["spc"], 24)
        else:
            far_c[REACH] = sum(roll(coarse[k], 32 * k, 1) for k in range(4))

    def refs(level):
        return [lv[level][key] for key in ("e", "y4", "z", "r", "t")]

    def gather(level, kind, messages, planes, reach, sides):
        landed = lv[level]["rp" + kind]
        array = raw if (level, kind) == (0, "t") else lv[level][kind]
        for side in sides:
            which = {0: messages[2:4], -1: messages[1:2] + messages[4:6], 1: messages[0:1] + messages[6:8]}
            arrived(which[side])
        if OY[level] < 128 and 0 in sides:
            sent(messages[:2] + (late_t[level] if kind == "t" else []))
        for side in sides:
            unpack_columns(level, array, landed, planes, reach, side)

    def first_sweep(level, low, high):
        t = lv[level]["t"]
        source, factor = (raw, lv[0]["r"]) if level == 0 else (t, lv[level]["q"])

        def body(i):
            t[i] = source[i] * factor[i]

        over_rows(RIM[level] + low, high - low, body, min(4, high - low))

    def sweep_range(level, src, dst, low, high):
        args = refs(level)

        over_rows(
            RIM[level] + low,
            high - low,
            lambda i: sweep_row(src, dst, *args, i),
            UNROLL[level],
        )

    def sweep(level, src, dst, rows):
        sweep_range(level, src, dst, -rows, OX[level] + rows)

    def remainder_rows(level, src, low, high):
        args = refs(level)
        width = max(OY[level], 128)

        def body(n):
            i = RIM[level] + 2 * n
            pair = [remainder_row(src, *args, lv[level]["g"], i + k, width) for k in range(2)]
            rest[n, :, 0:width] = pair[0] + pair[1]

        over_rows(low, high - low, body, min(UNROLL_R[level], high - low))

    def restricted(level):
        width, own = max(OY[level], 128), OX[level + 1]
        block = rest[0:own, :, 0:width].reshape(own * 32, width)
        return exact_dot(block, restrict_matrix(level)).reshape(own, 32, 128)

    def prolonged(level, src, dst, rows):
        low, high = RIM[level + 1] - rows, RIM[level + 1] + OX[level + 1] + rows
        n = high - low
        sel = prolong_matrix(level)
        spread = lv[level]["g"]
        block = src[low:high].reshape(n * 32, LN[level + 1])
        spread[0:n] = exact_dot(block, sel).reshape(n, 32, LN[level])

        def body(k):
            i = RIM[level] + 2 * (k - rows)
            extra = spread[k]
            dst[i] = dst[i] + extra
            dst[i + 1] = dst[i + 1] + extra

        over_rows(0, n, body, 6)

    def all_coefficients(level, low, high):
        refs_c = [lv[level].get(k) for k in ("c", "e", "y4", "z", "q", "r", "g")]
        coefficients(level, *refs_c, low, high)

    n0, h0 = OX[0], RIM[0] - 2
    gather(0, "c", msg_c[0], 24, h0 + 1, (0,))
    gather(0, "t", msg_t[0], 32, h0, (0,))
    all_coefficients(0, 1, n0 - 1)
    start(msg_c[1] + late + msg_c[2])
    first_sweep(0, 1, n0 - 1)
    sweep_range(0, t0, lv[0]["a"], 2, n0 - 2)
    remainder_rows(0, lv[0]["a"], 2, OX[1] - 2)
    gather(0, "c", msg_c[0], 24, h0 + 1, (-1, 1))
    gather(0, "t", msg_t[0], 32, h0, (-1, 1))
    for low, high in ((-h0, 1), (n0 - 1, n0 + h0)):
        all_coefficients(0, low, high)
        first_sweep(0, low, high)
    for low, high in ((1 - h0, 2), (n0 - 2, n0 + h0 - 1)):
        sweep_range(0, t0, lv[0]["a"], low, high)
    for low, high in ((0, 2), (OX[1] - 2, OX[1])):
        remainder_rows(0, lv[0]["a"], low, high)

    def outer_rows(level):
        own, h = OX[level], RIM[level] - 1
        arrived(late_t[level])
        for side in (-1, 1):
            unpack_columns(level, lv[level]["t"], lv[level]["rpt"], 32, h, side, 2)
        for low, high in ((-h, -2), (own + 2, own + h)):
            first_sweep(level, low, high)
        for low, high in ((1 - h, -1), (own + 1, own + h - 1)):
            sweep_range(level, lv[level]["t"], lv[level]["a"], low, high)

    for level in (1, 2):
        t, own, h = lv[level]["t"], OX[level], RIM[level] - 1
        if level == 2:
            remainder_rows(1, lv[1]["a"], 0, own)
        t[RIM[level] : RIM[level] + own, :, 0:128] = restricted(level - 1)
        start(msg_t[level][:2])
        pack_columns(level, t, lv[level]["spt"], 32)
        start(msg_t[level][4:] + msg_t[level][2:4] + late_t[level])
        if level == 2:
            outer_rows(1)
            pass_on(msg_fc, msg_sc)
        if level == 1:
            arrived(late)
            for side in (-1, 1):
                unpack_columns(0, c0, lv[0]["rpc"], 24, h0 + 2, side, h0 + 1)
                unpack_columns(0, raw, lv[0]["rpt"], 32, h0 + 1, side, h0)
            for row, inward in ((-h0 - 1, -h0), (n0 + h0, n0 + h0 - 1)):
                all_coefficients(0, row, row + 1)
                first_sweep(0, row, row + 1)
                sweep_range(0, t0, lv[0]["a"], inward, inward + 1)
        gather(level, "c", msg_c[level], 24, RIM[level], (0, -1, 1))
        all_coefficients(level, -h, own + h)
        gather(level, "t", msg_t[level], 32, 2, (0,))
        if OY[level] >= 128:
            sent(msg_t[level][:2] + late_t[level])
            start(msg_fc + msg_sc[REACH])
        first_sweep(level, 0, own)
        sweep_range(level, t, lv[level]["a"], 1, own - 1)
        gather(level, "t", msg_t[level], 32, 2, (-1, 1))
        first_sweep(level, -2, 0)
        first_sweep(level, own, own + 2)
        sweep_range(level, t, lv[level]["a"], -1, 1)
        sweep_range(level, t, lv[level]["a"], own - 1, own + 1)

    remainder_rows(2, lv[2]["a"], 0, OX[3])
    t_next = restricted(2)
    far_t[REACH] = sum(roll(t_next[k], 32 * k, 1) for k in range(4))
    start(msg_ft + msg_st[REACH])
    outer_rows(2)

    def unpack_far(dest, far, side, planes, factor):
        lane = lane_iota(planes)

        def body(b):
            own, left, right = far[b], side[0, b], side[1, b]
            for k in range(4):
                tile = jnp.where(lane < 32, roll(own, -32 * k, 1), 0.0)
                tile = jnp.where((lane >= 32) & (lane < 64), roll(right, 32 - 32 * k, 1), tile)
                tile = jnp.where(lane >= 96, roll(left, 96 - 32 * k, 1), tile)
                dest[4 * b + k] = tile if factor is None else tile * factor[4 * b + k]

        over_rows(0, FAR, body, FAR)

    for one in all_sc + all_st:
        one.pending = ["arrived", "sent"]
    arrived(all_sc + [one for one in msg_fc if "arrived" in one.pending])
    q3 = lv[3]["q"]
    unpack_far(lv[3]["c"], far_c, side_c, 24, None)
    all_coefficients(3, 1 - RIM[3], OX[3] + RIM[3] - 1)
    q3[0] = q3[1]
    q3[OX[3] + 2 * RIM[3] - 1] = q3[1]
    pass_on(msg_ft, msg_st)
    sent([one for one in every if one.pending == ["sent"]])
    arrived([one for one in msg_ft if "arrived" in one.pending] + all_st)
    t3, a3, b3 = lv[3]["t"], lv[3]["a"], lv[3]["b"]
    unpack_far(t3, far_t, side_t, 32, q3)
    args3 = refs(3)

    def coarse_sweep(src, dst, s):
        first = s + 2

        def body(n, _):
            for k in range(UNROLL[3]):
                sweep_row(src, dst, *args3, first + UNROLL[3] * n + k)
            return 0

        lax.fori_loop(0, (47 - 2 * s + UNROLL[3]) // UNROLL[3], body, 0)

    coarse_sweep(t3, a3, 2)

    def coarse_pair(n, _):
        coarse_sweep(a3, b3, 2 * n + 3)
        coarse_sweep(b3, a3, 2 * n + 4)
        return 0

    lax.fori_loop(0, (ITERS - 2) // 2, coarse_pair, 0)

    prolonged(2, a3, lv[2]["a"], 2)
    sweep(2, lv[2]["a"], lv[2]["b"], 3)
    sweep(2, lv[2]["b"], lv[2]["a"], 2)
    prolonged(1, lv[2]["a"], lv[1]["a"], 2)
    sweep(1, lv[1]["a"], lv[1]["b"], 2)
    sweep(1, lv[1]["b"], lv[1]["a"], 1)
    prolonged(0, lv[1]["a"], lv[0]["a"], 1)
    a0, b0 = lv[0]["a"], lv[0]["b"]
    sweep(0, a0, b0, 1)
    args0 = refs(0)
    stores = []
    for part, (low, rows) in enumerate(((0, 16), (16, 8), (24, 8))):
        first = RIM[0] + low

        over_rows(first, rows, lambda i: sweep_row(b0, a0, *args0, i), UNROLL[0])
        for n in range(2):
            for k in range(16):
                kk = (k % 2) * 8 + k // 2
                store = pltpu.make_async_copy(
                    a0.at[pl.ds(first, rows), 16 * n + kk, pl.ds(0, 256)],
                    o_ref.at[n, k, pl.ds(low, rows), :],
                    out_sem.at[part],
                )
                store.start()
        done = a0.at[pl.ds(first, rows), :, pl.ds(0, 256)]
        stores.append(pltpu.make_async_copy(done, done, out_sem.at[part]))
    sent([one for one in every if one.pending])
    for store in stores:
        store.wait()


def solution(mesh):
    nx, ny = mesh.shape["gx"], mesh.shape["gy"]
    f32 = jnp.float32
    scratch = []
    for level in range(4):
        rows, lanes = TX[level], LN[level]
        planes = [24, 16, 64, 24, 32, 32, 32, 32]
        planes += [32] if level > 0 else []
        planes += [32] if level < 3 else []
        scratch += [pltpu.VMEM((rows, p, lanes), f32) for p in planes]
        if level < 3:
            scratch += [pltpu.VMEM((n, p, 128), f32) for p in (24, 32) for n in (2, 6)]
        if level == 0:
            scratch += [pltpu.VMEM((rows, 32, lanes), f32)]
    scratch += [pltpu.VMEM((16, 32, 256), f32)]
    scratch += [pltpu.VMEM((FAR, 24, 128), f32), pltpu.VMEM((FAR, 32, 128), f32)]
    scratch += [pltpu.VMEM((2, FAR, 24, 128), f32), pltpu.VMEM((2, FAR, 32, 128), f32)]
    scratch += [
        pltpu.VMEM((32, 256), f32),
        pltpu.VMEM((32, 256), jnp.int32),
        pltpu.VMEM((32, 256), jnp.int32),
    ]
    messages = 8 + 6 * 8 + 4 * REACH + 8 * (REACH - DIRECT) + 8
    scratch += [pltpu.SemaphoreType.DMA((5,)), pltpu.SemaphoreType.DMA((3,))]
    scratch += [pltpu.SemaphoreType.DMA((messages,)), pltpu.SemaphoreType.DMA((messages,))]

    def per_device(misfit, viscosity, friction, ice_mask, grounded):
        return pl.pallas_call(
            functools.partial(kernel, nx, ny),
            out_shape=jax.ShapeDtypeStruct(misfit.shape, f32),
            in_specs=[pl.BlockSpec(memory_space=HBM)] * 5,
            out_specs=pl.BlockSpec(memory_space=HBM),
            scratch_shapes=scratch,
            compiler_params=pltpu.CompilerParams(
                collective_id=0, has_side_effects=True, vmem_limit_bytes=62 * 2**20
            ),
        )(misfit, viscosity, friction, ice_mask, grounded)

    placed = (
        P(None, None, "gx", "gy"),
        P(None, "gx", "gy"),
        P("gx", "gy"),
        P("gx", "gy"),
        P("gx", "gy"),
    )
    return jax.shard_map(
        per_device, mesh=mesh, in_specs=placed, out_specs=P(None, None, "gx", "gy"), check_vma=False
    )
```

```python
import functools

import jax
import jax.numpy as jnp
from jax import lax
from jax.experimental import pallas as pl
from jax.experimental.pallas import tpu as pltpu
from jax.sharding import PartitionSpec as P

MESH = pl.DeviceIdType.MESH
HBM = pltpu.MemorySpace.HBM
OMEGA = 0.6
CROSS = 0.75
ITERS = 20

OX = (32, 16, 8, 4)
OY = (256, 128, 64, 32)
LN = (384, 256, 128, 128)
RIM = (4, 5, 6, 24)
PW = (4, 8, 16, 32)
TX = tuple(o + 2 * h for o, h in zip(OX[:3], RIM)) + (64,)
UNROLL = (8, 10, 9, 16)
UNROLL_C = (4, 4, 6, 10)
UNROLL_R = (2, 4, 4)
DIRECT = 6
REACH = 6
FAR = 2 * REACH + 1
SIDES = ((0, -1), (0, 1), (-1, -1), (-1, 1), (1, -1), (1, 1))


def over_rows(first, count, body, unroll):
    steps = count // unroll

    def step(n, _):
        for k in range(unroll):
            body(first + n * unroll + k)
        return 0

    if steps > 0:
        lax.fori_loop(0, steps, step, 0)
    for k in range(steps * unroll, count):
        body(first + k)


def lane_iota(rows):
    return lax.broadcasted_iota(jnp.int32, (rows, 128), 1)


def roll(x, shift, axis):
    return pltpu.roll(x, shift % x.shape[axis], axis)


def exact_dot(x, sel):
    hi = x.astype(jnp.bfloat16)
    rest = x - hi.astype(jnp.float32)
    mid = rest.astype(jnp.bfloat16)
    low = (rest - mid.astype(jnp.float32)).astype(jnp.bfloat16)
    rows = x.shape[0]
    out = jnp.dot(
        jnp.concatenate([hi, mid, low], 0), sel, preferred_element_type=jnp.float32
    )
    return (out[:rows] + out[rows : 2 * rows]) + out[2 * rows :]


def restrict_matrix(level):
    width = min(LN[level], OY[level]) if OY[level] >= 128 else 128
    fine = lax.broadcasted_iota(jnp.int32, (width, 128), 0)
    coarse = lax.broadcasted_iota(jnp.int32, (width, 128), 1)
    hit = (fine // 2 == coarse) & (fine < OY[level])
    return jnp.where(hit, 0.25, 0.0).astype(jnp.bfloat16)


def prolong_matrix(level):
    lc, lf = LN[level + 1], LN[level]
    coarse = lax.broadcasted_iota(jnp.int32, (lc, lf), 0)
    fine = lax.broadcasted_iota(jnp.int32, (lc, lf), 1)
    middle = (OY[level] + lf) // 2
    source = jnp.where(fine < middle, fine // 2, lc - (lf - fine + 1) // 2)
    return jnp.where(source == coarse, 1.0, 0.0).astype(jnp.bfloat16)


class Message:
    def __init__(self, place, sems, index, src, dst, dx, dy):
        gx, gy, nx, ny = place
        self.way = (dx, dy)
        self.to_there = (gx + dx >= 0) & (gx + dx < nx) & (gy + dy >= 0) & (gy + dy < ny)
        self.from_there = (gx - dx >= 0) & (gx - dx < nx) & (gy - dy >= 0) & (gy - dy < ny)
        target = (jnp.clip(gx + dx, 0, nx - 1), jnp.clip(gy + dy, 0, ny - 1))
        self.dst = dst
        self.pending = []
        self.copy = pltpu.make_async_remote_copy(
            src_ref=src,
            dst_ref=dst,
            send_sem=sems[0].at[index],
            recv_sem=sems[1].at[index],
            device_id=target,
            device_id_type=MESH,
        )


def by_way(messages):
    groups = {}
    for one in messages:
        groups.setdefault(one.way, []).append(one)
    return groups.values()


def clear(messages):
    for group in by_way(messages):

        @pl.when(jnp.logical_not(group[0].from_there))
        def _(group=group):
            for one in group:
                one.dst[...] = jnp.zeros(one.dst.shape, one.dst.dtype)


def start(messages):
    for group in by_way(messages):

        @pl.when(group[0].to_there)
        def _(group=group):
            for one in group:
                one.copy.start()

    for one in messages:
        one.pending = ["arrived", "sent"]


def arrived(messages):
    for group in by_way(messages):

        @pl.when(group[0].from_there)
        def _(group=group):
            for one in group:
                one.copy.wait_recv()

    for one in messages:
        one.pending.remove("arrived")


def sent(messages):
    for group in by_way(messages):

        @pl.when(group[0].to_there)
        def _(group=group):
            for one in group:
                one.copy.wait_send()

    for one in messages:
        one.pending.remove("sent")


def pack_columns(level, source, dest, planes):
    w, rim = PW[level], RIM[level]
    lane = lane_iota(planes)
    tile = (OY[level] - 1) // 128
    edge = (OY[level] - w) % 128
    zero = jnp.zeros((planes, 128), jnp.float32)
    left, right = zero, zero
    for i in range(OX[level]):
        here = (lane >= w * i) & (lane < w * i + w)
        a = source[rim + i, :, 0:128]
        b = source[rim + i, :, tile * 128 : tile * 128 + 128]
        left = jnp.where(here, roll(a, w * i, 1), left)
        right = jnp.where(here, roll(b, w * i - edge, 1), right)
    dest[0] = left
    dest[1] = right


def unpack_columns(level, dest, packs, planes, reach, side, skip=0):
    w, rim, own = PW[level], RIM[level], OX[level]
    lane = lane_iota(planes)
    last = LN[level] - 128
    start = OY[level] % 128
    row0, count, shift, slot = {
        -1: (-reach, reach - skip, own - reach, 2),
        0: (0, own, 0, 0),
        1: (own + skip, reach - skip, skip, 4),
    }[side]
    for i in range(count):
        at = w * (i + shift)
        right = roll(packs[slot + 1], start - at, 1)
        left = roll(packs[slot], -w - at, 1)
        row = rim + row0 + i
        if OY[level] < 128:
            rest = dest[row, :, last : last + 128]
        else:
            rest = jnp.zeros((planes, 128), jnp.float32)
        tile = jnp.where((lane >= start) & (lane < start + w), right, rest)
        dest[row, :, last : last + 128] = jnp.where(lane >= 128 - w, left, tile)


def coefficients(level, c, e, y4, z, q, r, g, low, high):
    scale = 0.25**level
    half, cross = 0.5 * scale, CROSS * scale
    lanes, rim = LN[level], RIM[level]
    first, count = rim + low, high - low
    sub = lax.broadcasted_iota(jnp.int32, (8, lanes), 0)
    e[first - 1] = half * (c[first - 1, 0:16, :] + c[first, 0:16, :])

    def body(i):
        here = c[i, 0:16, :]
        north, south = roll(here, -1, 1), roll(here, 1, 1)
        east = half * (here + c[i + 1, 0:16, :])
        west = half * (here + c[i - 1, 0:16, :])
        nf, sf = half * (here + north), half * (here + south)
        e[i] = east
        y4[i, 0:16, :] = nf
        y4[i, 16:32, :] = sf
        y4[i, 32:48, :] = cross * north
        y4[i, 48:64, :] = cross * south
        even, odd = here[0:8], here[8:16]
        inner = 2.0 * (even + odd)
        upper = jnp.where(sub < 7, 2.0 * (odd + roll(even, -1, 0)), 0.0)
        lower = roll(upper, 1, 0)
        z[i, 0:8, :] = inner
        z[i, 8:16, :] = upper
        z[i, 16:24, :] = lower
        ice = c[i, 16:17, :]
        drag = jnp.where(sub == 0, c[i, 17:18, :], 0.0)
        vertical = jnp.concatenate([inner + lower + drag, inner + upper], 0)
        xs, ys = east + west, nf + sf
        for k, lateral in enumerate((4.0 * xs + ys, xs + 4.0 * ys)):
            diag = ice * (lateral + vertical) + (1.0 - ice)
            inv = OMEGA / diag
            if q is not None:
                q[i, 16 * k : 16 * k + 16, :] = inv
            r[i, 16 * k : 16 * k + 16, :] = ice * inv
            if g is not None:
                g[i, 16 * k : 16 * k + 16, :] = diag * (1.0 / OMEGA)

    over_rows(first, count, body, UNROLL_C[level])


def off_diagonal(w, e, y4, z, i):
    u0, u, u2 = w[i - 1, 0:16, :], w[i, 0:16, :], w[i + 1, 0:16, :]
    v0, v, v2 = w[i - 1, 16:32, :], w[i, 16:32, :], w[i + 1, 16:32, :]
    west, east = e[i - 1], e[i]
    nf, sf, mn, ms = (y4[i, 16 * k : 16 * k + 16, :] for k in range(4))
    inner, upper, lower = (z[i, 8 * k : 8 * k + 8, :] for k in range(3))
    du, dv, v4 = u2 - u0, v2 - v0, 4.0 * v
    xu = 4.0 * (east * u2 + west * u0)
    xv = east * v2 + west * v0
    yu = roll(sf * u + ms * dv, -1, 1) + roll(nf * u - mn * dv, 1, 1)
    yv = roll(sf * v4 + ms * du, -1, 1) + roll(nf * v4 - mn * du, 1, 1)

    def column(f):
        even, odd = f[0:8], f[8:16]
        return jnp.concatenate(
            [inner * odd + lower * roll(odd, 1, 0), inner * even + upper * roll(even, -1, 0)], 0
        )

    return (u, v), (xu + yu + column(u), xv + yv + column(v))


def sweep_row(src, dst, e, y4, z, r, tt, i):
    fields, sums = off_diagonal(src, e, y4, z, i)
    for k in range(2):
        at = slice(16 * k, 16 * k + 16)
        dst[i, at, :] = (1.0 - OMEGA) * fields[k] + (tt[i, at, :] + r[i, at, :] * sums[k])


def remainder_row(src, e, y4, z, r, tt, g, i, lanes):
    fields, sums = off_diagonal(src, e, y4, z, i)
    parts = []
    for k in range(2):
        at = slice(16 * k, 16 * k + 16)
        change = tt[i, at, :] + r[i, at, :] * sums[k] - OMEGA * fields[k]
        parts.append(change[:, 0:lanes] * g[i, at, 0:lanes])
    return jnp.concatenate(parts, 0)


def kernel(nx, ny, m_ref, v_ref, f_ref, i_ref, b_ref, o_ref, *scratch):
    names = iter(scratch)
    lv = []
    for level in range(4):
        keys = ["c", "e", "y4", "z", "r", "t", "a", "b"]
        keys += ["q"] if level > 0 else []
        keys += ["g"] if level < 3 else []
        keys += ["spc", "rpc", "spt", "rpt"] if level < 3 else []
        keys += ["raw"] if level == 0 else []
        lv.append({key: next(names) for key in keys})
    rest, far_c, far_t, side_c, side_t, fr, ic, gr = (next(names) for _ in range(8))
    in_sem, out_sem, send_sem, recv_sem = (next(names) for _ in range(4))

    gx, gy = lax.axis_index("gx"), lax.axis_index("gy")
    place = (gx, gy, nx, ny)
    sems = (send_sem, recv_sem)
    count = iter(range(10**6))

    def message(src, dst, dx, dy):
        return Message(place, sems, next(count), src, dst, dx, dy)

    def rim_messages(level, array, packs, landed, reach):
        rim, own = RIM[level], OX[level]
        lanes = pl.ds(0, max(OY[level], 128))
        out = [
            message(
                array.at[pl.ds(rim, reach), :, lanes],
                array.at[pl.ds(rim + own, reach), :, lanes], -1, 0),
            message(
                array.at[pl.ds(rim + own - reach, reach), :, lanes],
                array.at[pl.ds(rim - reach, reach), :, lanes], 1, 0),
        ]
        for slot, (dx, dy) in enumerate(SIDES):
            out.append(message(packs.at[0 if dy > 0 else 1], landed.at[slot], -dx, -dy))
        return out

    def far_messages(far, side):
        out = []
        for d in [k * s for k in range(REACH, 0, -1) for s in (1, -1)]:
            out.append(message(far.at[REACH], far.at[REACH - d], d, 0))
            for n in range(2 if abs(d) > DIRECT else 0):
                out.append(message(far.at[REACH], side.at[n, REACH - d], d, 1 - 2 * n))
        return out

    def side_messages(far, side):
        near = pl.ds(REACH - DIRECT, 2 * DIRECT + 1)
        whole = [message(far.at[near], side.at[n, near], 0, 1 - 2 * n) for n in range(2)]
        first = next(count) - 2
        blocks = {
            b: [
                Message(place, sems, first + n, far.at[b], side.at[n, b], 0, 1 - 2 * n)
                for n in range(2)
            ]
            for b in range(REACH - DIRECT, REACH + DIRECT + 1)
        }
        return whole, blocks

    def pass_on(far, side):
        for d in range(1, DIRECT + 1):
            for s in (d, -d):
                arrived([one for one in far if one.way == (s, 0)])
                start(side[REACH - s])

    c0, t0, raw = lv[0]["c"], lv[0]["t"], lv[0]["raw"]
    msg_c = [rim_messages(n, lv[n]["c"], lv[n]["spc"], lv[n]["rpc"], RIM[n] - (n == 0)) for n in range(3)]
    msg_t = [
        rim_messages(
            n, lv[n]["t"] if n > 0 else raw, lv[n]["spt"], lv[n]["rpt"], 2
        )
        for n in range(3)
    ]
    def late_messages(level, array, near, far):
        rim, own, lanes = RIM[level], OX[level], pl.ds(0, max(OY[level], 128))
        return [
            message(
                array.at[pl.ds(source, far - near), :, lanes],
                array.at[pl.ds(target, far - near), :, lanes], dx, 0)
            for dx, source, target in (
                (-1, rim + near, rim + own + near),
                (1, rim + own - far, rim - far),
            )
        ]

    late = late_messages(0, c0, RIM[0] - 1, RIM[0]) + late_messages(0, raw, 2, RIM[0] - 1)
    late_t = {n: late_messages(n, lv[n]["t"], 2, RIM[n] - 1) for n in (1, 2)}
    msg_fc, msg_ft = far_messages(far_c, side_c), far_messages(far_t, side_t)
    all_sc, msg_sc = side_messages(far_c, side_c)
    all_st, msg_st = side_messages(far_t, side_t)
    every = sum(msg_c + msg_t, late + late_t[1] + late_t[2]) + msg_fc + msg_ft + all_sc + all_st

    barrier = pltpu.get_barrier_semaphore()
    far_away = [d for d in range(-REACH, REACH + 1) if abs(d) > DIRECT]
    partners = [(d, 0) for d in range(-REACH, REACH + 1) if d != 0] + list(SIDES)
    partners += [(d, s) for d in far_away for s in (-1, 1)]
    arrivals = 0
    for dx, dy in partners:
        there = (gx + dx >= 0) & (gx + dx < nx) & (gy + dy >= 0) & (gy + dy < ny)
        arrivals = arrivals + there.astype(jnp.int32)

        @pl.when(there)
        def _(dx=dx, dy=dy):
            pl.semaphore_signal(
                barrier,
                inc=1,
                device_id=(jnp.clip(gx + dx, 0, nx - 1), jnp.clip(gy + dy, 0, ny - 1)),
                device_id_type=MESH,
            )

    own0 = pl.ds(RIM[0], OX[0])
    loads = []
    for k in range(16):
        kk = (k % 2) * 8 + k // 2
        loads.append((v_ref.at[k], c0.at[own0, kk, pl.ds(0, 256)], 0))
        for n in range(2):
            loads.append((m_ref.at[n, k], raw.at[own0, 16 * n + kk, pl.ds(0, 256)], 1))
    loads += [(f_ref, fr, 2), (i_ref, ic, 3), (b_ref, gr, 4)]
    for source, target, n in loads:
        pltpu.make_async_copy(source, target, in_sem.at[n]).start()
    landed = [c0.at[own0, pl.ds(0, 16), pl.ds(0, 256)], raw.at[own0, :, pl.ds(0, 256)], fr, ic, gr]

    clear(every)
    for n, target in enumerate(landed):
        pltpu.make_async_copy(target, target, in_sem.at[n]).wait()

    ic_f = ic[...].astype(jnp.float32)
    ic_f = ic_f.reshape(OX[0], 1, 256)
    dr_f = (fr[...] * gr[...].astype(jnp.float32)).reshape(OX[0], 1, 256)
    sub = lax.broadcasted_iota(jnp.int32, (OX[0], 8, 256), 1)
    c0[own0, 16:24, 0:256] = jnp.where(sub == 0, ic_f, jnp.where(sub == 1, dr_f, 0.0))

    pack_columns(0, c0, lv[0]["spc"], 24)
    pack_columns(0, raw, lv[0]["spt"], 32)

    pl.semaphore_wait(barrier, arrivals)
    start(msg_c[0][2:4] + msg_t[0][2:4])
    start(msg_c[0][:2] + msg_t[0][:2] + msg_c[0][4:] + msg_t[0][4:])

    for level in range(3):
        rim, own, width = RIM[level], OX[level + 1], max(OY[level], 128)
        fine = lv[level]["c"]
        block = fine[rim : rim + 2 * own, :, 0:width].reshape(own, 2, 24, width)
        block = (block[:, 0] + block[:, 1]).reshape(own * 24, width)
        coarse = exact_dot(block, restrict_matrix(level)).reshape(own, 24, 128)
        if level < 2:
            target = lv[level + 1]["c"]
            target[RIM[level + 1] : RIM[level + 1] + own, :, 0:128] = coarse
            pack_columns(level + 1, target, lv[level + 1]["spc"], 24)
        else:
            far_c[REACH] = sum(roll(coarse[k], 32 * k, 1) for k in range(4))

    def refs(level):
        return [lv[level][key] for key in ("e", "y4", "z", "r", "t")]

    def gather(level, kind, messages, planes, reach, sides):
        landed = lv[level]["rp" + kind]
        array = raw if (level, kind) == (0, "t") else lv[level][kind]
        for side in sides:
            which = {0: messages[2:4], -1: messages[1:2] + messages[4:6], 1: messages[0:1] + messages[6:8]}
            arrived(which[side])
        if OY[level] < 128 and 0 in sides:
            sent(messages[:2] + (late_t[level] if kind == "t" else []))
        for side in sides:
            unpack_columns(level, array, landed, planes, reach, side)

    def first_sweep(level, low, high):
        t = lv[level]["t"]
        source, factor = (raw, lv[0]["r"]) if level == 0 else (t, lv[level]["q"])

        def body(i):
            t[i] = source[i] * factor[i]

        over_rows(RIM[level] + low, high - low, body, min(4, high - low))

    def sweep_range(level, src, dst, low, high):
        args = refs(level)

        over_rows(
            RIM[level] + low,
            high - low,
            lambda i: sweep_row(src, dst, *args, i),
            UNROLL[level],
        )

    def sweep(level, src, dst, rows):
        sweep_range(level, src, dst, -rows, OX[level] + rows)

    def remainder_rows(level, src, low, high):
        args = refs(level)
        width = max(OY[level], 128)

        def body(n):
            i = RIM[level] + 2 * n
            pair = [remainder_row(src, *args, lv[level]["g"], i + k, width) for k in range(2)]
            rest[n, :, 0:width] = pair[0] + pair[1]

        over_rows(low, high - low, body, min(UNROLL_R[level], high - low))

    def restricted(level):
        width, own = max(OY[level], 128), OX[level + 1]
        block = rest[0:own, :, 0:width].reshape(own * 32, width)
        return exact_dot(block, restrict_matrix(level)).reshape(own, 32, 128)

    def prolonged(level, src, dst, rows):
        low, high = RIM[level + 1] - rows, RIM[level + 1] + OX[level + 1] + rows
        n = high - low
        sel = prolong_matrix(level)
        spread = lv[level]["g"]
        block = src[low:high].reshape(n * 32, LN[level + 1])
        spread[0:n] = exact_dot(block, sel).reshape(n, 32, LN[level])

        def body(k):
            i = RIM[level] + 2 * (k - rows)
            extra = spread[k]
            dst[i] = dst[i] + extra
            dst[i + 1] = dst[i + 1] + extra

        over_rows(0, n, body, 6)

    def all_coefficients(level, low, high):
        refs_c = [lv[level].get(k) for k in ("c", "e", "y4", "z", "q", "r", "g")]
        coefficients(level, *refs_c, low, high)

    n0, h0 = OX[0], RIM[0] - 2
    gather(0, "c", msg_c[0], 24, h0 + 1, (0,))
    gather(0, "t", msg_t[0], 32, h0, (0,))
    all_coefficients(0, 1, n0 - 1)
    start(msg_c[1] + late + msg_c[2])
    first_sweep(0, 1, n0 - 1)
    sweep_range(0, t0, lv[0]["a"], 2, n0 - 2)
    remainder_rows(0, lv[0]["a"], 2, OX[1] - 2)
    gather(0, "c", msg_c[0], 24, h0 + 1, (-1, 1))
    gather(0, "t", msg_t[0], 32, h0, (-1, 1))
    for low, high in ((-h0, 1), (n0 - 1, n0 + h0)):
        all_coefficients(0, low, high)
        first_sweep(0, low, high)
    for low, high in ((1 - h0, 2), (n0 - 2, n0 + h0 - 1)):
        sweep_range(0, t0, lv[0]["a"], low, high)
    for low, high in ((0, 2), (OX[1] - 2, OX[1])):
        remainder_rows(0, lv[0]["a"], low, high)

    def outer_rows(level):
        own, h = OX[level], RIM[level] - 1
        arrived(late_t[level])
        for side in (-1, 1):
            unpack_columns(level, lv[level]["t"], lv[level]["rpt"], 32, h, side, 2)
        for low, high in ((-h, -2), (own + 2, own + h)):
            first_sweep(level, low, high)
        for low, high in ((1 - h, -1), (own + 1, own + h - 1)):
            sweep_range(level, lv[level]["t"], lv[level]["a"], low, high)

    for level in (1, 2):
        t, own, h = lv[level]["t"], OX[level], RIM[level] - 1
        if level == 2:
            remainder_rows(1, lv[1]["a"], 0, own)
        t[RIM[level] : RIM[level] + own, :, 0:128] = restricted(level - 1)
        start(msg_t[level][:2])
        pack_columns(level, t, lv[level]["spt"], 32)
        start(msg_t[level][4:] + msg_t[level][2:4] + late_t[level])
        if level == 2:
            outer_rows(1)
            pass_on(msg_fc, msg_sc)
        if level == 1:
            arrived(late)
            for side in (-1, 1):
                unpack_columns(0, c0, lv[0]["rpc"], 24, h0 + 2, side, h0 + 1)
                unpack_columns(0, raw, lv[0]["rpt"], 32, h0 + 1, side, h0)
            for row, inward in ((-h0 - 1, -h0), (n0 + h0, n0 + h0 - 1)):
                all_coefficients(0, row, row + 1)
                first_sweep(0, row, row + 1)
                sweep_range(0, t0, lv[0]["a"], inward, inward + 1)
        gather(level, "c", msg_c[level], 24, RIM[level], (0, -1, 1))
        all_coefficients(level, -h, own + h)
        gather(level, "t", msg_t[level], 32, 2, (0,))
        if OY[level] >= 128:
            sent(msg_t[level][:2] + late_t[level])
            start(msg_fc + msg_sc[REACH])
        first_sweep(level, 0, own)
        sweep_range(level, t, lv[level]["a"], 1, own - 1)
        gather(level, "t", msg_t[level], 32, 2, (-1, 1))
        first_sweep(level, -2, 0)
        first_sweep(level, own, own + 2)
        sweep_range(level, t, lv[level]["a"], -1, 1)
        sweep_range(level, t, lv[level]["a"], own - 1, own + 1)

    remainder_rows(2, lv[2]["a"], 0, OX[3])
    t_next = restricted(2)
    far_t[REACH] = sum(roll(t_next[k], 32 * k, 1) for k in range(4))
    start(msg_ft + msg_st[REACH])
    outer_rows(2)

    def unpack_far(dest, far, side, planes, factor):
        lane = lane_iota(planes)

        def body(b):
            own, left, right = far[b], side[0, b], side[1, b]
            for k in range(4):
                tile = jnp.where(lane < 32, roll(own, -32 * k, 1), 0.0)
                tile = jnp.where((lane >= 32) & (lane < 64), roll(right, 32 - 32 * k, 1), tile)
                tile = jnp.where(lane >= 96, roll(left, 96 - 32 * k, 1), tile)
                dest[4 * b + k] = tile if factor is None else tile * factor[4 * b + k]

        over_rows(0, FAR, body, FAR)

    for one in all_sc + all_st:
        one.pending = ["arrived", "sent"]
    arrived(all_sc + [one for one in msg_fc if "arrived" in one.pending])
    q3 = lv[3]["q"]
    unpack_far(lv[3]["c"], far_c, side_c, 24, None)
    all_coefficients(3, 1 - RIM[3], OX[3] + RIM[3] - 1)
    q3[0] = q3[1]
    q3[OX[3] + 2 * RIM[3] - 1] = q3[1]
    pass_on(msg_ft, msg_st)
    sent([one for one in every if one.pending == ["sent"]])
    arrived([one for one in msg_ft if "arrived" in one.pending] + all_st)
    t3, a3, b3 = lv[3]["t"], lv[3]["a"], lv[3]["b"]
    unpack_far(t3, far_t, side_t, 32, q3)
    args3 = refs(3)

    def coarse_sweep(src, dst, s):
        first = s + 2

        def body(n, _):
            for k in range(UNROLL[3]):
                sweep_row(src, dst, *args3, first + UNROLL[3] * n + k)
            return 0

        lax.fori_loop(0, (47 - 2 * s + UNROLL[3]) // UNROLL[3], body, 0)

    coarse_sweep(t3, a3, 2)

    def coarse_pair(n, _):
        coarse_sweep(a3, b3, 2 * n + 3)
        coarse_sweep(b3, a3, 2 * n + 4)
        return 0

    lax.fori_loop(0, (ITERS - 2) // 2, coarse_pair, 0)

    prolonged(2, a3, lv[2]["a"], 2)
    sweep(2, lv[2]["a"], lv[2]["b"], 3)
    sweep(2, lv[2]["b"], lv[2]["a"], 2)
    prolonged(1, lv[2]["a"], lv[1]["a"], 2)
    sweep(1, lv[1]["a"], lv[1]["b"], 2)
    sweep(1, lv[1]["b"], lv[1]["a"], 1)
    prolonged(0, lv[1]["a"], lv[0]["a"], 1)
    a0, b0 = lv[0]["a"], lv[0]["b"]
    sweep(0, a0, b0, 1)
    args0 = refs(0)
    stores = []
    for part, (low, rows) in enumerate(((0, 24), (24, 8))):
        first = RIM[0] + low

        over_rows(first, rows, lambda i: sweep_row(b0, a0, *args0, i), UNROLL[0])
        for n in range(2):
            for k in range(16):
                kk = (k % 2) * 8 + k // 2
                store = pltpu.make_async_copy(
                    a0.at[pl.ds(first, rows), 16 * n + kk, pl.ds(0, 256)],
                    o_ref.at[n, k, pl.ds(low, rows), :],
                    out_sem.at[part],
                )
                store.start()
        done = a0.at[pl.ds(first, rows), :, pl.ds(0, 256)]
        stores.append(pltpu.make_async_copy(done, done, out_sem.at[part]))
    sent([one for one in every if one.pending])
    for store in stores:
        store.wait()


def solution(mesh):
    nx, ny = mesh.shape["gx"], mesh.shape["gy"]
    f32 = jnp.float32
    scratch = []
    for level in range(4):
        rows, lanes = TX[level], LN[level]
        planes = [24, 16, 64, 24, 32, 32, 32, 32]
        planes += [32] if level > 0 else []
        planes += [32] if level < 3 else []
        scratch += [pltpu.VMEM((rows, p, lanes), f32) for p in planes]
        if level < 3:
            scratch += [pltpu.VMEM((n, p, 128), f32) for p in (24, 32) for n in (2, 6)]
        if level == 0:
            scratch += [pltpu.VMEM((rows, 32, lanes), f32)]
    scratch += [pltpu.VMEM((16, 32, 256), f32)]
    scratch += [pltpu.VMEM((FAR, 24, 128), f32), pltpu.VMEM((FAR, 32, 128), f32)]
    scratch += [pltpu.VMEM((2, FAR, 24, 128), f32), pltpu.VMEM((2, FAR, 32, 128), f32)]
    scratch += [
        pltpu.VMEM((32, 256), f32),
        pltpu.VMEM((32, 256), jnp.int32),
        pltpu.VMEM((32, 256), jnp.int32),
    ]
    messages = 8 + 6 * 8 + 4 * REACH + 8 * (REACH - DIRECT) + 8
    scratch += [pltpu.SemaphoreType.DMA((5,)), pltpu.SemaphoreType.DMA((3,))]
    scratch += [pltpu.SemaphoreType.DMA((messages,)), pltpu.SemaphoreType.DMA((messages,))]

    def per_device(misfit, viscosity, friction, ice_mask, grounded):
        return pl.pallas_call(
            functools.partial(kernel, nx, ny),
            out_shape=jax.ShapeDtypeStruct(misfit.shape, f32),
            in_specs=[pl.BlockSpec(memory_space=HBM)] * 5,
            out_specs=pl.BlockSpec(memory_space=HBM),
            scratch_shapes=scratch,
            compiler_params=pltpu.CompilerParams(
                collective_id=0, has_side_effects=True, vmem_limit_bytes=62 * 2**20
            ),
        )(misfit, viscosity, friction, ice_mask, grounded)

    placed = (
        P(None, None, "gx", "gy"),
        P(None, "gx", "gy"),
        P("gx", "gy"),
        P("gx", "gy"),
        P("gx", "gy"),
    )
    return jax.shard_map(
        per_device, mesh=mesh, in_specs=placed, out_specs=P(None, None, "gx", "gy"), check_vma=False
    )
```
